32 devices in a mesh: dp: 2 (over x), seq: 4 (over y, core), tensor: 4 (over z).
Axes of the slice: x: 2, y: 2, z: 4, core: 2. Of those that a mesh axis runs over, the one named last changes fastest.
Arguments:
- features: bfloat16 [2, 2, 1536, 768], P(None, 'dp', 'seq'), may hold values from -6 to 6
- upstream: bfloat16 [2, 2, 1536, 768], P(None, 'dp', 'seq'), may hold values from -6 to 6
- key_mask: int32 [2, 2, 1536], P(None, 'dp'), may hold values from 0 to 1, as said below
- vectors: bfloat16 [2, 6, 768], P(None, None, ('dp', 'seq')), may hold values from 0.099609375 to 1.8984375
- proj_qkv: bfloat16 [2, 768, 3, 768], P(None, ('dp', 'seq'), None, 'tensor')
- qv_bias: bfloat16 [2, 2, 768], P(None, None, ('tensor', 'dp', 'seq')), may hold values from -3 to 3
- proj_out: bfloat16 [2, 768, 768], P(None, 'tensor', ('dp', 'seq')), may hold values from -0.21875 to 0.21875
- expand_weight: bfloat16 [2, 768, 3072], P(None, ('dp', 'seq'), 'tensor'), may hold values from -0.21875 to 0.21875
- expand_bias: bfloat16 [2, 3072], P(None, ('tensor', 'dp', 'seq')), may hold values from -3 to 3
- shrink_weight: bfloat16 [2, 3072, 768], P(None, 'tensor', ('dp', 'seq')), may hold values from -0.109375 to 0.109375
Outputs:
- encoded: bfloat16 [2, 2, 1536, 768], P(None, 'dp', 'seq')
- grad_features: float32 [2, 2, 1536, 768], P(None, 'dp', 'seq')
- grad_vectors: float32 [2, 6, 768], P(None, None, ('dp', 'seq'))
- grad_proj_qkv: float32 [2, 768, 3, 768], P(None, ('dp', 'seq'), None, 'tensor')
- grad_qv_bias: float32 [2, 2, 768], P(None, None, ('tensor', 'dp', 'seq'))
- grad_proj_out: float32 [2, 768, 768], P(None, 'tensor', ('dp', 'seq'))
- grad_expand_weight: float32 [2, 768, 3072], P(None, ('dp', 'seq'), 'tensor')
- grad_expand_bias: float32 [2, 3072], P(None, ('tensor', 'dp', 'seq'))
- grad_shrink_weight: float32 [2, 3072, 768], P(None, 'tensor', ('dp', 'seq'))
The draws below stay inside these ranges and needn't reach their ends.
Inputs may be any that keep to these rules, and one draw needn't show every extreme that they name: `key_mask`: each clip's last frames, between 0 and 36 of them, are 0 and all others 1; some clip has exactly 36 padded frames.
All inputs are finite; a program needn't handle non-finite values.
Results may differ from the reference program's by a relative error of at most 0.009.
Values may be sent and summed in bfloat16 or wider, within the bound.
No kernel may reach another device: no remote copies, remote signals or barrier semaphores. Data moves between devices by JAX's collectives and lax.ppermute only.
A program may use at most 192 MiB of HBM per device.

```python
import math
import jax
import jax.numpy as jnp
from jax import lax

D = 768
HEADS = 12
HD = 64
FF = 3072
LEN = 1536
PAD = 36
LAYERS = 2
MICRO = 2
CLIPS = 2


def draw_key_mask(key, part):
    first, second = jax.random.split(jax.random.fold_in(key, 11))
    total = MICRO * CLIPS
    padding = jax.random.randint(first, (total,), 0, PAD + 1)
    chosen = jax.random.randint(second, (), 0, total)
    padding = jnp.where(jnp.arange(total) == chosen, PAD, padding)
    frames = jnp.arange(LEN)
    marked = (frames[None, :] < LEN - padding[:, None]).astype(jnp.int32)
    return marked.reshape(MICRO, CLIPS, LEN)


def draw_proj_qkv(key, part):
    first, second, third = jax.random.split(jax.random.fold_in(key, 23), 3)
    shape = (LAYERS, D, D)
    query_part = jax.random.normal(first, shape, jnp.float32) / math.sqrt(D)
    key_part = jax.random.normal(second, shape, jnp.float32) / math.sqrt(D)
    value_part = jax.random.normal(third, shape, jnp.float32) / math.sqrt(D)
    return jnp.stack([query_part, key_part, value_part], axis=2).astype(jnp.bfloat16)


def steps_of(own_key, extent, cuts, smallest, largest):
    factor_of, own = 1.0, jax.random.fold_in(own_key, 6)
    for axis_at, parts in cuts:
        heights = jnp.exp(jax.random.uniform(jax.random.fold_in(own, axis_at), (parts,), jnp.float32, smallest / len(cuts), largest / len(cuts)))
        factor_of = factor_of * jnp.repeat(heights, extent[axis_at] // parts).reshape([-1 if axis == axis_at else 1 for axis in range(len(extent))])
    return factor_of


def normal_values(key, dims, scale, reach, cuts=(), held_as=jnp.bfloat16):
    drawn = scale * jax.random.normal(key, dims, jnp.float32)
    if cuts:
        drawn = drawn * steps_of(key, dims, cuts, -0.22, 0.18)
    return jnp.clip(drawn, -reach, reach).astype(held_as)


def setup_inputs(seed: int = 0) -> dict:
    arg_keys = jax.random.split(jax.random.key(seed), 11)
    return {
        "features": normal_values(arg_keys[0], (MICRO, CLIPS, LEN, D), 1.0, 6.0, ((1, 2), (2, 4))),
        "upstream": normal_values(arg_keys[1], (MICRO, CLIPS, LEN, D), 1.0, 6.0, ((1, 2), (2, 4))),
        "key_mask": draw_key_mask(jax.random.fold_in(arg_keys[10], 71), 0),
        "vectors": jnp.clip(1.0 + 0.18 * jax.random.normal(arg_keys[3], (LAYERS, 6, D), jnp.float32), 0.099609375, 1.8984375).astype(jnp.bfloat16),
        "proj_qkv": draw_proj_qkv(jax.random.fold_in(arg_keys[10], 71), 0),
        "qv_bias": normal_values(arg_keys[5], (LAYERS, 2, D), 0.5, 3.0, ((2, 32),)),
        "proj_out": normal_values(arg_keys[6], (LAYERS, D, D), D ** -0.5, 0.21875, ((1, 4), (2, 8))),
        "expand_weight": normal_values(arg_keys[7], (LAYERS, D, FF), D ** -0.5, 0.21875, ((1, 8), (2, 4))),
        "expand_bias": normal_values(arg_keys[8], (LAYERS, FF), 0.5, 3.0, ((1, 32),)),
        "shrink_weight": normal_values(arg_keys[9], (LAYERS, FF, D), FF ** -0.5, 0.109375, ((1, 4), (2, 8))),
    }


@jax.custom_vjp
def low(v):
    return lax.optimization_barrier(v.astype(jnp.bfloat16)).astype(jnp.float32)

@jax.custom_vjp
def low_back(v):
    return v

def low_keep(v):
    return (low(v), None)

def low_pass(kept, grad):
    return (grad,)

def back_keep(v):
    return (v, None)

def back_low(kept, grad):
    return (low(grad),)
low.defvjp(low_keep, low_pass)
low_back.defvjp(back_keep, back_low)

def layer_norm(values, gain, shift):
    center = values - lax.optimization_barrier(jnp.mean(values, axis=-1, keepdims=True))
    spread = lax.optimization_barrier(jnp.mean(center * center, axis=-1, keepdims=True))
    return center * lax.rsqrt(spread + 1e-05) * gain + shift

def matmul(left, right):
    return jnp.dot(left, right, precision=lax.Precision.HIGHEST)

def encoder_layer(frames, valid, vectors, proj_qkv, qv_bias, proj_out, expand_weight, expand_bias, shrink_weight):
    normed = low(layer_norm(frames, vectors[0], vectors[1]))
    queries = low(low_back(matmul(normed, proj_qkv[:, 0, :]) + qv_bias[0])).reshape(LEN, HEADS, HD)
    key_rows = low(low_back(matmul(normed, proj_qkv[:, 1, :]))).reshape(LEN, HEADS, HD)
    value_rows = low(low_back(matmul(normed, proj_qkv[:, 2, :]) + qv_bias[1])).reshape(LEN, HEADS, HD)
    scores = jnp.einsum('qhe,khe->hqk', queries, key_rows, precision=lax.Precision.HIGHEST) * HD ** (-0.5)
    scores = jnp.where(valid[None, None, :], low_back(scores), -1000000000.0)
    probs = low(jax.nn.softmax(scores, axis=-1))
    mixed = jnp.einsum('hqk,khe->qhe', probs, value_rows, precision=lax.Precision.HIGHEST).reshape(LEN, D)
    mixed = low(low_back(mixed))
    after = frames + low_back(matmul(mixed, proj_out) + vectors[2])
    normed_two = low(layer_norm(after, vectors[3], vectors[4]))
    hidden = low_back(matmul(normed_two, expand_weight) + expand_bias)
    active = low(jax.nn.gelu(hidden, approximate=False))
    return after + low_back(matmul(active, shrink_weight) + vectors[5])

def reference(features, upstream, key_mask, vectors, proj_qkv, qv_bias, proj_out, expand_weight, expand_bias, shrink_weight):
    clips = features.astype(jnp.float32).reshape(MICRO * CLIPS, LEN, D)
    valid = (key_mask > 0).reshape(MICRO * CLIPS, LEN)
    params = tuple((p.astype(jnp.float32) for p in (vectors, proj_qkv, qv_bias, proj_out, expand_weight, expand_bias, shrink_weight)))

    def forward(clip_data, weights):

        def per_clip(frames, valid_row, layer_weights):
            for depth in range(LAYERS):
                frames = encoder_layer(frames, valid_row, *(w[depth] for w in layer_weights))
            return frames
        checked = jax.checkpoint(per_clip)

        def advance(carry, item):
            return (carry, checked(item[0], item[1], weights))
        _, results = lax.scan(advance, jnp.zeros((), jnp.float32), (clip_data, valid))
        return results
    results, pullback = jax.vjp(forward, clips, params)
    grad_clips, grad_params = pullback(upstream.astype(jnp.float32).reshape(results.shape))
    return (results.astype(jnp.bfloat16).reshape(features.shape), grad_clips.reshape(features.shape), grad_params[0], grad_params[1], grad_params[2], grad_params[3], grad_params[4], grad_params[5], grad_params[6])
```

```python
from functools import partial

import jax
import jax.numpy as jnp
from jax import lax
from jax.experimental import pallas as pl
from jax.experimental.pallas import tpu as pltpu
from jax.sharding import PartitionSpec as P

HD = 64
LAYERS = 2
AXES = ("dp", "seq", "tensor")
BF = jnp.bfloat16
F32 = jnp.float32
VMEM_LIMIT = 48 * 1024 * 1024

BITS = {"x": 16, "y": 8, "c": 4, "z2": 2, "z1": 1}

ORDER_E = ("z2", "z1", "x", "y")
ORDER_S = ("z2", "z1", "y", "x")
ORDERS_A = (("z2", "z1", "x", "y"), ("z2", "x", "y", "z1"), ("z2", "y", "z1", "x"))

SPEC_V = pl.BlockSpec(memory_space=pltpu.VMEM)
SPEC_S = pl.BlockSpec(memory_space=pltpu.SMEM)
SPEC_A = pl.BlockSpec(memory_space=pl.ANY)


def swap(value, bit, mesh_shape):
    dp_size, seq_size, ten_size = mesh_shape
    pairs = []
    for d in range(dp_size):
        for s in range(seq_size):
            for t in range(ten_size):
                e, u, v = d, s, t
                if bit == "x":
                    e = d ^ 1
                elif bit == "y":
                    u = s ^ 2
                elif bit == "c":
                    u = s ^ 1
                elif bit == "z2":
                    v = t ^ 2
                else:
                    v = t ^ 1
                pairs.append(((d * seq_size + s) * ten_size + t, (e * seq_size + u) * ten_size + v))
    return lax.ppermute(value, AXES, pairs)


def swap_group(value, pair, mesh_shape):
    dp_size, seq_size, ten_size = mesh_shape
    ry, rp = pair >> 1, pair & 1
    pairs = []
    for d in range(dp_size):
        for s in range(seq_size):
            for t in range(ten_size):
                to = (d * seq_size + (s ^ (2 * ry))) * ten_size + (t ^ rp)
                pairs.append(((d * seq_size + s) * ten_size + t, to))
    return lax.ppermute(value, AXES, pairs)


def gather_block(block, order, mesh_shape):
    cur = block[None]
    for bit in order[:3]:
        cur = jnp.concatenate([cur, swap(cur, bit, mesh_shape)], axis=0)
    more = swap(cur, order[3], mesh_shape)
    return [cur, more, swap(cur, "c", mesh_shape), swap(more, "c", mesh_shape)]


def scatter_sum(parts, order, mesh_shape):
    parts = list(parts)
    for step in range(4):
        got = swap(parts[step].astype(BF), order[step], mesh_shape).astype(F32)
        for later in range(step + 1, 5):
            size = 8 >> later if later < 4 else 1
            start = size if later < 4 else 0
            parts[later] = parts[later].astype(F32) + got[start : start + size]
    return parts[4][0]


def part_of(rel, order):
    flags = [1 if rel & BITS[b] else 0 for b in order]
    for step in range(4):
        if flags[step]:
            place = 0
            for f in flags[step + 1 :]:
                place = place * 2 + f
            return step, place
    return 4, 0


def place():
    dp, seq, ten = lax.axis_index("dp"), lax.axis_index("seq"), lax.axis_index("tensor")
    return lax.rem(dp, 2), lax.div(seq, 2), lax.rem(seq, 2), ten


def xor_bit(value, flag):
    return 1 - value if flag else value


def xor_two(value, flags):
    if flags == 0:
        return value
    high, low = lax.div(value, 2), lax.rem(value, 2)
    return xor_bit(high, flags & 2) * 2 + xor_bit(low, flags & 1)


def row_block(x, y, c, rel):
    return (xor_bit(x, rel & 16) * 2 + xor_bit(y, rel & 8)) * 2 + xor_bit(c, rel & 4)


def group_of(y, ten, pair):
    return xor_bit(y, pair & 2) * 2 + xor_bit(lax.rem(ten, 2), pair & 1)


class Loader:
    def __init__(self, refs, orders, scratch, sems, col=0, width=None):
        x, y, c, ten = place()
        self.copies = {rz: [] for rz in range(4)}
        count = 0
        rows = 96 // len(orders)
        for n, order in enumerate(orders):
            for a in range(4):
                ref = refs[n * 4 + a]
                for j in range(8):
                    rel = sum(BITS[order[k]] for k in range(3) if j & (1 << k))
                    rel |= BITS[order[3]] if a & 1 else 0
                    rel |= BITS["c"] if a & 2 else 0
                    row = row_block(x, y, c, rel) * 96 + n * rows
                    dst = scratch.at[xor_two(ten, rel & 3), pl.ds(pl.multiple_of(row, 32), rows)]
                    src = ref.at[j] if width is None else ref.at[j, :, pl.ds(col, width)]
                    self.copies[rel & 3].append(pltpu.make_async_copy(src, dst, sems.at[count]))
                    count += 1
        self.ten = ten

    def start(self):
        for rz in range(4):
            for copy in self.copies[rz]:
                copy.start()

    def wait(self, rz):
        for copy in self.copies[rz]:
            copy.wait()

    def index(self, rz):
        return xor_two(self.ten, rz)


def dot_nn(left, right):
    return jnp.dot(left, right, preferred_element_type=F32)


def dot_nt(left, right):
    return lax.dot_general(left, right, (((1,), (1,)), ((), ())), preferred_element_type=F32)


def norm_parts(value):
    center = value - jnp.mean(value, axis=-1, keepdims=True)
    spread = jnp.mean(center * center, axis=-1, keepdims=True)
    rstd = lax.rsqrt(spread + 1e-05)
    return center * rstd, rstd


def norm_back(hat, rstd, gain, grad):
    scaled = grad * gain
    first = jnp.mean(scaled, axis=-1, keepdims=True)
    second = jnp.mean(scaled * hat, axis=-1, keepdims=True)
    return rstd * (scaled - first - hat * second)


def put_transposed(value, turned, own_ref, other_ref):
    x, y, c, _ = place()
    turned[...] = value.T
    for xy in range(4):
        for side, ref in ((0, own_ref), (4, other_ref)):
            row = row_block(x, y, c, (16 if xy & 2 else 0) | (8 if xy & 1 else 0) | side) * 96
            ref[pl.ds(xy * 96, 96), :] = turned[pl.ds(pl.multiple_of(row, 32), 96), :].astype(BF)


def call(kernel, outs, scratch, specs, args, flops=0, name=None):
    return pl.pallas_call(
        kernel,
        out_shape=[jax.ShapeDtypeStruct(s, d) for s, d in outs],
        in_specs=specs,
        out_specs=[SPEC_V] * len(outs),
        scratch_shapes=scratch,
        compiler_params=pltpu.CompilerParams(vmem_limit_bytes=VMEM_LIMIT),
        cost_estimate=pl.CostEstimate(flops=flops, bytes_accessed=4000000, transcendentals=0),
        name=name,
    )(*args)


def project_kernel(n_a, x_ref, vec_ref, bias_ref, *refs):
    a_refs, refs = refs[:n_a], refs[n_a:]
    outs, (own_ref, other_ref, w, turned, sems) = refs[:4], refs[4:]
    load = Loader(a_refs, ORDERS_A if n_a == 12 else (ORDER_A,), w, sems, 0, 640)
    load.start()
    _, y, _, ten = place()
    hat, _ = norm_parts(x_ref[...].astype(F32))
    normed = hat * vec_ref[0:1, :] + vec_ref[1:2, :]
    low = normed.astype(BF)
    put_transposed(normed, turned, own_ref, other_ref)
    for rz in range(4):
        load.wait(rz)
    for pair in range(4):
        g = group_of(y, ten, pair)
        packed = dot_nn(low, w[g])[:, :576] + bias_ref[g]
        outs[pair][...] = packed.astype(BF)


ORDER_A = ("z2", "x", "y", "z1")


def project(x, vec, bias, a, tokens):
    outs = [((tokens, 576), BF)] * 4 + [((384, tokens), BF)] * 2
    scratch = [pltpu.VMEM((4, 768, 640), BF), pltpu.VMEM((768, tokens), F32), pltpu.SemaphoreType.DMA((8 * len(a),))]
    return call(
        partial(project_kernel, len(a)), outs, scratch, [SPEC_V] * 3 + [SPEC_A] * len(a), (x, vec, bias, *a),
        flops=2 * tokens * 768 * 2304, name="project",
    )


def attend_kernel(count_ref, p0, p1, p2, p3, o0, o1, o2, o3, m0, m1, m2, m3, kv_ref, q_ref, mixed_ref, lse_ref):
    _, y, c, ten = place()
    tokens = p0.shape[0]
    half = lax.rem(ten, 2)
    for pair, (p, o) in enumerate(((p0, o0), (p1, o1), (p2, o2), (p3, o3))):
        for side, ref in ((0, p), (1, o)):
            block = (xor_bit(y, pair & 2) * 2 + xor_bit(c, side)) * 2 + xor_bit(half, pair & 1)
            kv_ref[pl.ds(pl.multiple_of(block * tokens, 64), tokens), :] = ref[:, :384]
        q_ref[pl.ds(pair * tokens, tokens), :] = p[:, 384:576] * jnp.asarray(HD ** (-0.5), BF)
    total = kv_ref.shape[0]
    count = count_ref[0]
    ones = jnp.ones((total, HD), BF)
    valid = lax.broadcasted_iota(jnp.int32, (tokens, 128), 1) + (total - 128) < count
    for h in range(3):
        keys = kv_ref[:, h * HD : (h + 1) * HD]
        values = jnp.concatenate([kv_ref[:, 192 + h * HD : 192 + (h + 1) * HD], ones], axis=1)
        for pair, m in enumerate((m0, m1, m2, m3)):
            rows = pl.ds(pair * tokens, tokens)
            scores = dot_nt(q_ref[rows, h * HD : (h + 1) * HD], keys)
            last = jnp.where(valid, scores[:, total - 128 :], -1000000000.0)
            scores = jnp.concatenate([scores[:, : total - 128], last], axis=1)
            highest = jnp.max(scores, axis=-1, keepdims=True)
            expo = jnp.exp(scores - highest).astype(BF)
            both = dot_nn(expo, values)
            weight = both[:, HD : HD + 1]
            mixed = both[:, :HD] / weight
            mixed_ref[rows, h * HD : (h + 1) * HD] = mixed
            m[:, h * HD : (h + 1) * HD] = mixed.astype(BF)
            lse_ref[rows, h : h + 1] = highest + jnp.log(weight)


def attend(count, pieces, others):
    tokens = pieces[0].shape[0]
    outs = [((tokens, 192), BF)] * 4 + [
        ((8 * tokens, 384), BF),
        ((4 * tokens, 192), BF),
        ((4 * tokens, 192), F32),
        ((4 * tokens, 128), F32),
    ]
    return call(
        attend_kernel, outs, [], [SPEC_S] + [SPEC_V] * 8, (count, *pieces, *others),
        flops=4 * 4 * tokens * 8 * tokens * 192 * 4, name="attend",
    )


def mlp_kernel(n_a, m0, m1, m2, m3, x_ref, vec_ref, eb_ref, *refs):
    a_refs, e_refs, s_refs, refs = refs[:n_a], refs[n_a : n_a + 4], refs[n_a + 4 : n_a + 8], refs[n_a + 8 :]
    (x_out, after_ref, mixed_ref, own_ref, other_ref, active_ref, slope_ref, wo, we, ws, turned, sa, se, ss) = refs
    load_a = Loader(a_refs, ORDERS_A if n_a == 12 else (ORDER_A,), wo, sa, 512, 256)
    load_e = Loader(e_refs, (ORDER_E,), we, se)
    load_s = Loader(s_refs, (ORDER_S,), ws, ss)
    load_a.start()
    load_e.start()
    load_s.start()
    _, y, _, ten = place()
    for rz in range(4):
        load_a.wait(rz)
    after = x_ref[...].astype(F32) + vec_ref[2:3, :]
    for pair, m in enumerate((m0, m1, m2, m3)):
        g = group_of(y, ten, pair)
        piece = m[...]
        mixed_ref[g] = piece
        after = after + dot_nt(piece, wo[g][:, 64:])
    after_ref[...] = after
    hat, _ = norm_parts(after)
    normed = hat * vec_ref[3:4, :] + vec_ref[4:5, :]
    low = normed.astype(BF)
    put_transposed(normed, turned, own_ref, other_ref)
    out = after + vec_ref[5:6, :]
    for rz in range(4):
        z = load_e.index(rz)
        load_e.wait(rz)
        hidden = dot_nn(low, we[z]) + eb_ref[z]
        lower = 0.5 * (1.0 + lax.erf(hidden * 0.7071067811865476))
        slope_ref[z] = lower + hidden * (jnp.exp(-0.5 * hidden * hidden) * 0.3989422804014327)
        active = (hidden * lower).astype(BF)
        active_ref[z] = active
        load_s.wait(rz)
        out = out + dot_nt(active, ws[z])
    x_out[...] = out


def mlp(pieces, x, vec, eb, a, e, s):
    tokens = x.shape[0]
    outs = [
        ((tokens, 768), F32),
        ((tokens, 768), F32),
        ((4, tokens, 192), BF),
        ((384, tokens), BF),
        ((384, tokens), BF),
        ((4, tokens, 768), BF),
        ((4, tokens, 768), F32),
    ]
    scratch = [
        pltpu.VMEM((4, 768, 256), BF),
        pltpu.VMEM((4, 768, 768), BF),
        pltpu.VMEM((4, 768, 768), BF),
        pltpu.VMEM((768, tokens), F32),
        pltpu.SemaphoreType.DMA((8 * len(a),)),
        pltpu.SemaphoreType.DMA((32,)),
        pltpu.SemaphoreType.DMA((32,)),
    ]
    return call(
        partial(mlp_kernel, len(a)), outs, scratch, [SPEC_V] * 7 + [SPEC_A] * (len(a) + 8), (*pieces, x, vec, eb, *a, *e, *s),
        flops=2 * tokens * 768 * 6912, name="mlp",
    )


def mlp_back_kernel(n_a, dy_ref, after_ref, vec_ref, slope_ref, *refs):
    a_refs, e_refs, s_refs, refs = refs[:n_a], refs[n_a : n_a + 4], refs[n_a + 4 : n_a + 8], refs[n_a + 8 :]
    d_out, refs = refs[:4], refs[4:]
    (da_ref, hid_ref, z_own, z_other, a_own, a_other, sums_ref, ebs_ref, wo, we, ws, turned, sa, se, ss) = refs
    load_a = Loader(a_refs, ORDERS_A if n_a == 12 else (ORDER_A,), wo, sa, 512, 256)
    load_e = Loader(e_refs, (ORDER_E,), we, se)
    load_s = Loader(s_refs, (ORDER_S,), ws, ss)
    load_s.start()
    load_e.start()
    load_a.start()
    _, y, _, ten = place()
    dy = dy_ref[...].astype(F32)
    dz = dy.astype(BF)
    dz_wide = dz.astype(F32)
    put_transposed(dz_wide, turned, z_own, z_other)
    grad = jnp.zeros(dy.shape, F32)
    for rz in range(4):
        z = load_s.index(rz)
        load_s.wait(rz)
        d_active = dot_nn(dz, ws[z])
        d_hidden = (d_active * slope_ref[z]).astype(BF)
        hid_ref[z] = d_hidden
        ebs_ref[z] = jnp.sum(d_hidden.astype(F32), axis=0, keepdims=True)
        load_e.wait(rz)
        grad = grad + dot_nt(d_hidden, we[z])
    hat, rstd = norm_parts(after_ref[...])
    d_after = dy + norm_back(hat, rstd, vec_ref[3:4, :], grad)
    da_ref[...] = d_after
    da = d_after.astype(BF)
    da_wide = da.astype(F32)
    put_transposed(da_wide, turned, a_own, a_other)
    sums_ref[0:1, :] = jnp.sum(da_wide, axis=0, keepdims=True)
    sums_ref[1:2, :] = jnp.sum(grad * hat, axis=0, keepdims=True)
    sums_ref[2:3, :] = jnp.sum(grad, axis=0, keepdims=True)
    sums_ref[3:4, :] = jnp.sum(dz_wide, axis=0, keepdims=True)
    sums_ref[4:8, :] = jnp.zeros((4, dy.shape[1]), F32)
    for rz in range(4):
        load_a.wait(rz)
    for pair in range(4):
        g = group_of(y, ten, pair)
        d_out[pair][...] = dot_nn(da, wo[g])[:, 64:].astype(BF)


def mlp_back(dy, after, vec, slope, a, e, s):
    tokens = dy.shape[0]
    outs = [((tokens, 192), BF)] * 4 + [
        ((tokens, 768), F32),
        ((4, tokens, 768), BF),
        ((384, tokens), BF),
        ((384, tokens), BF),
        ((384, tokens), BF),
        ((384, tokens), BF),
        ((8, 768), F32),
        ((4, 1, 768), F32),
    ]
    scratch = [
        pltpu.VMEM((4, 768, 256), BF),
        pltpu.VMEM((4, 768, 768), BF),
        pltpu.VMEM((4, 768, 768), BF),
        pltpu.VMEM((768, tokens), F32),
        pltpu.SemaphoreType.DMA((8 * len(a),)),
        pltpu.SemaphoreType.DMA((32,)),
        pltpu.SemaphoreType.DMA((32,)),
    ]
    return call(
        partial(mlp_back_kernel, len(a)), outs, scratch, [SPEC_V] * 4 + [SPEC_A] * (len(a) + 8),
        (dy, after, vec, slope, *a, *e, *s), flops=2 * tokens * 768 * 6912, name="mlp_back",
    )


def attend_back_kernel(count_ref, d0, d1, d2, d3, kv_ref, q_ref, mixed_ref, lse_ref, dq_ref, own_ref, other_ref, do, inner, stat, dkv):
    _, y, c, ten = place()
    tokens = d0.shape[0]
    half = lax.rem(ten, 2)
    inner[...] = jnp.zeros(inner.shape, F32)
    for pair, d in enumerate((d0, d1, d2, d3)):
        rows = pl.ds(pair * tokens, tokens)
        grad = d[...]
        do[rows, :] = grad
        for h in range(3):
            cols = slice(h * HD, (h + 1) * HD)
            inner[rows, h : h + 1] = jnp.sum(grad[:, cols].astype(F32) * mixed_ref[rows, cols], axis=-1, keepdims=True)
    stat[0] = lse_ref[...].T
    stat[1] = inner[...].T
    total, queries = kv_ref.shape[0], q_ref.shape[0]
    count = count_ref[0]
    step = 256
    valid = lax.broadcasted_iota(jnp.int32, (128, step), 0) + (total - 128) < count
    for h in range(3):
        cols = slice(h * HD, (h + 1) * HD)
        keys = kv_ref[:, cols]
        values = kv_ref[:, 192 + h * HD : 192 + (h + 1) * HD]
        turned = keys.astype(F32).T.astype(BF)
        d_keys = jnp.zeros((total, HD), F32)
        d_values = jnp.zeros((total, HD), F32)
        for block in range(queries // step):
            rows = slice(block * step, (block + 1) * step)
            query = q_ref[rows, cols]
            grad = do[rows, cols]
            scores = dot_nt(keys, query)
            last = jnp.where(valid, scores[total - 128 :], -1000000000.0)
            scores = jnp.concatenate([scores[: total - 128], last], axis=0)
            probs = jnp.exp(scores - stat[0, h : h + 1, rows])
            d_probs = dot_nt(values, grad)
            d_scores = (probs * (d_probs - stat[1, h : h + 1, rows])).astype(BF)
            d_values = d_values + dot_nn(probs.astype(BF), grad)
            d_keys = d_keys + dot_nn(d_scores, query)
            d_query = dot_nn(turned, d_scores) * HD ** (-0.5)
            dq_ref[rows, cols] = d_query.T.astype(BF)
        dkv[:, cols] = d_keys.astype(BF)
        dkv[:, 192 + h * HD : 192 + (h + 1) * HD] = d_values.astype(BF)
    for pair in range(4):
        for side, ref in ((0, own_ref), (1, other_ref)):
            block = (xor_bit(y, pair & 2) * 2 + xor_bit(c, side)) * 2 + xor_bit(half, pair & 1)
            ref[pair] = dkv[pl.ds(pl.multiple_of(block * tokens, 64), tokens), :]


def attend_back(count, pieces, kv, q, mixed, lse):
    tokens = pieces[0].shape[0]
    outs = [((4 * tokens, 192), BF), ((4, tokens, 384), BF), ((4, tokens, 384), BF)]
    scratch = [
        pltpu.VMEM((4 * tokens, 192), BF),
        pltpu.VMEM((4 * tokens, 128), F32),
        pltpu.VMEM((2, 128, 4 * tokens), F32),
        pltpu.VMEM((8 * tokens, 384), BF),
    ]
    return call(
        attend_back_kernel, outs, scratch, [SPEC_S] + [SPEC_V] * 8, (count, *pieces, kv, q, mixed, lse),
        flops=10 * 4 * tokens * 8 * tokens * 192 * 4, name="attend_back",
    )


def project_back_kernel(n_a, d0, d1, d2, d3, da_ref, x_ref, vec_ref, *refs):
    a_refs, refs = refs[:n_a], refs[n_a:]
    dx_ref, dqkv_ref, sums_ref, bias_ref, w, sems = refs
    load = Loader(a_refs, ORDERS_A if n_a == 12 else (ORDER_A,), w, sems, 0, 640)
    load.start()
    _, y, _, ten = place()
    hat, rstd = norm_parts(x_ref[...].astype(F32))
    for rz in range(4):
        load.wait(rz)
    grad = jnp.zeros(hat.shape, F32)
    for pair, d in enumerate((d0, d1, d2, d3)):
        g = group_of(y, ten, pair)
        piece = d[...]
        dqkv_ref[g] = piece
        bias_ref[g] = jnp.sum(piece.astype(F32), axis=0, keepdims=True)
        grad = grad + dot_nt(piece, w[g][:, :576])
    dx_ref[...] = da_ref[...] + norm_back(hat, rstd, vec_ref[0:1, :], grad)
    sums_ref[0:1, :] = jnp.sum(grad * hat, axis=0, keepdims=True)
    sums_ref[1:2, :] = jnp.sum(grad, axis=0, keepdims=True)
    sums_ref[2:8, :] = jnp.zeros((6, hat.shape[1]), F32)


def project_back(pieces, da, x, vec, a):
    tokens = x.shape[0]
    outs = [((tokens, 768), F32), ((4, tokens, 576), BF), ((8, 768), F32), ((4, 1, 576), F32)]
    scratch = [pltpu.VMEM((4, 768, 640), BF), pltpu.SemaphoreType.DMA((8 * len(a),))]
    return call(
        partial(project_back_kernel, len(a)), outs, scratch, [SPEC_V] * 7 + [SPEC_A] * len(a), (*pieces, da, x, vec, *a),
        flops=2 * tokens * 768 * 2304, name="project_back",
    )


def emit(value, rz, order, outs):
    for xy in range(4):
        part, at = part_of((16 if xy & 2 else 0) | (8 if xy & 1 else 0) | rz, order)
        outs[part][at] = value[xy * 96 : (xy + 1) * 96].astype(BF)


def weigh_kernel(order, l_own, l_got, r_own, r_got, *outs):
    _, _, _, ten = place()
    for rz in range(4):
        z = xor_two(ten, rz)
        emit(dot_nn(l_own[...], r_own[z]) + dot_nn(l_got[...], r_got[z]), rz, order, outs)


def weigh(order, l_own, l_got, r_own, r_got, name):
    outs = [((n, 96, 768), BF) for n in (8, 4, 2, 1, 1)]
    return call(
        partial(weigh_kernel, order), outs, [], [SPEC_V] * 4, (l_own, l_got, r_own, r_got),
        flops=4 * r_own.shape[1] * 384 * 3072, name=name,
    )


def weigh_attention_kernel(order, n_own, n_got, a_own, a_got, q_own, q_got, m_own, m_got, *outs):
    _, _, _, ten = place()
    for rz in range(4):
        z = xor_two(ten, rz)
        qkv = dot_nn(n_own[...], q_own[z]) + dot_nn(n_got[...], q_got[z])
        out = dot_nn(a_own[...], m_own[z]) + dot_nn(a_got[...], m_got[z])
        emit(jnp.concatenate([qkv, out], axis=1), rz, order, outs)


def weigh_attention(order, args):
    outs = [((n, 96, 768), BF) for n in (8, 4, 2, 1, 1)]
    return call(
        partial(weigh_attention_kernel, order), outs, [], [SPEC_V] * 8, args,
        flops=4 * args[4].shape[1] * 384 * 3072, name="weigh_attention",
    )


def spread_kernel(p0, p1, p2, p3, out_ref):
    ten = lax.axis_index("tensor")
    for rz, p in enumerate((p0, p1, p2, p3)):
        out_ref[xor_two(ten, rz)] = p[...].astype(out_ref.dtype)


def spread(block, dtype, shape):
    first = swap(block, "z1", shape)
    second = swap(block, "z2", shape)
    third = swap(first, "z2", shape)
    tokens, width = block.shape
    out = call(
        spread_kernel, [((4, tokens, width), dtype)], [], [SPEC_V] * 4, (block, first, second, third), name="spread"
    )[0]
    return out.reshape(2, 1, 2 * tokens, width)


def small_params(vectors, qv_bias, expand_bias, shape):
    dp_size, seq_size, ten_size = shape
    if dp_size == 2:
        pad = lambda v: jnp.pad(v, ((0, 0), (0, 0), (0, 128 - v.shape[2])))
        rows = jnp.concatenate(
            [pad(vectors), pad(expand_bias[:, None]), pad(qv_bias.reshape(LAYERS, 1, 48))], axis=1
        ).reshape(1, LAYERS * 8, 128)
        for bit in ("z1", "z2", "c", "y", "x"):
            rows = jnp.concatenate([rows, swap(rows, bit, shape)], axis=0)
        x, y, c, ten = place()
        me = ((x * 2 + y) * 2 + c) * 4 + ten
        order = jnp.bitwise_xor(jnp.arange(32, dtype=jnp.int32), me)
        pick = (order[:, None] == jnp.arange(32, dtype=jnp.int32)[None, :]).astype(BF)
        every = jnp.dot(pick, rows.reshape(32, -1), preferred_element_type=F32)
        every = every.reshape(8, 4, LAYERS, 8, 128)
        vec = every[:, 0, :, :6, :96].transpose(1, 2, 0, 3).reshape(LAYERS, 6, 768)
        eb = every[:, :, :, 6, :96].transpose(2, 1, 0, 3).reshape(LAYERS, 4, 1, 768)
        qv = every[:, :, :, 7, :48].reshape(8, 4, LAYERS, 2, 24).transpose(2, 3, 1, 0, 4).reshape(LAYERS, 2, 4, 192)
    else:
        vec = lax.all_gather(vectors, ("dp", "seq"), axis=2, tiled=True).astype(F32)
        eb = lax.all_gather(expand_bias, ("tensor", "dp", "seq"), axis=1, tiled=True)
        eb = eb.astype(F32).reshape(LAYERS, 4, 1, 768)
        qv = lax.all_gather(qv_bias, ("tensor", "dp", "seq"), axis=2, tiled=True)
        qv = qv.astype(F32).reshape(LAYERS, 2, 4, 192)
    qvb = jnp.concatenate([jnp.zeros_like(qv[:, 0]), qv[:, 1], qv[:, 0]], axis=-1)[:, :, None, :]
    return jnp.pad(vec, ((0, 0), (0, 2), (0, 0))), qvb, eb


def body(shape, features, upstream, key_mask, vectors, proj_qkv, qv_bias, proj_out, expand_weight, expand_bias, shrink_weight):
    dp_size, seq_size, ten_size = shape
    dp, seq, ten = lax.axis_index("dp"), lax.axis_index("seq"), lax.axis_index("tensor")
    tokens = features.shape[2] // 2
    at = (lax.div(ten, 2), 0, lax.rem(ten, 2) * tokens, 0)
    x0 = lax.dynamic_slice(features, at, (1, 1, tokens, 768)).reshape(tokens, 768)
    dy0 = lax.dynamic_slice(upstream, at, (1, 1, tokens, 768)).reshape(tokens, 768)
    count = jnp.sum(lax.dynamic_slice(key_mask, (lax.div(ten, 2), 0, 0), (1, 1, key_mask.shape[2])), axis=(1, 2))

    width = proj_qkv.shape[1]
    wa = jnp.concatenate(
        [
            proj_qkv[:, :, 1],
            proj_qkv[:, :, 2],
            proj_qkv[:, :, 0],
            proj_out.transpose(0, 2, 1),
        ],
        axis=-1,
    )
    we = expand_weight
    ws = shrink_weight.transpose(0, 2, 1)
    if dp_size != 2:
        start = (lax.rem(dp, 2) * 4 + seq) * 96
        wa, we, ws = (
            lax.dynamic_slice_in_dim(lax.all_gather(w, ("dp", "seq"), axis=1, tiled=True), start, 96, axis=1)
            for w in (wa, we, ws)
        )
    vec, qvb, eb = small_params(vectors, qv_bias, expand_bias, shape)
    a_w = [
        [g for n, order in enumerate(ORDERS_A) for g in gather_block(wa[0, n * 32 : (n + 1) * 32], order, shape)],
        gather_block(wa[1], ORDER_A, shape),
    ]
    e_w = [gather_block(we[d], ORDER_E, shape) for d in range(LAYERS)]
    s_w = [gather_block(ws[d], ORDER_S, shape) for d in range(LAYERS)]

    state = x0
    kept = []
    for d in range(LAYERS):
        *pieces, n_own, n_other = project(state, vec[d], qvb[d], a_w[d], tokens)
        pieces = [pieces[0]] + [swap_group(pieces[p], p, shape) for p in (1, 2, 3)]
        others = [swap(p[:, :384], "c", shape) for p in pieces]
        *mixed, kv, q, mixed_wide, lse = attend(count, pieces, others)
        mixed = [mixed[0]] + [swap_group(mixed[p], p, shape) for p in (1, 2, 3)]
        x_in = state
        state, after, mixed_all, m_own, m_other, active, slope = mlp(mixed, x_in, vec[d], eb[d], a_w[d], e_w[d], s_w[d])
        kept.append((x_in, n_own, n_other, kv, q, mixed_wide, lse, after, mixed_all, m_own, m_other, active, slope))
    encoded = spread(state.astype(BF), BF, shape)

    grad = dy0
    g_a, g_e, g_s = [None] * LAYERS, [None] * LAYERS, [None] * LAYERS
    small = [None] * LAYERS
    for d in reversed(range(LAYERS)):
        x_in, n_own, n_other, kv, q, mixed_wide, lse, after, mixed_all, m_own, m_other, active, slope = kept[d]
        *d_mixed, d_after, d_hid, z_own, z_other, da_own, da_other, sums_two, ebs = mlp_back(
            grad, after, vec[d], slope, a_w[d], e_w[d], s_w[d]
        )
        d_mixed = [d_mixed[0]] + [swap_group(d_mixed[p], p, shape) for p in (1, 2, 3)]
        order_e, order_s = ORDER_E[::-1], ORDER_S[::-1]
        parts = weigh(order_e, m_own, swap(m_other, "c", shape), d_hid, swap(d_hid, "c", shape), "weigh_expand")
        g_e[d] = scatter_sum(parts, order_e, shape)
        parts = weigh(order_s, z_own, swap(z_other, "c", shape), active, swap(active, "c", shape), "weigh_shrink")
        g_s[d] = scatter_sum(parts, order_s, shape)
        dq, own, other = attend_back(count, d_mixed, kv, q, mixed_wide, lse)
        d_kv = (own.astype(F32) + swap(other, "c", shape).astype(F32)).astype(BF)
        back = [jnp.concatenate([d_kv[p], dq[p * tokens : (p + 1) * tokens]], axis=1) for p in range(4)]
        back = [back[0]] + [swap_group(back[p], p, shape) for p in (1, 2, 3)]
        grad, d_qkv, sums_one, qvs = project_back(back, d_after, x_in, vec[d], a_w[d])
        order_a = ORDER_A[::-1]
        parts = weigh_attention(
            order_a,
            (
                n_own,
                swap(n_other, "c", shape),
                da_own,
                swap(da_other, "c", shape),
                d_qkv,
                swap(d_qkv, "c", shape),
                mixed_all,
                swap(mixed_all, "c", shape),
            ),
        )
        g_a[d] = scatter_sum(parts, order_a, shape)
        total = jnp.concatenate(
            [sums_one[:2], sums_two[:4], ebs.reshape(4, 768), jnp.pad(qvs.reshape(4, 576), ((0, 2), (0, 192)))], axis=0
        )
        if dp_size == 2:
            for bit in ("c", "x", "y", "z1", "z2"):
                total = total + swap(total, bit, shape)
        else:
            total = lax.psum(total, AXES)
        small[d] = total
    grad_features = spread(grad.astype(BF), F32, shape)

    if dp_size != 2:
        start = (lax.rem(dp, 2) * 4 + seq) * 96

        def down(block):
            whole = lax.dynamic_update_slice_in_dim(jnp.zeros((768, 768), F32), block, start, axis=0)
            return lax.psum_scatter(whole, ("dp", "seq"), scatter_dimension=0, tiled=True)

        g_a, g_e, g_s = ([down(g) for g in gs] for gs in (g_a, g_e, g_s))
    ga, ge, gs = jnp.stack(g_a), jnp.stack(g_e), jnp.stack(g_s)
    g_small = jnp.stack(small)
    mine = dp * seq_size + seq
    grad_vectors = lax.dynamic_slice_in_dim(g_small[:, :6], mine * width, width, axis=2)
    eb_width, qv_width = expand_bias.shape[1], qv_bias.shape[2]
    grad_eb = lax.dynamic_slice_in_dim(
        lax.dynamic_index_in_dim(g_small[:, 6:10], ten, axis=1, keepdims=False), mine * eb_width, eb_width, axis=1
    )
    qv = lax.dynamic_index_in_dim(g_small[:, 10:14], ten, axis=1, keepdims=False)
    grad_qv = jnp.stack(
        [
            lax.dynamic_slice_in_dim(qv[:, 384:576], mine * qv_width, qv_width, axis=1),
            lax.dynamic_slice_in_dim(qv[:, 192:384], mine * qv_width, qv_width, axis=1),
        ],
        axis=1,
    )
    grad_qkv = jnp.stack([ga[:, :, 384:576], ga[:, :, :192], ga[:, :, 192:384]], axis=2)
    return (
        encoded,
        grad_features,
        grad_vectors,
        grad_qkv,
        grad_qv,
        ga[:, :, 576:].transpose(0, 2, 1),
        ge,
        grad_eb,
        gs.transpose(0, 2, 1),
    )


def solution(mesh):
    placed = (
        P(None, "dp", "seq", None),
        P(None, "dp", "seq", None),
        P(None, "dp", None),
        P(None, None, ("dp", "seq")),
        P(None, ("dp", "seq"), None, "tensor"),
        P(None, None, ("tensor", "dp", "seq")),
        P(None, "tensor", ("dp", "seq")),
        P(None, ("dp", "seq"), "tensor"),
        P(None, ("tensor", "dp", "seq")),
        P(None, "tensor", ("dp", "seq")),
    )
    shape = tuple(mesh.shape[axis] for axis in AXES)
    return jax.shard_map(
        partial(body, shape),
        mesh=mesh,
        in_specs=placed,
        out_specs=(
            P(None, "dp", "seq", None),
            P(None, "dp", "seq", None),
            P(None, None, ("dp", "seq")),
            P(None, ("dp", "seq"), None, "tensor"),
            P(None, None, ("tensor", "dp", "seq")),
            P(None, "tensor", ("dp", "seq")),
            P(None, ("dp", "seq"), "tensor"),
            P(None, ("tensor", "dp", "seq")),
            P(None, "tensor", ("dp", "seq")),
        ),
        check_vma=False,
    )
```

```python
from functools import partial

import jax
import jax.numpy as jnp
from jax import lax
from jax.experimental import pallas as pl
from jax.experimental.pallas import tpu as pltpu
from jax.sharding import PartitionSpec as P

HD = 64
LAYERS = 2
AXES = ("dp", "seq", "tensor")
BF = jnp.bfloat16
F32 = jnp.float32
LIMIT = 48
COST = 3.0e8

BITS = {"x": 16, "y": 8, "c": 4, "z2": 2, "z1": 1}

ORDER_E = ("z2", "z1", "x", "y")
ORDER_S = ("z2", "y", "z1", "x")
ORDER_A = ("z2", "x", "y", "z1")
SUM_A = (("x", "y", "z1", "z2"), ("y", "x", "z1", "z2"))
RING = (0, 1, 3, 2)


SPEC_V = pl.BlockSpec(memory_space=pltpu.VMEM)
SPEC_S = pl.BlockSpec(memory_space=pltpu.SMEM)
SPEC_A = pl.BlockSpec(memory_space=pl.ANY)


def swap(value, bit, mesh_shape):
    dp_size, seq_size, ten_size = mesh_shape
    pairs = []
    for d in range(dp_size):
        for s in range(seq_size):
            for t in range(ten_size):
                e, u, v = d, s, t
                if bit == "x":
                    e = d ^ 1
                elif bit == "y":
                    u = s ^ 2
                elif bit == "c":
                    u = s ^ 1
                elif bit == "z2":
                    v = t ^ 2
                else:
                    v = t ^ 1
                pairs.append(((d * seq_size + s) * ten_size + t, (e * seq_size + u) * ten_size + v))
    return lax.ppermute(value, AXES, pairs)


def swap_group(value, pair, mesh_shape):
    dp_size, seq_size, ten_size = mesh_shape
    ry, rp = pair >> 1, pair & 1
    pairs = []
    for d in range(dp_size):
        for s in range(seq_size):
            for t in range(ten_size):
                to = (d * seq_size + (s ^ (2 * ry))) * ten_size + (t ^ rp)
                pairs.append(((d * seq_size + s) * ten_size + t, to))
    return lax.ppermute(value, AXES, pairs)


def fence(*values):
    return lax.optimization_barrier(values)


class Gatherer:
    def __init__(self, blocks, orders, mesh_shape):
        self.cur, self.orders, self.mesh_shape, self.step = [b[None] for b in blocks], orders, mesh_shape, 0

    def go(self):
        got = [swap(c, o[self.step], self.mesh_shape) for c, o in zip(self.cur, self.orders)]
        self.step += 1
        if self.step < 4:
            self.cur = list(fence(*(jnp.concatenate([c, g], axis=0) for c, g in zip(self.cur, got))))
        else:
            self.more = list(fence(*got))

    def wait(self, *values):
        count = len(self.cur)
        out = fence(*self.cur, *values)
        self.cur = list(out[:count])
        return out[count:]

    def before(self, *values):
        now = self.more if self.step == 4 else self.cur
        count = len(now)
        out = fence(*now, *values)
        if self.step == 4:
            self.more = list(out[:count])
        else:
            self.cur = list(out[:count])
        return out[count:]

    def core(self):
        turned = [[swap(v, "c", self.mesh_shape) for v in pair] for pair in zip(self.cur, self.more)]
        return [[c, m, *t] for c, m, t in zip(self.cur, self.more, turned)]


class Reducer:
    def __init__(self, parts, order, mesh_shape):
        self.parts, self.order, self.mesh_shape, self.step = list(parts), order, mesh_shape, 0

    def send(self):
        return swap(self.parts[self.step].astype(BF), self.order[self.step], self.mesh_shape)

    def take(self, got):
        step = self.step
        for later in range(step + 1, 5):
            size = 8 >> later if later < 4 else 1
            start = size if later < 4 else 0
            self.parts[later] = self.parts[later].astype(F32) + got[start : start + size].astype(F32)
        self.step += 1

    def finish(self):
        return self.parts[4][0]


class Together:
    def __init__(self, sums):
        self.sums = sums

    def wait(self, *values):
        out = list(fence(*(r.parts[r.step] for r in self.sums), *values))
        for r in self.sums:
            r.parts[r.step] = out.pop(0)
        return out

    def go(self, *others):
        got = [r.send() for r in self.sums]
        out = fence(*got, *others)
        for r, g in zip(self.sums, out):
            r.take(g)
        return out[len(got) :]


def part_of(rel, order):
    flags = [1 if rel & BITS[b] else 0 for b in order]
    for step in range(4):
        if flags[step]:
            place = 0
            for f in flags[step + 1 :]:
                place = place * 2 + f
            return step, place
    return 4, 0


def place():
    dp, seq, ten = lax.axis_index("dp"), lax.axis_index("seq"), lax.axis_index("tensor")
    return lax.rem(dp, 2), lax.div(seq, 2), lax.rem(seq, 2), ten


def xor_bit(value, flag):
    return 1 - value if flag else value


def xor_two(value, flags):
    if flags == 0:
        return value
    high, low = lax.div(value, 2), lax.rem(value, 2)
    return xor_bit(high, flags & 2) * 2 + xor_bit(low, flags & 1)


def row_block(x, y, c, rel):
    return (xor_bit(x, rel & 16) * 2 + xor_bit(y, rel & 8)) * 2 + xor_bit(c, rel & 4)


def group_of(y, ten, pair):
    return xor_bit(y, pair & 2) * 2 + xor_bit(lax.rem(ten, 2), pair & 1)


class Loader:
    def __init__(self, refs, orders, scratch, sems, row=0, col=0, width=768):
        x, y, c, ten = place()
        self.copies = {k: [] for k in range(4)}
        self.ten = None if len(refs) == 1 else ten
        if len(refs) == 1:
            for n in range(32):
                block, key = divmod(n, 4)
                dst = scratch.at[key, pl.ds(block * 96, 96)]
                src = refs[0].at[n, pl.ds(row, 96), pl.ds(col, width)]
                self.copies[key].append(pltpu.make_async_copy(src, dst, sems.at[n]))
            return
        rows = 96 * 4 // len(refs)
        for n in range(8 * len(refs)):
            a, j = divmod(n, 8)
            order = orders[a // 4]
            rel = sum(BITS[order[k]] for k in range(3) if j & (1 << k))
            rel |= BITS[order[3]] if a & 1 else 0
            rel |= BITS["c"] if a & 2 else 0
            to = pl.multiple_of(row_block(x, y, c, rel) * 96 + a // 4 * rows, 32)
            dst = scratch.at[xor_two(ten, rel & 3), pl.ds(to, rows)]
            src = refs[a].at[j, pl.ds(0, rows), pl.ds(col, width)]
            self.copies[rel & 3].append(pltpu.make_async_copy(src, dst, sems.at[n]))

    def start(self):
        for k in range(4):
            for copy in self.copies[k]:
                copy.start()

    def wait(self, k):
        for copy in self.copies[k]:
            copy.wait()

    def index(self, k):
        return k if self.ten is None else xor_two(self.ten, k)


def dot_nn(left, right):
    return jnp.dot(left, right, preferred_element_type=F32)


def dot_nt(left, right):
    return lax.dot_general(left, right, (((1,), (1,)), ((), ())), preferred_element_type=F32)


def norm_parts(value):
    center = value - jnp.mean(value, axis=-1, keepdims=True)
    spread = jnp.mean(center * center, axis=-1, keepdims=True)
    rstd = lax.rsqrt(spread + 1e-05)
    return center * rstd, rstd


def norm_back(hat, rstd, gain, grad):
    scaled = grad * gain
    first = jnp.mean(scaled, axis=-1, keepdims=True)
    second = jnp.mean(scaled * hat, axis=-1, keepdims=True)
    return rstd * (scaled - first - hat * second)


def put_transposed(value, turned, own_ref, other_ref, absolute=False):
    x, y, c, _ = place()
    turned[...] = value.T
    for xy in range(4):
        for side, ref in ((0, own_ref), (4, other_ref)):
            if absolute:
                row = (2 * xy + xor_bit(c, side)) * 96
            else:
                row = row_block(x, y, c, (16 if xy & 2 else 0) | (8 if xy & 1 else 0) | side) * 96
            ref[pl.ds(xy * 96, 96), :] = turned[pl.ds(pl.multiple_of(row, 32), 96), :].astype(BF)


def call(kernel, outs, scratch, specs, args, micros=1, name=None, ties=(), limit=LIMIT):
    return pl.pallas_call(
        lambda *refs: kernel(*refs[len(ties) :]),
        out_shape=[jax.ShapeDtypeStruct(s, d) for s, d in outs],
        in_specs=[SPEC_A] * len(ties) + list(specs),
        out_specs=[SPEC_V] * len(outs),
        scratch_shapes=scratch,
        compiler_params=pltpu.CompilerParams(vmem_limit_bytes=limit * 1024 * 1024),
        cost_estimate=pl.CostEstimate(flops=int(micros * COST), bytes_accessed=1000, transcendentals=0),
        name=name,
    )(*ties, *args)


def project_kernel(n_a, x_ref, vec_ref, bias_ref, *refs):
    a_refs, refs = refs[:n_a], refs[n_a:]
    outs, (own_ref, other_ref, w, turned, sems) = refs[:4], refs[4:]
    load = Loader(a_refs, (ORDER_A,), w, sems, 0, 0, 640)
    load.start()
    _, y, _, ten = place()
    hat, _ = norm_parts(x_ref[...].astype(F32))
    normed = hat * vec_ref[0:1, :] + vec_ref[1:2, :]
    low = normed.astype(BF)
    put_transposed(normed, turned, own_ref, other_ref, n_a == 1)
    for rz in range(4):
        load.wait(rz)
    for pair in range(4):
        g = group_of(y, ten, pair)
        packed = dot_nn(low, w[g])[:, :576] + bias_ref[g]
        outs[pair][...] = packed.astype(BF)


def project(x, vec, bias, a, tokens, ties=()):
    outs = [((tokens, 576), BF)] * 4 + [((384, tokens), BF)] * 2
    scratch = [pltpu.VMEM((4, 768, 640), BF), pltpu.VMEM((768, tokens), F32), pltpu.SemaphoreType.DMA((32,))]
    return call(
        partial(project_kernel, len(a)), outs, scratch, [SPEC_V] * 3 + [SPEC_A] * len(a), (x, vec, bias, *a),
        micros=4, name="project", ties=ties,
    )


def attend_kernel(count_ref, p0, p1, p2, p3, o0, o1, o2, o3, m0, m1, m2, m3, kv_ref, q_ref, mixed_ref, lse_ref):
    _, y, c, ten = place()
    tokens = p0.shape[0]
    half = lax.rem(ten, 2)
    for pair, (p, o) in enumerate(((p0, o0), (p1, o1), (p2, o2), (p3, o3))):
        for side, ref in ((0, p), (1, o)):
            block = (xor_bit(y, pair & 2) * 2 + xor_bit(c, side)) * 2 + xor_bit(half, pair & 1)
            kv_ref[pl.ds(pl.multiple_of(block * tokens, 64), tokens), :] = ref[:, :384]
        q_ref[pl.ds(pair * tokens, tokens), :] = p[:, 384:576] * jnp.asarray(HD ** (-0.5), BF)
    total = kv_ref.shape[0]
    count = count_ref[0]
    ones = jnp.ones((total, HD), BF)
    valid = lax.broadcasted_iota(jnp.int32, (tokens, 128), 1) + (total - 128) < count
    for h in range(3):
        keys = kv_ref[:, h * HD : (h + 1) * HD]
        values = jnp.concatenate([kv_ref[:, 192 + h * HD : 192 + (h + 1) * HD], ones], axis=1)
        for pair, m in enumerate((m0, m1, m2, m3)):
            rows = pl.ds(pair * tokens, tokens)
            scores = dot_nt(q_ref[rows, h * HD : (h + 1) * HD], keys)
            last = jnp.where(valid, scores[:, total - 128 :], -1000000000.0)
            scores = jnp.concatenate([scores[:, : total - 128], last], axis=1)
            highest = jnp.max(scores, axis=-1, keepdims=True)
            expo = jnp.exp(scores - highest).astype(BF)
            both = dot_nn(expo, values)
            weight = both[:, HD : HD + 1]
            mixed = both[:, :HD] / weight
            mixed_ref[rows, h * HD : (h + 1) * HD] = mixed
            m[:, h * HD : (h + 1) * HD] = mixed.astype(BF)
            lse_ref[rows, h : h + 1] = highest + jnp.log(weight)


def attend(count, pieces, others, ties=()):
    tokens = pieces[0].shape[0]
    outs = [((tokens, 192), BF)] * 4 + [
        ((8 * tokens, 384), BF),
        ((4 * tokens, 192), BF),
        ((4 * tokens, 192), F32),
        ((4 * tokens, 128), F32),
    ]
    return call(
        attend_kernel, outs, [], [SPEC_S] + [SPEC_V] * 8, (count, *pieces, *others),
        micros=7, name="attend", ties=ties,
    )


def mlp_kernel(n_a, n_e, m0, m1, m2, m3, x_ref, vec_ref, eb_ref, *refs):
    a_refs, e_refs = refs[:n_a], refs[n_a : n_a + n_e]
    s_refs, refs = refs[n_a + n_e : n_a + 2 * n_e], refs[n_a + 2 * n_e :]
    (x_out, after_ref, mixed_ref, own_ref, other_ref, active_ref, slope_ref, wo, we, ws, turned, sa, se, ss) = refs
    load_a = Loader(a_refs, (ORDER_A,), wo, sa, 0, 512, 256)
    load_e = Loader(e_refs, (ORDER_E,), we, se, 96)
    load_s = Loader(s_refs, (ORDER_S,), ws, ss, 192)
    load_a.start()
    load_e.start()
    load_s.start()
    _, y, _, ten = place()
    for rz in range(4):
        load_a.wait(rz)
    after = x_ref[...].astype(F32) + vec_ref[2:3, :]
    for pair, m in enumerate((m0, m1, m2, m3)):
        g = group_of(y, ten, pair)
        piece = m[...]
        mixed_ref[g] = piece
        after = after + dot_nt(piece, wo[g][:, 64:])
    after_ref[...] = after
    hat, _ = norm_parts(after)
    normed = hat * vec_ref[3:4, :] + vec_ref[4:5, :]
    low = normed.astype(BF)
    put_transposed(normed, turned, own_ref, other_ref, True)
    out = after + vec_ref[5:6, :]
    for rz in range(4):
        z = load_e.index(rz)
        load_e.wait(rz)
        hidden = dot_nn(low, we[z]) + eb_ref[z]
        lower = 0.5 * (1.0 + lax.erf(hidden * 0.7071067811865476))
        slope_ref[z] = lower + hidden * (jnp.exp(-0.5 * hidden * hidden) * 0.3989422804014327)
        active = (hidden * lower).astype(BF)
        active_ref[z] = active
        load_s.wait(rz)
        out = out + dot_nt(active, ws[z])
    x_out[...] = out


def mlp(pieces, x, vec, eb, a, e, s, ties=()):
    tokens = x.shape[0]
    outs = [
        ((tokens, 768), F32),
        ((tokens, 768), F32),
        ((4, tokens, 192), BF),
        ((384, tokens), BF),
        ((384, tokens), BF),
        ((4, tokens, 768), BF),
        ((4, tokens, 768), F32),
    ]
    scratch = [
        pltpu.VMEM((4, 768, 256), BF),
        pltpu.VMEM((4, 768, 768), BF),
        pltpu.VMEM((4, 768, 768), BF),
        pltpu.VMEM((768, tokens), F32),
        pltpu.SemaphoreType.DMA((32,)),
        pltpu.SemaphoreType.DMA((32,)),
        pltpu.SemaphoreType.DMA((32,)),
    ]
    return call(
        partial(mlp_kernel, len(a), len(e)), outs, scratch, [SPEC_V] * 7 + [SPEC_A] * (len(a) + 2 * len(e)), (*pieces, x, vec, eb, *a, *e, *s),
        micros=12, name="mlp", ties=ties,
    )


def mlp_back_kernel(n_a, n_e, dy_ref, after_ref, vec_ref, slope_ref, *refs):
    a_refs, e_refs = refs[:n_a], refs[n_a : n_a + n_e]
    s_refs, refs = refs[n_a + n_e : n_a + 2 * n_e], refs[n_a + 2 * n_e :]
    d_out, refs = refs[:4], refs[4:]
    (da_ref, hid_ref, a_own, a_other, sums_ref, ebs_ref, z_own, z_other, wo, we, ws, turned, sa, se, ss) = refs
    load_a = Loader(a_refs, (ORDER_A,), wo, sa, 0, 512, 256)
    load_e = Loader(e_refs, (ORDER_E,), we, se, 96)
    load_s = Loader(s_refs, (ORDER_S,), ws, ss, 192)
    load_s.start()
    load_e.start()
    load_a.start()
    _, y, _, ten = place()
    dy = dy_ref[...].astype(F32)
    dz = dy.astype(BF)
    dz_wide = dz.astype(F32)
    put_transposed(dz_wide, turned, z_own, z_other, True)
    grad = jnp.zeros(dy.shape, F32)
    for rz in range(4):
        z = load_s.index(rz)
        load_s.wait(rz)
        d_active = dot_nn(dz, ws[z])
        d_hidden = (d_active * slope_ref[z]).astype(BF)
        hid_ref[z] = d_hidden
        ebs_ref[z] = jnp.sum(d_hidden.astype(F32), axis=0, keepdims=True)
        load_e.wait(rz)
        grad = grad + dot_nt(d_hidden, we[z])
    hat, rstd = norm_parts(after_ref[...])
    d_after = dy + norm_back(hat, rstd, vec_ref[3:4, :], grad)
    da_ref[...] = d_after
    da = d_after.astype(BF)
    da_wide = da.astype(F32)
    put_transposed(da_wide, turned, a_own, a_other, n_e == 1)
    sums_ref[0:1, :] = jnp.sum(da_wide, axis=0, keepdims=True)
    sums_ref[1:2, :] = jnp.sum(grad * hat, axis=0, keepdims=True)
    sums_ref[2:3, :] = jnp.sum(grad, axis=0, keepdims=True)
    sums_ref[3:4, :] = jnp.sum(dz_wide, axis=0, keepdims=True)
    sums_ref[4:8, :] = jnp.zeros((4, dy.shape[1]), F32)
    for rz in range(4):
        load_a.wait(rz)
    for pair in range(4):
        g = group_of(y, ten, pair)
        d_out[pair][...] = dot_nn(da, wo[g])[:, 64:].astype(BF)


def mlp_back(dy, after, vec, slope, a, e, s, ties=()):
    tokens = dy.shape[0]
    outs = [((tokens, 192), BF)] * 4 + [
        ((tokens, 768), F32),
        ((4, tokens, 768), BF),
        ((384, tokens), BF),
        ((384, tokens), BF),
        ((8, 768), F32),
        ((4, 1, 768), F32),
        ((384, tokens), BF),
        ((384, tokens), BF),
    ]
    scratch = [
        pltpu.VMEM((4, 768, 256), BF),
        pltpu.VMEM((4, 768, 768), BF),
        pltpu.VMEM((4, 768, 768), BF),
        pltpu.VMEM((768, tokens), F32),
        pltpu.SemaphoreType.DMA((32,)),
        pltpu.SemaphoreType.DMA((32,)),
        pltpu.SemaphoreType.DMA((32,)),
    ]
    return call(
        partial(mlp_back_kernel, len(a), len(e)), outs, scratch, [SPEC_V] * 4 + [SPEC_A] * (len(a) + 2 * len(e)),
        (dy, after, vec, slope, *a, *e, *s), micros=11, name="mlp_back", ties=ties,
    )


def attend_back_kernel(count_ref, d0, d1, d2, d3, kv_ref, q_ref, mixed_ref, lse_ref, dq_ref, own_ref, other_ref, do, inner, stat, dkv):
    _, y, c, ten = place()
    tokens = d0.shape[0]
    half = lax.rem(ten, 2)
    inner[...] = jnp.zeros(inner.shape, F32)
    for pair, d in enumerate((d0, d1, d2, d3)):
        rows = pl.ds(pair * tokens, tokens)
        grad = d[...]
        do[rows, :] = grad
        for h in range(3):
            cols = slice(h * HD, (h + 1) * HD)
            inner[rows, h : h + 1] = jnp.sum(grad[:, cols].astype(F32) * mixed_ref[rows, cols], axis=-1, keepdims=True)
    stat[0] = lse_ref[...].T
    stat[1] = inner[...].T
    total, queries = kv_ref.shape[0], q_ref.shape[0]
    count = count_ref[0]
    step = 256
    valid = lax.broadcasted_iota(jnp.int32, (128, step), 0) + (total - 128) < count
    for h in range(3):
        cols = slice(h * HD, (h + 1) * HD)
        keys = kv_ref[:, cols]
        values = kv_ref[:, 192 + h * HD : 192 + (h + 1) * HD]
        turned = keys.astype(F32).T.astype(BF)
        d_keys = jnp.zeros((total, HD), F32)
        d_values = jnp.zeros((total, HD), F32)
        for block in range(queries // step):
            rows = slice(block * step, (block + 1) * step)
            query = q_ref[rows, cols]
            grad = do[rows, cols]
            scores = dot_nt(keys, query)
            last = jnp.where(valid, scores[total - 128 :], -1000000000.0)
            scores = jnp.concatenate([scores[: total - 128], last], axis=0)
            probs = jnp.exp(scores - stat[0, h : h + 1, rows])
            d_probs = dot_nt(values, grad)
            d_scores = (probs * (d_probs - stat[1, h : h + 1, rows])).astype(BF)
            d_values = d_values + dot_nn(probs.astype(BF), grad)
            d_keys = d_keys + dot_nn(d_scores, query)
            d_query = dot_nn(turned, d_scores) * HD ** (-0.5)
            dq_ref[rows, cols] = d_query.T.astype(BF)
        dkv[:, cols] = d_keys.astype(BF)
        dkv[:, 192 + h * HD : 192 + (h + 1) * HD] = d_values.astype(BF)
    for pair in range(4):
        for side, ref in ((0, own_ref), (1, other_ref)):
            block = (xor_bit(y, pair & 2) * 2 + xor_bit(c, side)) * 2 + xor_bit(half, pair & 1)
            ref[pair] = dkv[pl.ds(pl.multiple_of(block * tokens, 64), tokens), :]


def attend_back(count, pieces, kv, q, mixed, lse, ties=()):
    tokens = pieces[0].shape[0]
    outs = [((4 * tokens, 192), BF), ((4, tokens, 384), BF), ((4, tokens, 384), BF)]
    scratch = [
        pltpu.VMEM((4 * tokens, 192), BF),
        pltpu.VMEM((4 * tokens, 128), F32),
        pltpu.VMEM((2, 128, 4 * tokens), F32),
        pltpu.VMEM((8 * tokens, 384), BF),
    ]
    return call(
        attend_back_kernel, outs, scratch, [SPEC_S] + [SPEC_V] * 8, (count, *pieces, kv, q, mixed, lse),
        micros=11, name="attend_back", ties=ties,
    )


def project_back_kernel(n_a, n_high, d0, d1, d2, d3, da_ref, x_ref, vec_ref, two_ref, ebs_ref, *refs):
    high_refs, a_refs, refs = refs[:n_high], refs[n_high : n_high + n_a], refs[n_high + n_a :]
    dx_ref, dqkv_ref, sums_ref, w, sems = refs
    load = Loader(a_refs, (ORDER_A,), w, sems, 0, 0, 640)
    load.start()
    _, y, _, ten = place()
    hat, rstd = norm_parts(x_ref[...].astype(F32))
    sums_ref[2:6, :] = two_ref[0:4, :]
    sums_ref[10:16, :] = jnp.zeros((6, hat.shape[1]), F32)
    for z in range(4):
        sums_ref[6 + z : 7 + z, :] = ebs_ref[z]
    if n_high:
        sums_ref[16:32, :] = high_refs[0][...]
    for rz in range(4):
        load.wait(rz)
    grad = jnp.zeros(hat.shape, F32)
    for pair, d in enumerate((d0, d1, d2, d3)):
        g = group_of(y, ten, pair)
        piece = d[...]
        dqkv_ref[g] = piece
        sums_ref[pl.ds(10 + g, 1), :576] = jnp.sum(piece.astype(F32), axis=0, keepdims=True)
        grad = grad + dot_nt(piece, w[g][:, :576])
    dx_ref[...] = da_ref[...] + norm_back(hat, rstd, vec_ref[0:1, :], grad)
    sums_ref[0:1, :] = jnp.sum(grad * hat, axis=0, keepdims=True)
    sums_ref[1:2, :] = jnp.sum(grad, axis=0, keepdims=True)


def project_back(pieces, da, x, vec, two, ebs, high, a, ties=()):
    tokens = x.shape[0]
    outs = [((tokens, 768), F32), ((4, tokens, 576), BF), ((16 + 16 * len(high), 768), F32)]
    scratch = [pltpu.VMEM((4, 768, 640), BF), pltpu.SemaphoreType.DMA((32,))]
    return call(
        partial(project_back_kernel, len(a), len(high)),
        outs,
        scratch,
        [SPEC_V] * (9 + len(high)) + [SPEC_A] * len(a),
        (*pieces, da, x, vec, two, ebs, *high, *a),
        micros=4,
        name="project_back",
        ties=ties,
    )


def emit(value, rz, orders, outs):
    rows = 96 // len(orders)
    for xy in range(4):
        for n, order in enumerate(orders):
            part, at = part_of((16 if xy & 2 else 0) | (8 if xy & 1 else 0) | rz, order)
            outs[n * 5 + part][at] = value[xy * 96 + n * rows : xy * 96 + (n + 1) * rows].astype(BF)


def weigh_high_kernel(row, both, n_in, *refs):
    left, right = refs[: n_in // 2], refs[n_in // 2 : n_in]
    out_ref, part, sem = refs[-3:]
    for z in range(4):
        first = dot_nn(left[0][...], right[0][z]) + dot_nn(left[1][...], right[1][z])
        second = dot_nn(left[2][...], right[2][z]) + dot_nn(left[3][...], right[3][z])
        for at, xy in enumerate(RING):
            rows = slice(xy * 96, (xy + 1) * 96)
            if both:
                part[at * 4 + z, 0:96] = first[rows].astype(BF)
                part[at * 4 + z, 96:192] = second[rows].astype(BF)
            else:
                part[at * 4 + z] = jnp.concatenate([first[rows], second[rows]], axis=1).astype(BF)
    copy = pltpu.make_async_copy(part, out_ref.at[:, pl.ds(row, part.shape[1])], sem)
    copy.start()
    copy.wait()


def weigh_high(args, rows, row, both, into=None):
    more = [] if into is None else [into]
    return pl.pallas_call(
        partial(weigh_high_kernel, row, both, len(args)),
        out_shape=jax.ShapeDtypeStruct((16, rows, 768), BF),
        in_specs=[SPEC_V] * len(args) + [SPEC_A] * len(more),
        out_specs=SPEC_A,
        scratch_shapes=[pltpu.VMEM((16, 192 if both else 96, 768), BF), pltpu.SemaphoreType.DMA],
        input_output_aliases={len(args): 0} if more else {},
        compiler_params=pltpu.CompilerParams(vmem_limit_bytes=LIMIT * 1024 * 1024),
        cost_estimate=pl.CostEstimate(flops=int(5 * COST), bytes_accessed=1000, transcendentals=0),
        name="weigh_both" if both else "weigh_attention_high",
    )(*args, *more)


def sum_plane(chunks, mesh_shape):
    dp_size, seq_size, ten_size = mesh_shape
    groups = [
        [((h + (xy >> 1)) * seq_size + 2 * (xy & 1) + c) * ten_size + t for xy in RING]
        for h in range(0, dp_size, 2)
        for c in range(2)
        for t in range(ten_size)
    ]
    rows = chunks.shape[1]
    return lax.psum_scatter(
        chunks.reshape(16 * rows, 768), AXES, scatter_dimension=0, axis_index_groups=groups, tiled=True
    )


def sum_line(chunks):
    return lax.psum_scatter(chunks, "tensor", scatter_dimension=0, tiled=True).astype(F32)


def weigh_attention_kernel(orders, n_own, n_got, a_own, a_got, q_own, q_got, m_own, m_got, *outs):
    _, _, _, ten = place()
    for rz in range(4):
        z = xor_two(ten, rz)
        qkv = dot_nn(n_own[...], q_own[z]) + dot_nn(n_got[...], q_got[z])
        out = dot_nn(a_own[...], m_own[z]) + dot_nn(a_got[...], m_got[z])
        emit(jnp.concatenate([qkv, out], axis=1), rz, orders, outs)


def weigh_attention(orders, args, ties=()):
    outs = [((n, 96 // len(orders), 768), BF) for _ in orders for n in (8, 4, 2, 1, 1)]
    return call(
        partial(weigh_attention_kernel, orders), outs, [], [SPEC_V] * 8, args,
        micros=3, name="weigh_attention", ties=ties,
    )


def spread_kernel(*refs):
    ten = lax.axis_index("tensor")
    for n in range(2):
        for at, rz in enumerate((0, 2, 1, 3)):
            refs[8 + n][xor_two(ten, rz)] = refs[n * 4 + at][...].astype(refs[8 + n].dtype)


def spread(left, left_type, right, right_type):
    tokens, width = left[0].shape
    outs = [((4, tokens, width), left_type), ((4, tokens, width), right_type)]
    done = call(spread_kernel, outs, [], [SPEC_V] * 8, (*left, *right), name="spread")
    return [d.reshape(2, 1, 2 * tokens, width) for d in done]


def small_params(every):
    vec = every[:, 0, :, :6].transpose(1, 2, 0, 3).reshape(LAYERS, 6, 768)
    eb = every[:, :, :, 6].transpose(2, 1, 0, 3).reshape(LAYERS, 4, 1, 768)
    qv = every[:, :, :, 7, :48].reshape(8, 4, LAYERS, 2, 24).transpose(2, 3, 1, 0, 4).reshape(LAYERS, 2, 4, 192)
    qvb = jnp.concatenate([jnp.zeros_like(qv[:, 0]), qv[:, 1], qv[:, 0]], axis=-1)[:, :, None, :]
    return jnp.pad(vec, ((0, 0), (0, 2), (0, 0))), qvb, eb


def small_everywhere(chunks, order):
    x, y, c, ten = place()
    me = ((x * 2 + y) * 2 + c) * 4 + ten
    rels = []
    for a in range(4):
        for j in range(8):
            rel = sum(BITS[order[k]] for k in range(3) if j & (1 << k))
            rels.append(rel | (BITS[order[3]] if a & 1 else 0) | (BITS["c"] if a & 2 else 0))
    device = jnp.bitwise_xor(jnp.asarray(rels, jnp.int32), me)
    pick = (jnp.arange(32, dtype=jnp.int32)[:, None] == device[None, :]).astype(BF)
    rows = jnp.concatenate([chunk[:, 96:98].reshape(8, -1) for chunk in chunks], axis=0)
    every = jnp.dot(pick, rows, preferred_element_type=F32)
    return every.reshape(8, 4, LAYERS, 8, 96)


def body(shape, features, upstream, key_mask, vectors, proj_qkv, qv_bias, proj_out, expand_weight, expand_bias, shrink_weight):
    dp_size, seq_size, ten_size = shape
    dp, seq, ten = lax.axis_index("dp"), lax.axis_index("seq"), lax.axis_index("tensor")
    tokens = features.shape[2] // 2
    at = (lax.div(ten, 2), 0, lax.rem(ten, 2) * tokens, 0)
    x0 = lax.dynamic_slice(features, at, (1, 1, tokens, 768)).reshape(tokens, 768)
    dy0 = lax.dynamic_slice(upstream, at, (1, 1, tokens, 768)).reshape(tokens, 768)
    count = jnp.sum(lax.dynamic_slice(key_mask, (lax.div(ten, 2), 0, 0), (1, 1, key_mask.shape[2])), axis=(1, 2))

    width = proj_qkv.shape[1]
    wa = jnp.concatenate(
        [
            proj_qkv[:, :, 1],
            proj_qkv[:, :, 2],
            proj_qkv[:, :, 0],
            proj_out.transpose(0, 2, 1),
        ],
        axis=-1,
    )
    we = expand_weight
    ws = shrink_weight.transpose(0, 2, 1)
    if dp_size != 2:
        start = (lax.rem(dp, 2) * 4 + seq) * 96
        wa, we, ws = (
            lax.dynamic_slice_in_dim(lax.all_gather(w, ("dp", "seq"), axis=1, tiled=True), start, 96, axis=1)
            for w in (wa, we, ws)
        )
    if dp_size == 2:
        small = jnp.concatenate(
            [
                vectors.reshape(LAYERS, -1),
                expand_bias,
                qv_bias.reshape(LAYERS, -1),
                jnp.zeros((LAYERS, 48), BF),
            ],
            axis=1,
        )
    else:
        small = jnp.zeros((LAYERS, 768), BF)
    first = jnp.concatenate([wa[0], small, jnp.zeros((6, 768), BF)], axis=0)
    whole = [
        [(d * seq_size + s) * ten_size + t for d in range(h, h + 2) for s in range(seq_size) for t in range(ten_size)]
        for h in range(0, dp_size, 2)
    ]
    low_layer = Gatherer((first, we[0], ws[0]), (ORDER_A, ORDER_E, ORDER_S), shape)
    for _ in range(3):
        low_layer.go()
    (block,) = low_layer.before(jnp.concatenate([wa[1], we[1], ws[1]], axis=0))
    high = lax.all_gather(block, AXES, axis_index_groups=None if dp_size == 2 else whole)
    low_layer.go()
    a_w, e_w, s_w = ((w, [high]) for w in low_layer.core())
    if dp_size == 2:
        vec, qvb, eb = small_params(small_everywhere(a_w[0], ORDER_A))
    else:
        vec = lax.all_gather(vectors, ("dp", "seq"), axis=2, tiled=True).reshape(LAYERS, 6, 8, 96)
        eb = lax.all_gather(expand_bias, ("tensor", "dp", "seq"), axis=1, tiled=True).reshape(LAYERS, 1, 4, 8, 96)
        qv = lax.all_gather(qv_bias, ("tensor", "dp", "seq"), axis=2, tiled=True).reshape(LAYERS, 2, 4, 8, 24)
        vec = jnp.broadcast_to(vec[:, :, None], (LAYERS, 6, 4, 8, 96))
        qv = jnp.pad(qv.transpose(0, 2, 3, 1, 4).reshape(LAYERS, 1, 4, 8, 48), ((0, 0),) * 4 + ((0, 48),))
        vec, qvb, eb = small_params(jnp.concatenate([vec, eb, qv], axis=1).transpose(3, 2, 0, 1, 4).astype(F32))

    state = x0
    kept = []
    for d in range(LAYERS):
        *pieces, n_own, n_other = project(state, vec[d], qvb[d], a_w[d], tokens)
        pieces = [pieces[0]] + [swap_group(pieces[p], p, shape) for p in (1, 2, 3)]
        others = [swap(p[:, :384], "c", shape) for p in pieces]
        *mixed, kv, q, mixed_wide, lse = attend(count, pieces, others)
        mixed = [mixed[0]] + [swap_group(mixed[p], p, shape) for p in (1, 2, 3)]
        x_in = state
        state, after, mixed_all, m_own, m_other, active, slope = mlp(mixed, x_in, vec[d], eb[d], a_w[d], e_w[d], s_w[d])
        kept.append((x_in, n_own, n_other, kv, q, mixed_wide, lse, after, mixed_all, m_own, m_other, active, slope))
    encoded = [state.astype(BF)]

    grad = dy0
    for d in (1, 0):
        x_in, n_own, n_other, kv, q, mixed_wide, lse, after, mixed_all, m_own, m_other, active, slope = kept[d]
        d0, d1, d2, d3, d_after, d_hid, da_own, da_other, sums_two, ebs, z_own, z_other = mlp_back(
            grad, after, vec[d], slope, a_w[d], e_w[d], s_w[d]
        )
        d_mixed = [d0] + [swap_group(v, p + 1, shape) for p, v in enumerate((d1, d2, d3))]
        m_got, hid_got, z_got, active_got = (swap(v, "c", shape) for v in (m_other, d_hid, z_other, active))
        given = (m_own, m_got, z_own, z_got, d_hid, hid_got, active, active_got)
        if d:
            chunks = weigh_high(given, 192, 0, True)
            high_sum = sum_plane(chunks, shape)
            encoded[0], *d_mixed = fence(encoded[0], *d_mixed)
            encoded.append(swap(encoded[0], "z2", shape))
        else:
            chunks = weigh_high(given, 288, 0, True, chunks)
            low_sum = sum_line(sum_plane(chunks, shape))
            encoded[1], *d_mixed = fence(encoded[1], *d_mixed)
            encoded.append(swap(encoded[1], "z1", shape))
        dq, own, other = attend_back(count, d_mixed, kv, q, mixed_wide, lse, [chunks])
        if d:
            *encoded, other = fence(*encoded, other)
        else:
            *encoded, high_sum, other = fence(*encoded, high_sum, other)
        d_kv = (own.astype(F32) + swap(other, "c", shape).astype(F32)).astype(BF)
        back = [jnp.concatenate([d_kv[p], dq[p * tokens : (p + 1) * tokens]], axis=1) for p in range(4)]
        back = [back[0]] + [swap_group(back[p], p, shape) for p in (1, 2, 3)]
        if d:
            encoded[0], *back = fence(encoded[0], *back)
            got_z = swap(encoded[0], "z1", shape)
        grad, d_qkv, total = project_back(back, d_after, x_in, vec[d], sums_two, ebs, [] if d else [high_total], a_w[d])
        given = (
            n_own,
            swap(n_other, "c", shape),
            da_own,
            swap(da_other, "c", shape),
            d_qkv,
            swap(d_qkv, "c", shape),
            mixed_all,
            swap(mixed_all, "c", shape),
        )
        if d:
            high_total = total
            chunks = weigh_high(given, 288, 192, False)
            chunks, got_z, high_sum, grad = fence(chunks, got_z, high_sum, grad)
            high_sum = sum_line(high_sum)
            encoded.append(got_z)
    if dp_size == 2:
        total = total + swap(total, "c", shape)
    else:
        total = lax.psum(total, AXES)
    parts = weigh_attention(SUM_A, given)
    sums_a = [Reducer(parts[n * 5 : n * 5 + 5], order, shape) for n, order in enumerate(SUM_A)]
    features_grad = [grad.astype(BF)]
    last = Together(sums_a)
    total, features_grad[0] = last.wait(total, features_grad[0])
    for step, bit in enumerate(("x", "y", "z1", "z2")):
        got = [swap(total, bit, shape)] if dp_size == 2 else []
        if step == 0:
            got.append(swap(features_grad[0], "z2", shape))
        elif step == 1:
            got += [swap(v, "z1", shape) for v in features_grad]
        got = list(last.go(*got))
        if dp_size == 2:
            total = total + got.pop(0)
        features_grad += got
    small = total.reshape(LAYERS, 16, 768)
    encoded, grad_features = spread(encoded, BF, features_grad, F32)
    g_a = [jnp.concatenate([r.finish() for r in sums_a], axis=0), low_sum[192:]]
    g_e, g_s = ([low_sum[:96], high_sum[:96]], [low_sum[96:192], high_sum[96:]])

    if dp_size != 2:
        start = (lax.rem(dp, 2) * 4 + seq) * 96

        def down(block):
            whole = lax.dynamic_update_slice_in_dim(jnp.zeros((768, 768), F32), block, start, axis=0)
            return lax.psum_scatter(whole, ("dp", "seq"), scatter_dimension=0, tiled=True)

        g_a, g_e, g_s = ([down(g) for g in gs] for gs in (g_a, g_e, g_s))
    ga, ge, gs = jnp.stack(g_a), jnp.stack(g_e), jnp.stack(g_s)
    g_small = small
    mine = dp * seq_size + seq
    grad_vectors = lax.dynamic_slice_in_dim(g_small[:, :6], mine * width, width, axis=2)
    eb_width, qv_width = expand_bias.shape[1], qv_bias.shape[2]
    grad_eb = lax.dynamic_slice_in_dim(
        lax.dynamic_index_in_dim(g_small[:, 6:10], ten, axis=1, keepdims=False), mine * eb_width, eb_width, axis=1
    )
    qv = lax.dynamic_index_in_dim(g_small[:, 10:14], ten, axis=1, keepdims=False)
    grad_qv = jnp.stack(
        [
            lax.dynamic_slice_in_dim(qv[:, 384:576], mine * qv_width, qv_width, axis=1),
            lax.dynamic_slice_in_dim(qv[:, 192:384], mine * qv_width, qv_width, axis=1),
        ],
        axis=1,
    )
    grad_qkv = jnp.stack([ga[:, :, 384:576], ga[:, :, :192], ga[:, :, 192:384]], axis=2)
    return (
        encoded,
        grad_features,
        grad_vectors,
        grad_qkv,
        grad_qv,
        ga[:, :, 576:].transpose(0, 2, 1),
        ge,
        grad_eb,
        gs.transpose(0, 2, 1),
    )


def solution(mesh):
    placed = (
        P(None, "dp", "seq", None),
        P(None, "dp", "seq", None),
        P(None, "dp", None),
        P(None, None, ("dp", "seq")),
        P(None, ("dp", "seq"), None, "tensor"),
        P(None, None, ("tensor", "dp", "seq")),
        P(None, "tensor", ("dp", "seq")),
        P(None, ("dp", "seq"), "tensor"),
        P(None, ("tensor", "dp", "seq")),
        P(None, "tensor", ("dp", "seq")),
    )
    shape = tuple(mesh.shape[axis] for axis in AXES)
    return jax.shard_map(
        partial(body, shape),
        mesh=mesh,
        in_specs=placed,
        out_specs=(
            P(None, "dp", "seq", None),
            P(None, "dp", "seq", None),
            P(None, None, ("dp", "seq")),
            P(None, ("dp", "seq"), None, "tensor"),
            P(None, None, ("tensor", "dp", "seq")),
            P(None, "tensor", ("dp", "seq")),
            P(None, ("dp", "seq"), "tensor"),
            P(None, ("tensor", "dp", "seq")),
            P(None, "tensor", ("dp", "seq")),
        ),
        check_vma=False,
    )
```

```python
from functools import partial

import jax
import jax.numpy as jnp
from jax import lax
from jax.experimental import pallas as pl
from jax.experimental.pallas import tpu as pltpu
from jax.sharding import PartitionSpec as P

HD = 64
LAYERS = 2
AXES = ("dp", "seq", "tensor")
BF = jnp.bfloat16
F32 = jnp.float32
LIMIT = 48
COST = 3.0e8

BITS = {"x": 16, "y": 8, "c": 4, "z2": 2, "z1": 1}

ORDER_E = ("z2", "z1", "x", "y")
ORDER_S = ("z2", "y", "z1", "x")
ORDER_A = ("z2", "x", "y", "z1")
SUM_A = (("x", "y", "z1", "z2"), ("y", "x", "z1", "z2"))
RING = (0, 1, 3, 2)


SPEC_V = pl.BlockSpec(memory_space=pltpu.VMEM)
SPEC_S = pl.BlockSpec(memory_space=pltpu.SMEM)
SPEC_A = pl.BlockSpec(memory_space=pl.ANY)


def swap(value, bit, mesh_shape):
    dp_size, seq_size, ten_size = mesh_shape
    pairs = []
    for d in range(dp_size):
        for s in range(seq_size):
            for t in range(ten_size):
                e, u, v = d, s, t
                if bit == "x":
                    e = d ^ 1
                elif bit == "y":
                    u = s ^ 2
                elif bit == "c":
                    u = s ^ 1
                elif bit == "z2":
                    v = t ^ 2
                else:
                    v = t ^ 1
                pairs.append(((d * seq_size + s) * ten_size + t, (e * seq_size + u) * ten_size + v))
    return lax.ppermute(value, AXES, pairs)


def swap_group(value, pair, mesh_shape):
    dp_size, seq_size, ten_size = mesh_shape
    ry, rp = pair >> 1, pair & 1
    pairs = []
    for d in range(dp_size):
        for s in range(seq_size):
            for t in range(ten_size):
                to = (d * seq_size + (s ^ (2 * ry))) * ten_size + (t ^ rp)
                pairs.append(((d * seq_size + s) * ten_size + t, to))
    return lax.ppermute(value, AXES, pairs)


def fence(*values):
    return lax.optimization_barrier(values)


class Gatherer:
    def __init__(self, blocks, orders, mesh_shape):
        self.cur, self.orders, self.mesh_shape, self.step = [b[None] for b in blocks], orders, mesh_shape, 0

    def go(self):
        got = [swap(c, o[self.step], self.mesh_shape) for c, o in zip(self.cur, self.orders)]
        self.step += 1
        if self.step < 4:
            self.cur = list(fence(*(jnp.concatenate([c, g], axis=0) for c, g in zip(self.cur, got))))
        else:
            self.more = list(fence(*got))

    def wait(self, *values):
        count = len(self.cur)
        out = fence(*self.cur, *values)
        self.cur = list(out[:count])
        return out[count:]

    def before(self, *values):
        now = self.more if self.step == 4 else self.cur
        count = len(now)
        out = fence(*now, *values)
        if self.step == 4:
            self.more = list(out[:count])
        else:
            self.cur = list(out[:count])
        return out[count:]

    def core(self):
        turned = [[swap(v, "c", self.mesh_shape) for v in pair] for pair in zip(self.cur, self.more)]
        return [[c, m, *t] for c, m, t in zip(self.cur, self.more, turned)]


class Reducer:
    def __init__(self, parts, order, mesh_shape):
        self.parts, self.order, self.mesh_shape, self.step = list(parts), order, mesh_shape, 0

    def send(self):
        return swap(self.parts[self.step].astype(BF), self.order[self.step], self.mesh_shape)

    def take(self, got):
        step = self.step
        for later in range(step + 1, 5):
            size = 8 >> later if later < 4 else 1
            start = size if later < 4 else 0
            self.parts[later] = self.parts[later].astype(F32) + got[start : start + size].astype(F32)
        self.step += 1

    def finish(self):
        return self.parts[4][0]


class Together:
    def __init__(self, sums):
        self.sums = sums

    def wait(self, *values):
        out = list(fence(*(r.parts[r.step] for r in self.sums), *values))
        for r in self.sums:
            r.parts[r.step] = out.pop(0)
        return out

    def go(self, *others):
        got = [r.send() for r in self.sums]
        out = fence(*got, *others)
        for r, g in zip(self.sums, out):
            r.take(g)
        return out[len(got) :]


def part_of(rel, order):
    flags = [1 if rel & BITS[b] else 0 for b in order]
    for step in range(4):
        if flags[step]:
            place = 0
            for f in flags[step + 1 :]:
                place = place * 2 + f
            return step, place
    return 4, 0


def place():
    dp, seq, ten = lax.axis_index("dp"), lax.axis_index("seq"), lax.axis_index("tensor")
    return lax.rem(dp, 2), lax.div(seq, 2), lax.rem(seq, 2), ten


def xor_bit(value, flag):
    return 1 - value if flag else value


def xor_two(value, flags):
    if flags == 0:
        return value
    high, low = lax.div(value, 2), lax.rem(value, 2)
    return xor_bit(high, flags & 2) * 2 + xor_bit(low, flags & 1)


def row_block(x, y, c, rel):
    return (xor_bit(x, rel & 16) * 2 + xor_bit(y, rel & 8)) * 2 + xor_bit(c, rel & 4)


def group_of(y, ten, pair):
    return xor_bit(y, pair & 2) * 2 + xor_bit(lax.rem(ten, 2), pair & 1)


class Loader:
    def __init__(self, refs, orders, scratch, sems, row=0, col=0, width=768):
        x, y, c, ten = place()
        self.copies = {k: [] for k in range(4)}
        self.ten = None if len(refs) == 1 else ten
        if len(refs) == 1:
            for n in range(32):
                block, key = divmod(n, 4)
                dst = scratch.at[key, pl.ds(block * 96, 96)]
                src = refs[0].at[n, pl.ds(row, 96), pl.ds(col, width)]
                self.copies[key].append(pltpu.make_async_copy(src, dst, sems.at[n]))
            return
        rows = 96 * 4 // len(refs)
        for n in range(8 * len(refs)):
            a, j = divmod(n, 8)
            order = orders[a // 4]
            rel = sum(BITS[order[k]] for k in range(3) if j & (1 << k))
            rel |= BITS[order[3]] if a & 1 else 0
            rel |= BITS["c"] if a & 2 else 0
            to = pl.multiple_of(row_block(x, y, c, rel) * 96 + a // 4 * rows, 32)
            dst = scratch.at[xor_two(ten, rel & 3), pl.ds(to, rows)]
            src = refs[a].at[j, pl.ds(0, rows), pl.ds(col, width)]
            self.copies[rel & 3].append(pltpu.make_async_copy(src, dst, sems.at[n]))

    def start(self):
        for k in range(4):
            for copy in self.copies[k]:
                copy.start()

    def wait(self, k):
        for copy in self.copies[k]:
            copy.wait()

    def index(self, k):
        return k if self.ten is None else xor_two(self.ten, k)


def dot_nn(left, right):
    return jnp.dot(left, right, preferred_element_type=F32)


def dot_nt(left, right):
    return lax.dot_general(left, right, (((1,), (1,)), ((), ())), preferred_element_type=F32)


def norm_parts(value):
    center = value - jnp.mean(value, axis=-1, keepdims=True)
    spread = jnp.mean(center * center, axis=-1, keepdims=True)
    rstd = lax.rsqrt(spread + 1e-05)
    return center * rstd, rstd


def norm_back(hat, rstd, gain, grad):
    scaled = grad * gain
    first = jnp.mean(scaled, axis=-1, keepdims=True)
    second = jnp.mean(scaled * hat, axis=-1, keepdims=True)
    return rstd * (scaled - first - hat * second)


def put_transposed(value, turned, own_ref, other_ref, absolute=False):
    x, y, c, _ = place()
    turned[...] = value.T
    for xy in range(4):
        for side, ref in ((0, own_ref), (4, other_ref)):
            if absolute:
                row = (2 * xy + xor_bit(c, side)) * 96
            else:
                row = row_block(x, y, c, (16 if xy & 2 else 0) | (8 if xy & 1 else 0) | side) * 96
            ref[pl.ds(xy * 96, 96), :] = turned[pl.ds(pl.multiple_of(row, 32), 96), :].astype(BF)


def call(kernel, outs, scratch, specs, args, micros=1, name=None, ties=(), limit=LIMIT):
    return pl.pallas_call(
        lambda *refs: kernel(*refs[len(ties) :]),
        out_shape=[jax.ShapeDtypeStruct(s, d) for s, d in outs],
        in_specs=[SPEC_A] * len(ties) + list(specs),
        out_specs=[SPEC_V] * len(outs),
        scratch_shapes=scratch,
        compiler_params=pltpu.CompilerParams(vmem_limit_bytes=limit * 1024 * 1024),
        cost_estimate=pl.CostEstimate(flops=int(micros * COST), bytes_accessed=1000, transcendentals=0),
        name=name,
    )(*ties, *args)


def project_kernel(n_a, x_ref, vec_ref, bias_ref, *refs):
    a_refs, refs = refs[:n_a], refs[n_a:]
    outs, (own_ref, other_ref, w, turned, sems) = refs[:4], refs[4:]
    load = Loader(a_refs, (ORDER_A,), w, sems, 0, 0, 640)
    load.start()
    _, y, _, ten = place()
    hat, _ = norm_parts(x_ref[...].astype(F32))
    normed = hat * vec_ref[0:1, :] + vec_ref[1:2, :]
    low = normed.astype(BF)
    put_transposed(normed, turned, own_ref, other_ref)
    for rz in range(4):
        load.wait(rz)
    for pair in range(4):
        g = group_of(y, ten, pair)
        packed = dot_nn(low, w[g])[:, :576] + bias_ref[g]
        outs[pair][...] = packed.astype(BF)


def project(x, vec, bias, a, tokens, ties=()):
    outs = [((tokens, 576), BF)] * 4 + [((384, tokens), BF)] * 2
    scratch = [pltpu.VMEM((4, 768, 640), BF), pltpu.VMEM((768, tokens), F32), pltpu.SemaphoreType.DMA((32,))]
    return call(
        partial(project_kernel, len(a)), outs, scratch, [SPEC_V] * 3 + [SPEC_A] * len(a), (x, vec, bias, *a),
        micros=4, name="project", ties=ties,
    )


def attend_kernel(count_ref, p0, p1, p2, p3, o0, o1, o2, o3, m0, m1, m2, m3, kv_ref, q_ref, mixed_ref):
    _, y, c, ten = place()
    tokens = p0.shape[0]
    half = lax.rem(ten, 2)
    for pair, (p, o) in enumerate(((p0, o0), (p1, o1), (p2, o2), (p3, o3))):
        for side, ref in ((0, p), (1, o)):
            block = (xor_bit(y, pair & 2) * 2 + xor_bit(c, side)) * 2 + xor_bit(half, pair & 1)
            kv_ref[pl.ds(pl.multiple_of(block * tokens, 64), tokens), :] = ref[:, :384]
        q_ref[pl.ds(pair * tokens, tokens), :] = p[:, 384:576] * jnp.asarray(HD ** (-0.5), BF)
    total = kv_ref.shape[0]
    count = count_ref[0]
    ones = jnp.ones((total, HD), BF)
    valid = lax.broadcasted_iota(jnp.int32, (tokens, 128), 1) + (total - 128) < count
    mixed_ref[:, 192:256] = jnp.zeros((4 * tokens, 64), F32)
    for h in range(3):
        keys = kv_ref[:, h * HD : (h + 1) * HD]
        values = jnp.concatenate([kv_ref[:, 192 + h * HD : 192 + (h + 1) * HD], ones], axis=1)
        for pair, m in enumerate((m0, m1, m2, m3)):
            rows = pl.ds(pair * tokens, tokens)
            scores = dot_nt(q_ref[rows, h * HD : (h + 1) * HD], keys)
            last = jnp.where(valid, scores[:, total - 128 :], -1000000000.0)
            scores = jnp.concatenate([scores[:, : total - 128], last], axis=1)
            highest = jnp.max(scores, axis=-1, keepdims=True)
            expo = jnp.exp(scores - highest).astype(BF)
            both = dot_nn(expo, values)
            weight = both[:, HD : HD + 1]
            mixed = both[:, :HD] / weight
            mixed_ref[rows, h * HD : (h + 1) * HD] = mixed
            m[:, h * HD : (h + 1) * HD] = mixed.astype(BF)
            mixed_ref[rows, 192 + h : 193 + h] = highest + jnp.log(weight)


def attend(count, pieces, others, ties=()):
    tokens = pieces[0].shape[0]
    outs = [((tokens, 192), BF)] * 4 + [
        ((8 * tokens, 384), BF),
        ((4 * tokens, 192), BF),
        ((4 * tokens, 256), F32),
    ]
    return call(
        attend_kernel, outs, [], [SPEC_S] + [SPEC_V] * 8, (count, *pieces, *others),
        micros=7, name="attend", ties=ties,
    )


def mlp_kernel(n_a, n_e, m0, m1, m2, m3, x_ref, vec_ref, eb_ref, *refs):
    a_refs, e_refs = refs[:n_a], refs[n_a : n_a + n_e]
    s_refs, refs = refs[n_a + n_e : n_a + 2 * n_e], refs[n_a + 2 * n_e :]
    (x_out, after_ref, mixed_ref, own_ref, other_ref, active_ref, slope_ref, wo, we, ws, turned, sa, se, ss) = refs
    load_a = Loader(a_refs, (ORDER_A,), wo, sa, 0, 512, 256)
    load_e = Loader(e_refs, (ORDER_E,), we, se, 96)
    load_s = Loader(s_refs, (ORDER_S,), ws, ss, 192)
    load_a.start()
    load_e.start()
    load_s.start()
    _, y, _, ten = place()
    for rz in range(4):
        load_a.wait(rz)
    after = x_ref[...].astype(F32) + vec_ref[2:3, :]
    for pair, m in enumerate((m0, m1, m2, m3)):
        g = group_of(y, ten, pair)
        piece = m[...]
        mixed_ref[g] = piece
        after = after + dot_nt(piece, wo[g][:, 64:])
    after_ref[...] = after
    hat, _ = norm_parts(after)
    normed = hat * vec_ref[3:4, :] + vec_ref[4:5, :]
    low = normed.astype(BF)
    put_transposed(normed, turned, own_ref, other_ref, True)
    out = after + vec_ref[5:6, :]
    for rz in range(4):
        z = load_e.index(rz)
        load_e.wait(rz)
        hidden = dot_nn(low, we[z]) + eb_ref[z]
        lower = 0.5 * (1.0 + lax.erf(hidden * 0.7071067811865476))
        slope_ref[z] = lower + hidden * (jnp.exp(-0.5 * hidden * hidden) * 0.3989422804014327)
        active = (hidden * lower).astype(BF)
        active_ref[z] = active
        load_s.wait(rz)
        out = out + dot_nt(active, ws[z])
    x_out[...] = out


def mlp(pieces, x, vec, eb, a, e, s, ties=()):
    tokens = x.shape[0]
    outs = [
        ((tokens, 768), F32),
        ((tokens, 768), F32),
        ((4, tokens, 192), BF),
        ((384, tokens), BF),
        ((384, tokens), BF),
        ((4, tokens, 768), BF),
        ((4, tokens, 768), F32),
    ]
    scratch = [
        pltpu.VMEM((4, 768, 256), BF),
        pltpu.VMEM((4, 768, 768), BF),
        pltpu.VMEM((4, 768, 768), BF),
        pltpu.VMEM((768, tokens), F32),
        pltpu.SemaphoreType.DMA((32,)),
        pltpu.SemaphoreType.DMA((32,)),
        pltpu.SemaphoreType.DMA((32,)),
    ]
    return call(
        partial(mlp_kernel, len(a), len(e)), outs, scratch, [SPEC_V] * 7 + [SPEC_A] * (len(a) + 2 * len(e)), (*pieces, x, vec, eb, *a, *e, *s),
        micros=12, name="mlp", ties=ties,
    )


def mlp_back_kernel(n_a, n_e, dy_ref, after_ref, vec_ref, slope_ref, *refs):
    a_refs, e_refs = refs[:n_a], refs[n_a : n_a + n_e]
    s_refs, refs = refs[n_a + n_e : n_a + 2 * n_e], refs[n_a + 2 * n_e :]
    d_out, refs = refs[:4], refs[4:]
    (da_ref, hid_ref, a_own, a_other, sums_ref, ebs_ref, z_own, z_other, wo, we, ws, turned, sa, se, ss) = refs
    load_a = Loader(a_refs, (ORDER_A,), wo, sa, 0, 512, 256)
    load_e = Loader(e_refs, (ORDER_E,), we, se, 96)
    load_s = Loader(s_refs, (ORDER_S,), ws, ss, 192)
    load_s.start()
    load_e.start()
    load_a.start()
    _, y, _, ten = place()
    dy = dy_ref[...].astype(F32)
    dz = dy.astype(BF)
    dz_wide = dz.astype(F32)
    put_transposed(dz_wide, turned, z_own, z_other, True)
    grad = jnp.zeros(dy.shape, F32)
    for rz in range(4):
        z = load_s.index(rz)
        load_s.wait(rz)
        d_active = dot_nn(dz, ws[z])
        d_hidden = (d_active * slope_ref[z]).astype(BF)
        hid_ref[z] = d_hidden
        ebs_ref[z] = jnp.sum(d_hidden.astype(F32), axis=0, keepdims=True)
        load_e.wait(rz)
        grad = grad + dot_nt(d_hidden, we[z])
    hat, rstd = norm_parts(after_ref[...])
    d_after = dy + norm_back(hat, rstd, vec_ref[3:4, :], grad)
    da_ref[...] = d_after
    da = d_after.astype(BF)
    da_wide = da.astype(F32)
    put_transposed(da_wide, turned, a_own, a_other)
    sums_ref[0:1, :] = jnp.sum(da_wide, axis=0, keepdims=True)
    sums_ref[1:2, :] = jnp.sum(grad * hat, axis=0, keepdims=True)
    sums_ref[2:3, :] = jnp.sum(grad, axis=0, keepdims=True)
    sums_ref[3:4, :] = jnp.sum(dz_wide, axis=0, keepdims=True)
    sums_ref[4:8, :] = jnp.zeros((4, dy.shape[1]), F32)
    for rz in range(4):
        load_a.wait(rz)
    for pair in range(4):
        g = group_of(y, ten, pair)
        d_out[pair][...] = dot_nn(da, wo[g])[:, 64:].astype(BF)


def mlp_back(dy, after, vec, slope, a, e, s, ties=()):
    tokens = dy.shape[0]
    outs = [((tokens, 192), BF)] * 4 + [
        ((tokens, 768), F32),
        ((4, tokens, 768), BF),
        ((384, tokens), BF),
        ((384, tokens), BF),
        ((8, 768), F32),
        ((4, 1, 768), F32),
        ((384, tokens), BF),
        ((384, tokens), BF),
    ]
    scratch = [
        pltpu.VMEM((4, 768, 256), BF),
        pltpu.VMEM((4, 768, 768), BF),
        pltpu.VMEM((4, 768, 768), BF),
        pltpu.VMEM((768, tokens), F32),
        pltpu.SemaphoreType.DMA((32,)),
        pltpu.SemaphoreType.DMA((32,)),
        pltpu.SemaphoreType.DMA((32,)),
    ]
    return call(
        partial(mlp_back_kernel, len(a), len(e)), outs, scratch, [SPEC_V] * 4 + [SPEC_A] * (len(a) + 2 * len(e)),
        (dy, after, vec, slope, *a, *e, *s), micros=11, name="mlp_back", ties=ties,
    )


def attend_back_kernel(count_ref, d0, d1, d2, d3, kv_ref, q_ref, mixed_ref, dq_ref, own_ref, other_ref, do, inner, stat, dkv):
    _, y, c, ten = place()
    tokens = d0.shape[0]
    half = lax.rem(ten, 2)
    inner[...] = jnp.zeros(inner.shape, F32)
    for pair, d in enumerate((d0, d1, d2, d3)):
        rows = pl.ds(pair * tokens, tokens)
        grad = d[...]
        do[rows, :] = grad
        for h in range(3):
            cols = slice(h * HD, (h + 1) * HD)
            inner[rows, h : h + 1] = jnp.sum(grad[:, cols].astype(F32) * mixed_ref[rows, cols], axis=-1, keepdims=True)
    stat[0] = mixed_ref[:, 128:256].T
    stat[1] = inner[...].T
    total, queries = kv_ref.shape[0], q_ref.shape[0]
    count = count_ref[0]
    step = 256
    valid = lax.broadcasted_iota(jnp.int32, (128, step), 0) + (total - 128) < count
    for h in range(3):
        cols = slice(h * HD, (h + 1) * HD)
        keys = kv_ref[:, cols]
        values = kv_ref[:, 192 + h * HD : 192 + (h + 1) * HD]
        turned = keys.astype(F32).T.astype(BF)
        d_keys = jnp.zeros((total, HD), F32)
        d_values = jnp.zeros((total, HD), F32)
        for block in range(queries // step):
            rows = slice(block * step, (block + 1) * step)
            query = q_ref[rows, cols]
            grad = do[rows, cols]
            scores = dot_nt(keys, query)
            last = jnp.where(valid, scores[total - 128 :], -1000000000.0)
            scores = jnp.concatenate([scores[: total - 128], last], axis=0)
            probs = jnp.exp(scores - stat[0, 64 + h : 65 + h, rows])
            d_probs = dot_nt(values, grad)
            d_scores = (probs * (d_probs - stat[1, h : h + 1, rows])).astype(BF)
            d_values = d_values + dot_nn(probs.astype(BF), grad)
            d_keys = d_keys + dot_nn(d_scores, query)
            d_query = dot_nn(turned, d_scores) * HD ** (-0.5)
            dq_ref[rows, cols] = d_query.T.astype(BF)
        dkv[:, cols] = d_keys.astype(BF)
        dkv[:, 192 + h * HD : 192 + (h + 1) * HD] = d_values.astype(BF)
    for pair in range(4):
        for side, ref in ((0, own_ref), (1, other_ref)):
            block = (xor_bit(y, pair & 2) * 2 + xor_bit(c, side)) * 2 + xor_bit(half, pair & 1)
            ref[pair] = dkv[pl.ds(pl.multiple_of(block * tokens, 64), tokens), :]


def attend_back(count, pieces, kv, q, mixed, ties=()):
    tokens = pieces[0].shape[0]
    outs = [((4 * tokens, 192), BF), ((4, tokens, 384), BF), ((4, tokens, 384), BF)]
    scratch = [
        pltpu.VMEM((4 * tokens, 192), BF),
        pltpu.VMEM((4 * tokens, 128), F32),
        pltpu.VMEM((2, 128, 4 * tokens), F32),
        pltpu.VMEM((8 * tokens, 384), BF),
    ]
    return call(
        attend_back_kernel, outs, scratch, [SPEC_S] + [SPEC_V] * 7, (count, *pieces, kv, q, mixed),
        micros=11, name="attend_back", ties=ties,
    )


def project_back_kernel(n_a, n_high, d0, d1, d2, d3, da_ref, x_ref, vec_ref, two_ref, ebs_ref, *refs):
    high_refs, a_refs, refs = refs[:n_high], refs[n_high : n_high + n_a], refs[n_high + n_a :]
    dx_ref, dqkv_ref, sums_ref, w, sems = refs
    load = Loader(a_refs, (ORDER_A,), w, sems, 0, 0, 640)
    load.start()
    _, y, _, ten = place()
    hat, rstd = norm_parts(x_ref[...].astype(F32))
    sums_ref[2:6, :] = two_ref[0:4, :]
    sums_ref[10:16, :] = jnp.zeros((6, hat.shape[1]), F32)
    for z in range(4):
        sums_ref[6 + z : 7 + z, :] = ebs_ref[z]
    if n_high:
        sums_ref[16:32, :] = high_refs[0][...]
    for rz in range(4):
        load.wait(rz)
    grad = jnp.zeros(hat.shape, F32)
    for pair, d in enumerate((d0, d1, d2, d3)):
        g = group_of(y, ten, pair)
        piece = d[...]
        dqkv_ref[g] = piece
        sums_ref[pl.ds(10 + g, 1), :576] = jnp.sum(piece.astype(F32), axis=0, keepdims=True)
        grad = grad + dot_nt(piece, w[g][:, :576])
    dx_ref[...] = da_ref[...] + norm_back(hat, rstd, vec_ref[0:1, :], grad)
    sums_ref[0:1, :] = jnp.sum(grad * hat, axis=0, keepdims=True)
    sums_ref[1:2, :] = jnp.sum(grad, axis=0, keepdims=True)


def project_back(pieces, da, x, vec, two, ebs, high, a, ties=()):
    tokens = x.shape[0]
    outs = [((tokens, 768), F32), ((4, tokens, 576), BF), ((16 + 16 * len(high), 768), F32)]
    scratch = [pltpu.VMEM((4, 768, 640), BF), pltpu.SemaphoreType.DMA((32,))]
    return call(
        partial(project_back_kernel, len(a), len(high)),
        outs,
        scratch,
        [SPEC_V] * (9 + len(high)) + [SPEC_A] * len(a),
        (*pieces, da, x, vec, two, ebs, *high, *a),
        micros=4,
        name="project_back",
        ties=ties,
    )


def weigh_both_kernel(m_own, m_got, z_own, z_got, h_own, h_got, a_own, a_got, out_ref):
    for z in range(4):
        expand = dot_nn(m_own[...], h_own[z]) + dot_nn(m_got[...], h_got[z])
        shrink = dot_nn(z_own[...], a_own[z]) + dot_nn(z_got[...], a_got[z])
        for at, xy in enumerate(RING):
            rows = slice(xy * 96, (xy + 1) * 96)
            out_ref[at * 4 + z, 0:96] = expand[rows].astype(BF)
            out_ref[at * 4 + z, 96:192] = shrink[rows].astype(BF)


def weigh_both(args):
    return call(weigh_both_kernel, [((16, 192, 768), BF)], [], [SPEC_V] * 8, args, micros=5, name="weigh_both")[0]


def sum_plane(chunks, mesh_shape):
    dp_size, seq_size, ten_size = mesh_shape
    groups = [
        [((h + (xy >> 1)) * seq_size + 2 * (xy & 1) + c) * ten_size + t for xy in RING]
        for h in range(0, dp_size, 2)
        for c in range(2)
        for t in range(ten_size)
    ]
    rows = chunks.shape[1]
    return lax.psum_scatter(
        chunks.reshape(16 * rows, 768), AXES, scatter_dimension=0, axis_index_groups=groups, tiled=True
    )


def sum_line(chunks):
    return lax.psum_scatter(chunks, "tensor", scatter_dimension=0, tiled=True).astype(F32)


def weigh_attention_kernel(total_ref, *refs):
    x, y, c, ten = place()
    low, high, outs, turned = refs[:8], refs[8:16], refs[16:26], refs[26]
    turned[...] = jnp.concatenate([total_ref[...], jnp.zeros((96, 768), F32)], axis=0).T
    for rz in range(4):
        z = xor_two(ten, rz)
        values = []
        for n_own, n_got, a_own, a_got, q_own, q_got, m_own, m_got in (low, high):
            qkv = dot_nn(n_own[...], q_own[z]) + dot_nn(n_got[...], q_got[z])
            out = dot_nn(a_own[...], m_own[z]) + dot_nn(a_got[...], m_got[z])
            values.append(jnp.concatenate([qkv, out], axis=1).astype(BF))
        for xy in range(4):
            rel = (16 if xy & 2 else 0) | (8 if xy & 1 else 0) | rz
            for n, order in enumerate(SUM_A):
                part, at = part_of(rel, order)
                lines = slice(xy * 96 + n * 48, xy * 96 + (n + 1) * 48)
                for k, value in enumerate(values):
                    outs[n * 5 + part][at, k * 48 : (k + 1) * 48, 0:768] = value[lines]
            block = row_block(x, y, c, rel)
            query = turned[pl.ds(pl.multiple_of(384 + block * 24, 8), 24), :][:, :32]
            other = turned[pl.ds(pl.multiple_of(192 + block * 24, 8), 24), :][:, :32]
            none = jnp.zeros((24, 32), F32)
            pair = jnp.concatenate([none, query, other, none], axis=1)
            more = turned[pl.ds(pl.multiple_of(block * 96, 32), 96), :]
            more = more + jnp.concatenate([pair, jnp.zeros((72, 128), F32)], axis=0)
            part, at = part_of(rel, SUM_A[0])
            outs[part][at, :, 768:896] = more.astype(BF)


def weigh_attention(total, low, high):
    outs = [((n, 96, width), BF) for width in (896, 768) for n in (8, 4, 2, 1, 1)]
    return call(
        weigh_attention_kernel, outs, [pltpu.VMEM((768, 128), F32)], [SPEC_V] * 17, (total, *low, *high), micros=6,
        name="weigh_attention",
    )


def spread_kernel(p0, p1, p2, p3, first_ref, second_ref):
    ten = lax.axis_index("tensor")
    for rz, p in ((0, p0), (2, p1), (1, p2), (3, p3)):
        first_ref[xor_two(ten, rz)] = p[0]
        second_ref[xor_two(ten, rz)] = p[1].astype(F32)


def spread(frames):
    _, tokens, width = frames[0].shape
    outs = [((4, tokens, width), BF), ((4, tokens, width), F32)]
    done = call(spread_kernel, outs, [], [SPEC_V] * 4, frames, name="spread")
    return [d.reshape(2, 1, 2 * tokens, width) for d in done]


def small_params(every):
    vec = every[:, 0, :, :6].transpose(1, 2, 0, 3).reshape(LAYERS, 6, 768)
    eb = every[:, :, :, 6].transpose(2, 1, 0, 3).reshape(LAYERS, 4, 1, 768)
    qv = every[:, :, :, 7, :48].reshape(8, 4, LAYERS, 2, 24).transpose(2, 3, 1, 0, 4).reshape(LAYERS, 2, 4, 192)
    qvb = jnp.concatenate([jnp.zeros_like(qv[:, 0]), qv[:, 1], qv[:, 0]], axis=-1)[:, :, None, :]
    return jnp.pad(vec, ((0, 0), (0, 2), (0, 0))), qvb, eb


def small_everywhere(chunks, order):
    x, y, c, ten = place()
    me = ((x * 2 + y) * 2 + c) * 4 + ten
    rels = []
    for a in range(4):
        for j in range(8):
            rel = sum(BITS[order[k]] for k in range(3) if j & (1 << k))
            rels.append(rel | (BITS[order[3]] if a & 1 else 0) | (BITS["c"] if a & 2 else 0))
    device = jnp.bitwise_xor(jnp.asarray(rels, jnp.int32), me)
    pick = (jnp.arange(32, dtype=jnp.int32)[:, None] == device[None, :]).astype(BF)
    rows = jnp.concatenate([chunk[:, 96:98].reshape(8, -1) for chunk in chunks], axis=0)
    every = jnp.dot(pick, rows, preferred_element_type=F32)
    return every.reshape(8, 4, LAYERS, 8, 96)


def body(shape, features, upstream, key_mask, vectors, proj_qkv, qv_bias, proj_out, expand_weight, expand_bias, shrink_weight):
    dp_size, seq_size, ten_size = shape
    dp, seq, ten = lax.axis_index("dp"), lax.axis_index("seq"), lax.axis_index("tensor")
    tokens = features.shape[2] // 2
    at = (lax.div(ten, 2), 0, lax.rem(ten, 2) * tokens, 0)
    x0 = lax.dynamic_slice(features, at, (1, 1, tokens, 768)).reshape(tokens, 768)
    dy0 = lax.dynamic_slice(upstream, at, (1, 1, tokens, 768)).reshape(tokens, 768)
    count = jnp.sum(lax.dynamic_slice(key_mask, (lax.div(ten, 2), 0, 0), (1, 1, key_mask.shape[2])), axis=(1, 2))

    width = proj_qkv.shape[1]
    wa = jnp.concatenate(
        [
            proj_qkv[:, :, 1],
            proj_qkv[:, :, 2],
            proj_qkv[:, :, 0],
            proj_out.transpose(0, 2, 1),
        ],
        axis=-1,
    )
    we = expand_weight
    ws = shrink_weight.transpose(0, 2, 1)
    if dp_size != 2:
        start = (lax.rem(dp, 2) * 4 + seq) * 96
        wa, we, ws = (
            lax.dynamic_slice_in_dim(lax.all_gather(w, ("dp", "seq"), axis=1, tiled=True), start, 96, axis=1)
            for w in (wa, we, ws)
        )
    if dp_size == 2:
        small = jnp.concatenate(
            [
                vectors.reshape(LAYERS, -1),
                expand_bias,
                qv_bias.reshape(LAYERS, -1),
                jnp.zeros((LAYERS, 48), BF),
            ],
            axis=1,
        )
    else:
        small = jnp.zeros((LAYERS, 768), BF)
    first = jnp.concatenate([wa[0], small, jnp.zeros((6, 768), BF)], axis=0)
    whole = [
        [(d * seq_size + s) * ten_size + t for d in range(h, h + 2) for s in range(seq_size) for t in range(ten_size)]
        for h in range(0, dp_size, 2)
    ]
    low_layer = Gatherer((first, we[0], ws[0]), (ORDER_A, ORDER_E, ORDER_S), shape)
    for _ in range(3):
        low_layer.go()
    (block,) = low_layer.before(jnp.concatenate([wa[1], we[1], ws[1]], axis=0))
    high = lax.all_gather(block, AXES, axis_index_groups=None if dp_size == 2 else whole)
    low_layer.go()
    a_w, e_w, s_w = ((w, [high]) for w in low_layer.core())
    if dp_size == 2:
        vec, qvb, eb = small_params(small_everywhere(a_w[0], ORDER_A))
    else:
        vec = lax.all_gather(vectors, ("dp", "seq"), axis=2, tiled=True).reshape(LAYERS, 6, 8, 96)
        eb = lax.all_gather(expand_bias, ("tensor", "dp", "seq"), axis=1, tiled=True).reshape(LAYERS, 1, 4, 8, 96)
        qv = lax.all_gather(qv_bias, ("tensor", "dp", "seq"), axis=2, tiled=True).reshape(LAYERS, 2, 4, 8, 24)
        vec = jnp.broadcast_to(vec[:, :, None], (LAYERS, 6, 4, 8, 96))
        qv = jnp.pad(qv.transpose(0, 2, 3, 1, 4).reshape(LAYERS, 1, 4, 8, 48), ((0, 0),) * 4 + ((0, 48),))
        vec, qvb, eb = small_params(jnp.concatenate([vec, eb, qv], axis=1).transpose(3, 2, 0, 1, 4).astype(F32))

    state = x0
    kept = []
    for d in range(LAYERS):
        *pieces, n_own, n_other = project(state, vec[d], qvb[d], a_w[d], tokens)
        pieces = [pieces[0]] + [swap_group(pieces[p], p, shape) for p in (1, 2, 3)]
        others = [swap(p[:, :384], "c", shape) for p in pieces]
        *mixed, kv, q, mixed_wide = attend(count, pieces, others)
        mixed = [mixed[0]] + [swap_group(mixed[p], p, shape) for p in (1, 2, 3)]
        x_in = state
        state, after, mixed_all, m_own, m_other, active, slope = mlp(mixed, x_in, vec[d], eb[d], a_w[d], e_w[d], s_w[d])
        kept.append((x_in, n_own, n_other, kv, q, mixed_wide, after, mixed_all, m_own, m_other, active, slope))
    encoded = state.astype(BF)

    grad = dy0
    for d in (1, 0):
        x_in, n_own, n_other, kv, q, mixed_wide, after, mixed_all, m_own, m_other, active, slope = kept[d]
        d0, d1, d2, d3, d_after, d_hid, da_own, da_other, sums_two, ebs, z_own, z_other = mlp_back(
            grad, after, vec[d], slope, a_w[d], e_w[d], s_w[d]
        )
        d_mixed = [d0] + [swap_group(v, p + 1, shape) for p, v in enumerate((d1, d2, d3))]
        m_got, hid_got, z_got, active_got = (swap(v, "c", shape) for v in (m_other, d_hid, z_other, active))
        if d:
            d1, d2, d3, m_got, z_got, hid_got, active_got = fence(*d_mixed[1:], m_got, z_got, hid_got, active_got)
            d_mixed = [d0, d1, d2, d3]
            chunks = weigh_both((m_own, m_got, z_own, z_got, d_hid, hid_got, active, active_got))
            high_sum = sum_plane(chunks, shape)
        else:
            high_sum, *d_mixed = fence(high_sum, *d_mixed)
            high_sum = sum_line(high_sum)
        dq, own, other = attend_back(count, d_mixed, kv, q, mixed_wide, [chunks] if d else [])
        d_kv = (own.astype(F32) + swap(other, "c", shape).astype(F32)).astype(BF)
        back = [jnp.concatenate([d_kv[p], dq[p * tokens : (p + 1) * tokens]], axis=1) for p in range(4)]
        if d == 0:
            *back, m_got, z_got, hid_got, active_got = fence(*back, m_got, z_got, hid_got, active_got)
        back = [back[0]] + [swap_group(back[p], p, shape) for p in (1, 2, 3)]
        if d == 0:
            chunks = weigh_both((m_own, m_got, z_own, z_got, d_hid, hid_got, active, active_got))
            low_sum = sum_plane(chunks, shape)
            high_sum, *back = fence(high_sum, *back)
        grad, d_qkv, total = project_back(back, d_after, x_in, vec[d], sums_two, ebs, [] if d else [high_total], a_w[d], [chunks])
        given = (
            n_own,
            swap(n_other, "c", shape),
            da_own,
            swap(da_other, "c", shape),
            d_qkv,
            swap(d_qkv, "c", shape),
            mixed_all,
            swap(mixed_all, "c", shape),
        )
        if d:
            high_total = total
            high_given = given
    if dp_size == 2:
        total = total + swap(total, "c", shape)
        embedded = total
    else:
        embedded = jnp.zeros_like(total)
        total = lax.psum(total, AXES)
    parts = weigh_attention(embedded, given, high_given)
    sums_a = [Reducer(parts[n * 5 : n * 5 + 5], order, shape) for n, order in enumerate(SUM_A)]
    frames = [jnp.stack([encoded, grad.astype(BF)])]
    last = Together(sums_a)
    (frames[0],) = last.wait(frames[0])
    for step in range(4):
        got = []
        if step == 0:
            got = [low_sum, swap(frames[0], "z2", shape)]
        elif step == 1:
            got = [swap(v, "z1", shape) for v in frames]
        elif step == 3:
            got = [low_sum]
        got = list(last.go(*got))
        if step == 0:
            low_sum = sum_line(got.pop(0))
        elif step == 3:
            low_sum = got.pop()
        frames += got
    small = total.reshape(LAYERS, 16, 768)
    encoded, grad_features = spread(frames)
    chunk, rest = (r.finish() for r in sums_a)
    g_a = [jnp.concatenate([chunk[at : at + 48, :768], rest[at : at + 48]], axis=0) for at in (0, 48)]
    g_e, g_s = ([low_sum[:96], high_sum[:96]], [low_sum[96:], high_sum[96:]])

    if dp_size != 2:
        start = (lax.rem(dp, 2) * 4 + seq) * 96

        def down(block):
            whole = lax.dynamic_update_slice_in_dim(jnp.zeros((768, 768), F32), block, start, axis=0)
            return lax.psum_scatter(whole, ("dp", "seq"), scatter_dimension=0, tiled=True)

        g_a, g_e, g_s = ([down(g) for g in gs] for gs in (g_a, g_e, g_s))
    ga, ge, gs = jnp.stack(g_a), jnp.stack(g_e), jnp.stack(g_s)
    if dp_size == 2:
        turned = chunk[:, 768:864].T.reshape(3, LAYERS, 16, 96)
        grad_vectors = turned[0, :, :6]
        grad_eb = lax.dynamic_index_in_dim(turned[0, :, 6:10], ten, axis=1, keepdims=False)
        pair = lax.dynamic_index_in_dim(turned[1:, :, 10:14], ten, axis=2, keepdims=False)
        grad_qv = pair[:, :, :24].transpose(1, 0, 2)
    else:
        mine = dp * seq_size + seq
        grad_vectors = lax.dynamic_slice_in_dim(small[:, :6], mine * width, width, axis=2)
        eb_width, qv_width = expand_bias.shape[1], qv_bias.shape[2]
        grad_eb = lax.dynamic_slice_in_dim(
            lax.dynamic_index_in_dim(small[:, 6:10], ten, axis=1, keepdims=False), mine * eb_width, eb_width, axis=1
        )
        qv = lax.dynamic_index_in_dim(small[:, 10:14], ten, axis=1, keepdims=False)
        grad_qv = jnp.stack(
            [
                lax.dynamic_slice_in_dim(qv[:, 384:576], mine * qv_width, qv_width, axis=1),
                lax.dynamic_slice_in_dim(qv[:, 192:384], mine * qv_width, qv_width, axis=1),
            ],
            axis=1,
        )
    grad_qkv = jnp.stack([ga[:, :, 384:576], ga[:, :, :192], ga[:, :, 192:384]], axis=2)
    return (
        encoded,
        grad_features,
        grad_vectors,
        grad_qkv,
        grad_qv,
        ga[:, :, 576:].transpose(0, 2, 1),
        ge,
        grad_eb,
        gs.transpose(0, 2, 1),
    )


def solution(mesh):
    placed = (
        P(None, "dp", "seq", None),
        P(None, "dp", "seq", None),
        P(None, "dp", None),
        P(None, None, ("dp", "seq")),
        P(None, ("dp", "seq"), None, "tensor"),
        P(None, None, ("tensor", "dp", "seq")),
        P(None, "tensor", ("dp", "seq")),
        P(None, ("dp", "seq"), "tensor"),
        P(None, ("tensor", "dp", "seq")),
        P(None, "tensor", ("dp", "seq")),
    )
    shape = tuple(mesh.shape[axis] for axis in AXES)
    return jax.shard_map(
        partial(body, shape),
        mesh=mesh,
        in_specs=placed,
        out_specs=(
            P(None, "dp", "seq", None),
            P(None, "dp", "seq", None),
            P(None, None, ("dp", "seq")),
            P(None, ("dp", "seq"), None, "tensor"),
            P(None, None, ("tensor", "dp", "seq")),
            P(None, "tensor", ("dp", "seq")),
            P(None, ("dp", "seq"), "tensor"),
            P(None, ("tensor", "dp", "seq")),
            P(None, "tensor", ("dp", "seq")),
        ),
        check_vma=False,
    )
```

```python
from functools import partial

import jax
import jax.numpy as jnp
from jax import lax
from jax.experimental import pallas as pl
from jax.experimental.pallas import tpu as pltpu
from jax.sharding import PartitionSpec as P

HD = 64
LAYERS = 2
AXES = ("dp", "seq", "tensor")
BF = jnp.bfloat16
F32 = jnp.float32
LIMIT = 48
COST = 1.0e9

BITS = {"x": 16, "y": 8, "c": 4, "z2": 2, "z1": 1}

ORDER_E = ("z2", "z1", "x", "y")
ORDER_S = ("z2", "y", "z1", "x")
ORDER_A = ("z2", "x", "y", "z1")
SUM_A = (("x", "y", "z1", "z2"), ("y", "x", "z1", "z2"))
RING = (0, 1, 3, 2)


SPEC_V = pl.BlockSpec(memory_space=pltpu.VMEM)
SPEC_S = pl.BlockSpec(memory_space=pltpu.SMEM)
SPEC_A = pl.BlockSpec(memory_space=pl.ANY)


def swap(value, bit, mesh_shape):
    dp_size, seq_size, ten_size = mesh_shape
    pairs = []
    for d in range(dp_size):
        for s in range(seq_size):
            for t in range(ten_size):
                e, u, v = d, s, t
                if bit == "x":
                    e = d ^ 1
                elif bit == "y":
                    u = s ^ 2
                elif bit == "c":
                    u = s ^ 1
                elif bit == "z2":
                    v = t ^ 2
                else:
                    v = t ^ 1
                pairs.append(((d * seq_size + s) * ten_size + t, (e * seq_size + u) * ten_size + v))
    return lax.ppermute(value, AXES, pairs)


def swap_group(value, pair, mesh_shape):
    dp_size, seq_size, ten_size = mesh_shape
    ry, rp = pair >> 1, pair & 1
    pairs = []
    for d in range(dp_size):
        for s in range(seq_size):
            for t in range(ten_size):
                to = (d * seq_size + (s ^ (2 * ry))) * ten_size + (t ^ rp)
                pairs.append(((d * seq_size + s) * ten_size + t, to))
    return lax.ppermute(value, AXES, pairs)


def fence(*values):
    return lax.optimization_barrier(values)


class Gatherer:
    def __init__(self, blocks, orders, mesh_shape):
        self.cur, self.orders, self.mesh_shape, self.step = [b[None] for b in blocks], orders, mesh_shape, 0

    def go(self):
        got = [swap(c, o[self.step], self.mesh_shape) for c, o in zip(self.cur, self.orders)]
        self.step += 1
        if self.step < 4:
            self.cur = list(fence(*(jnp.concatenate([c, g], axis=0) for c, g in zip(self.cur, got))))
        else:
            self.more = list(fence(*got))

    def wait(self, *values):
        count = len(self.cur)
        out = fence(*self.cur, *values)
        self.cur = list(out[:count])
        return out[count:]

    def before(self, *values):
        now = self.more if self.step == 4 else self.cur
        count = len(now)
        out = fence(*now, *values)
        if self.step == 4:
            self.more = list(out[:count])
        else:
            self.cur = list(out[:count])
        return out[count:]

    def core(self):
        turned = [[swap(v, "c", self.mesh_shape) for v in pair] for pair in zip(self.cur, self.more)]
        return [[c, m, *t] for c, m, t in zip(self.cur, self.more, turned)]


class Reducer:
    def __init__(self, parts, order, mesh_shape):
        self.parts, self.order, self.mesh_shape, self.step = list(parts), order, mesh_shape, 0

    def send(self):
        return swap(self.parts[self.step].astype(BF), self.order[self.step], self.mesh_shape)

    def take(self, got):
        step = self.step
        for later in range(step + 1, 5):
            size = 8 >> later if later < 4 else 1
            start = size if later < 4 else 0
            self.parts[later] = self.parts[later].astype(F32) + got[start : start + size].astype(F32)
        self.step += 1

    def finish(self):
        return self.parts[4][0]


class Together:
    def __init__(self, sums):
        self.sums = sums

    def wait(self, *values):
        out = list(fence(*(r.parts[r.step] for r in self.sums), *values))
        for r in self.sums:
            r.parts[r.step] = out.pop(0)
        return out

    def go(self, *others):
        got = [r.send() for r in self.sums]
        out = fence(*got, *others)
        for r, g in zip(self.sums, out):
            r.take(g)
        return out[len(got) :]


def part_of(rel, order):
    flags = [1 if rel & BITS[b] else 0 for b in order]
    for step in range(4):
        if flags[step]:
            place = 0
            for f in flags[step + 1 :]:
                place = place * 2 + f
            return step, place
    return 4, 0


def place():
    dp, seq, ten = lax.axis_index("dp"), lax.axis_index("seq"), lax.axis_index("tensor")
    return lax.rem(dp, 2), lax.div(seq, 2), lax.rem(seq, 2), ten


def xor_bit(value, flag):
    return 1 - value if flag else value


def xor_two(value, flags):
    if flags == 0:
        return value
    high, low = lax.div(value, 2), lax.rem(value, 2)
    return xor_bit(high, flags & 2) * 2 + xor_bit(low, flags & 1)


def row_block(x, y, c, rel):
    return (xor_bit(x, rel & 16) * 2 + xor_bit(y, rel & 8)) * 2 + xor_bit(c, rel & 4)


def group_of(y, ten, pair):
    return xor_bit(y, pair & 2) * 2 + xor_bit(lax.rem(ten, 2), pair & 1)


class Loader:
    def __init__(self, refs, orders, scratch, sems, row=0, col=0, width=768):
        x, y, c, ten = place()
        self.copies = {k: [] for k in range(4)}
        self.ten = None if len(refs) == 1 else ten
        if len(refs) == 1:
            for n in range(32):
                block, key = divmod(n, 4)
                dst = scratch.at[key, pl.ds(block * 96, 96)]
                src = refs[0].at[n, pl.ds(row, 96), pl.ds(col, width)]
                self.copies[key].append(pltpu.make_async_copy(src, dst, sems.at[n]))
            return
        rows = 96 * 4 // len(refs)
        for n in range(8 * len(refs)):
            a, j = divmod(n, 8)
            order = orders[a // 4]
            rel = sum(BITS[order[k]] for k in range(3) if j & (1 << k))
            rel |= BITS[order[3]] if a & 1 else 0
            rel |= BITS["c"] if a & 2 else 0
            to = pl.multiple_of(row_block(x, y, c, rel) * 96 + a // 4 * rows, 32)
            dst = scratch.at[xor_two(ten, rel & 3), pl.ds(to, rows)]
            src = refs[a].at[j, pl.ds(0, rows), pl.ds(col, width)]
            self.copies[rel & 3].append(pltpu.make_async_copy(src, dst, sems.at[n]))

    def start(self):
        for k in range(4):
            for copy in self.copies[k]:
                copy.start()

    def wait(self, k):
        for copy in self.copies[k]:
            copy.wait()

    def index(self, k):
        return k if self.ten is None else xor_two(self.ten, k)


def dot_nn(left, right):
    return jnp.dot(left, right, preferred_element_type=F32)


def dot_nt(left, right):
    return lax.dot_general(left, right, (((1,), (1,)), ((), ())), preferred_element_type=F32)


def norm_parts(value):
    center = value - jnp.mean(value, axis=-1, keepdims=True)
    spread = jnp.mean(center * center, axis=-1, keepdims=True)
    rstd = lax.rsqrt(spread + 1e-05)
    return center * rstd, rstd


def norm_back(hat, rstd, gain, grad):
    scaled = grad * gain
    first = jnp.mean(scaled, axis=-1, keepdims=True)
    second = jnp.mean(scaled * hat, axis=-1, keepdims=True)
    return rstd * (scaled - first - hat * second)


def put_transposed(value, turned, own_ref, other_ref, absolute=False):
    x, y, c, _ = place()
    turned[...] = value.T
    for xy in range(4):
        for side, ref in ((0, own_ref), (4, other_ref)):
            if absolute:
                row = (2 * xy + xor_bit(c, side)) * 96
            else:
                row = row_block(x, y, c, (16 if xy & 2 else 0) | (8 if xy & 1 else 0) | side) * 96
            ref[pl.ds(xy * 96, 96), :] = turned[pl.ds(pl.multiple_of(row, 32), 96), :].astype(BF)


def call(kernel, outs, scratch, specs, args, micros=1, name=None, ties=(), limit=LIMIT):
    return pl.pallas_call(
        lambda *refs: kernel(*refs[len(ties) :]),
        out_shape=[jax.ShapeDtypeStruct(s, d) for s, d in outs],
        in_specs=[SPEC_A] * len(ties) + list(specs),
        out_specs=[SPEC_V] * len(outs),
        scratch_shapes=scratch,
        compiler_params=pltpu.CompilerParams(vmem_limit_bytes=limit * 1024 * 1024),
        cost_estimate=pl.CostEstimate(flops=int(micros * COST), bytes_accessed=1000, transcendentals=0),
        name=name,
    )(*ties, *args)


def project_kernel(n_a, x_ref, vec_ref, bias_ref, *refs):
    a_refs, refs = refs[:n_a], refs[n_a:]
    outs, (own_ref, other_ref, w, turned, sems) = refs[:4], refs[4:]
    load = Loader(a_refs, (ORDER_A,), w, sems, 0, 0, 640)
    load.start()
    _, y, _, ten = place()
    hat, _ = norm_parts(x_ref[...].astype(F32))
    normed = hat * vec_ref[0:1, :] + vec_ref[1:2, :]
    low = normed.astype(BF)
    put_transposed(normed, turned, own_ref, other_ref)
    for rz in range(4):
        load.wait(rz)
    for pair in range(4):
        g = group_of(y, ten, pair)
        packed = dot_nn(low, w[g])[:, :576] + bias_ref[g]
        outs[pair][...] = packed.astype(BF)


def project(x, vec, bias, a, tokens, ties=()):
    outs = [((tokens, 576), BF)] * 4 + [((384, tokens), BF)] * 2
    scratch = [pltpu.VMEM((4, 768, 640), BF), pltpu.VMEM((768, tokens), F32), pltpu.SemaphoreType.DMA((32,))]
    return call(
        partial(project_kernel, len(a)), outs, scratch, [SPEC_V] * 3 + [SPEC_A] * len(a), (x, vec, bias, *a),
        micros=4, name="project", ties=ties,
    )


def attend_kernel(count_ref, p0, p1, p2, p3, o0, o1, o2, o3, m0, m1, m2, m3, kv_ref, q_ref, mixed_ref):
    _, y, c, ten = place()
    tokens = p0.shape[0]
    half = lax.rem(ten, 2)
    for pair, (p, o) in enumerate(((p0, o0), (p1, o1), (p2, o2), (p3, o3))):
        for side, ref in ((0, p), (1, o)):
            block = (xor_bit(y, pair & 2) * 2 + xor_bit(c, side)) * 2 + xor_bit(half, pair & 1)
            kv_ref[pl.ds(pl.multiple_of(block * tokens, 64), tokens), :] = ref[:, :384]
        q_ref[pl.ds(pair * tokens, tokens), :] = p[:, 384:576] * jnp.asarray(HD ** (-0.5), BF)
    total = kv_ref.shape[0]
    count = count_ref[0]
    ones = jnp.ones((total, HD), BF)
    valid = lax.broadcasted_iota(jnp.int32, (tokens, 128), 1) + (total - 128) < count
    mixed_ref[:, 192:256] = jnp.zeros((4 * tokens, 64), F32)
    for h in range(3):
        keys = kv_ref[:, h * HD : (h + 1) * HD]
        values = jnp.concatenate([kv_ref[:, 192 + h * HD : 192 + (h + 1) * HD], ones], axis=1)
        for pair, m in enumerate((m0, m1, m2, m3)):
            rows = pl.ds(pair * tokens, tokens)
            scores = dot_nt(q_ref[rows, h * HD : (h + 1) * HD], keys)
            last = jnp.where(valid, scores[:, total - 128 :], -1000000000.0)
            scores = jnp.concatenate([scores[:, : total - 128], last], axis=1)
            highest = jnp.max(scores, axis=-1, keepdims=True)
            expo = jnp.exp(scores - highest).astype(BF)
            both = dot_nn(expo, values)
            weight = both[:, HD : HD + 1]
            mixed = both[:, :HD] / weight
            mixed_ref[rows, h * HD : (h + 1) * HD] = mixed
            m[:, h * HD : (h + 1) * HD] = mixed.astype(BF)
            mixed_ref[rows, 192 + h : 193 + h] = highest + jnp.log(weight)


def attend(count, pieces, others, ties=()):
    tokens = pieces[0].shape[0]
    outs = [((tokens, 192), BF)] * 4 + [
        ((8 * tokens, 384), BF),
        ((4 * tokens, 192), BF),
        ((4 * tokens, 256), F32),
    ]
    return call(
        attend_kernel, outs, [], [SPEC_S] + [SPEC_V] * 8, (count, *pieces, *others),
        micros=7, name="attend", ties=ties,
    )


def mlp_kernel(n_a, n_e, m0, m1, m2, m3, x_ref, vec_ref, eb_ref, *refs):
    a_refs, e_refs = refs[:n_a], refs[n_a : n_a + n_e]
    s_refs, refs = refs[n_a + n_e : n_a + 2 * n_e], refs[n_a + 2 * n_e :]
    (x_out, after_ref, mixed_ref, own_ref, other_ref, active_ref, slope_ref, wo, we, ws, turned, sa, se, ss) = refs
    load_a = Loader(a_refs, (ORDER_A,), wo, sa, 0, 512, 256)
    load_e = Loader(e_refs, (ORDER_E,), we, se, 96)
    load_s = Loader(s_refs, (ORDER_S,), ws, ss, 192)
    load_a.start()
    load_e.start()
    load_s.start()
    _, y, _, ten = place()
    for rz in range(4):
        load_a.wait(rz)
    after = x_ref[...].astype(F32) + vec_ref[2:3, :]
    for pair, m in enumerate((m0, m1, m2, m3)):
        g = group_of(y, ten, pair)
        piece = m[...]
        mixed_ref[g] = piece
        after = after + dot_nt(piece, wo[g][:, 64:])
    after_ref[...] = after
    hat, _ = norm_parts(after)
    normed = hat * vec_ref[3:4, :] + vec_ref[4:5, :]
    low = normed.astype(BF)
    put_transposed(normed, turned, own_ref, other_ref, True)
    out = after + vec_ref[5:6, :]
    for rz in range(4):
        z = load_e.index(rz)
        load_e.wait(rz)
        hidden = dot_nn(low, we[z]) + eb_ref[z]
        lower = 0.5 * (1.0 + lax.erf(hidden * 0.7071067811865476))
        slope_ref[z] = lower + hidden * (jnp.exp(-0.5 * hidden * hidden) * 0.3989422804014327)
        active = (hidden * lower).astype(BF)
        active_ref[z] = active
        load_s.wait(rz)
        out = out + dot_nt(active, ws[z])
    x_out[...] = out


def mlp(pieces, x, vec, eb, a, e, s, ties=()):
    tokens = x.shape[0]
    outs = [
        ((tokens, 768), F32),
        ((tokens, 768), F32),
        ((4, tokens, 192), BF),
        ((384, tokens), BF),
        ((384, tokens), BF),
        ((4, tokens, 768), BF),
        ((4, tokens, 768), F32),
    ]
    scratch = [
        pltpu.VMEM((4, 768, 256), BF),
        pltpu.VMEM((4, 768, 768), BF),
        pltpu.VMEM((4, 768, 768), BF),
        pltpu.VMEM((768, tokens), F32),
        pltpu.SemaphoreType.DMA((32,)),
        pltpu.SemaphoreType.DMA((32,)),
        pltpu.SemaphoreType.DMA((32,)),
    ]
    return call(
        partial(mlp_kernel, len(a), len(e)), outs, scratch, [SPEC_V] * 7 + [SPEC_A] * (len(a) + 2 * len(e)), (*pieces, x, vec, eb, *a, *e, *s),
        micros=12, name="mlp", ties=ties,
    )


def mlp_back_kernel(n_a, n_e, dy_ref, after_ref, vec_ref, slope_ref, *refs):
    a_refs, e_refs = refs[:n_a], refs[n_a : n_a + n_e]
    s_refs, refs = refs[n_a + n_e : n_a + 2 * n_e], refs[n_a + 2 * n_e :]
    d_out, refs = refs[:4], refs[4:]
    (da_ref, hid_ref, a_own, a_other, sums_ref, ebs_ref, z_own, z_other, wo, we, ws, turned, sa, se, ss) = refs
    load_a = Loader(a_refs, (ORDER_A,), wo, sa, 0, 512, 256)
    load_e = Loader(e_refs, (ORDER_E,), we, se, 96)
    load_s = Loader(s_refs, (ORDER_S,), ws, ss, 192)
    load_s.start()
    load_e.start()
    load_a.start()
    _, y, _, ten = place()
    dy = dy_ref[...].astype(F32)
    dz = dy.astype(BF)
    dz_wide = dz.astype(F32)
    put_transposed(dz_wide, turned, z_own, z_other, True)
    grad = jnp.zeros(dy.shape, F32)
    for rz in range(4):
        z = load_s.index(rz)
        load_s.wait(rz)
        d_active = dot_nn(dz, ws[z])
        d_hidden = (d_active * slope_ref[z]).astype(BF)
        hid_ref[z] = d_hidden
        ebs_ref[z] = jnp.sum(d_hidden.astype(F32), axis=0, keepdims=True)
        load_e.wait(rz)
        grad = grad + dot_nt(d_hidden, we[z])
    hat, rstd = norm_parts(after_ref[...])
    d_after = dy + norm_back(hat, rstd, vec_ref[3:4, :], grad)
    da_ref[...] = d_after
    da = d_after.astype(BF)
    da_wide = da.astype(F32)
    put_transposed(da_wide, turned, a_own, a_other)
    sums_ref[0:1, :] = jnp.sum(da_wide, axis=0, keepdims=True)
    sums_ref[1:2, :] = jnp.sum(grad * hat, axis=0, keepdims=True)
    sums_ref[2:3, :] = jnp.sum(grad, axis=0, keepdims=True)
    sums_ref[3:4, :] = jnp.sum(dz_wide, axis=0, keepdims=True)
    sums_ref[4:8, :] = jnp.zeros((4, dy.shape[1]), F32)
    for rz in range(4):
        load_a.wait(rz)
    for pair in range(4):
        g = group_of(y, ten, pair)
        d_out[pair][...] = dot_nn(da, wo[g])[:, 64:].astype(BF)


def mlp_back(dy, after, vec, slope, a, e, s, ties=()):
    tokens = dy.shape[0]
    outs = [((tokens, 192), BF)] * 4 + [
        ((tokens, 768), F32),
        ((4, tokens, 768), BF),
        ((384, tokens), BF),
        ((384, tokens), BF),
        ((8, 768), F32),
        ((4, 1, 768), F32),
        ((384, tokens), BF),
        ((384, tokens), BF),
    ]
    scratch = [
        pltpu.VMEM((4, 768, 256), BF),
        pltpu.VMEM((4, 768, 768), BF),
        pltpu.VMEM((4, 768, 768), BF),
        pltpu.VMEM((768, tokens), F32),
        pltpu.SemaphoreType.DMA((32,)),
        pltpu.SemaphoreType.DMA((32,)),
        pltpu.SemaphoreType.DMA((32,)),
    ]
    return call(
        partial(mlp_back_kernel, len(a), len(e)), outs, scratch, [SPEC_V] * 4 + [SPEC_A] * (len(a) + 2 * len(e)),
        (dy, after, vec, slope, *a, *e, *s), micros=11, name="mlp_back", ties=ties,
    )


def attend_back_kernel(count_ref, d0, d1, d2, d3, kv_ref, q_ref, mixed_ref, dq_ref, own_ref, other_ref, do, inner, stat, dkv):
    _, y, c, ten = place()
    tokens = d0.shape[0]
    half = lax.rem(ten, 2)
    inner[...] = jnp.zeros(inner.shape, F32)
    for pair, d in enumerate((d0, d1, d2, d3)):
        rows = pl.ds(pair * tokens, tokens)
        grad = d[...]
        do[rows, :] = grad
        for h in range(3):
            cols = slice(h * HD, (h + 1) * HD)
            inner[rows, h : h + 1] = jnp.sum(grad[:, cols].astype(F32) * mixed_ref[rows, cols], axis=-1, keepdims=True)
    stat[0] = mixed_ref[:, 128:256].T
    stat[1] = inner[...].T
    total, queries = kv_ref.shape[0], q_ref.shape[0]
    count = count_ref[0]
    step = 256
    valid = lax.broadcasted_iota(jnp.int32, (128, step), 0) + (total - 128) < count
    for h in range(3):
        cols = slice(h * HD, (h + 1) * HD)
        keys = kv_ref[:, cols]
        values = kv_ref[:, 192 + h * HD : 192 + (h + 1) * HD]
        turned = keys.astype(F32).T.astype(BF)
        d_keys = jnp.zeros((total, HD), F32)
        d_values = jnp.zeros((total, HD), F32)
        for block in range(queries // step):
            rows = slice(block * step, (block + 1) * step)
            query = q_ref[rows, cols]
            grad = do[rows, cols]
            scores = dot_nt(keys, query)
            last = jnp.where(valid, scores[total - 128 :], -1000000000.0)
            scores = jnp.concatenate([scores[: total - 128], last], axis=0)
            probs = jnp.exp(scores - stat[0, 64 + h : 65 + h, rows])
            d_probs = dot_nt(values, grad)
            d_scores = (probs * (d_probs - stat[1, h : h + 1, rows])).astype(BF)
            d_values = d_values + dot_nn(probs.astype(BF), grad)
            d_keys = d_keys + dot_nn(d_scores, query)
            d_query = dot_nn(turned, d_scores) * HD ** (-0.5)
            dq_ref[rows, cols] = d_query.T.astype(BF)
        dkv[:, cols] = d_keys.astype(BF)
        dkv[:, 192 + h * HD : 192 + (h + 1) * HD] = d_values.astype(BF)
    for pair in range(4):
        for side, ref in ((0, own_ref), (1, other_ref)):
            block = (xor_bit(y, pair & 2) * 2 + xor_bit(c, side)) * 2 + xor_bit(half, pair & 1)
            ref[pair] = dkv[pl.ds(pl.multiple_of(block * tokens, 64), tokens), :]


def attend_back(count, pieces, kv, q, mixed, ties=()):
    tokens = pieces[0].shape[0]
    outs = [((4 * tokens, 192), BF), ((4, tokens, 384), BF), ((4, tokens, 384), BF)]
    scratch = [
        pltpu.VMEM((4 * tokens, 192), BF),
        pltpu.VMEM((4 * tokens, 128), F32),
        pltpu.VMEM((2, 128, 4 * tokens), F32),
        pltpu.VMEM((8 * tokens, 384), BF),
    ]
    return call(
        attend_back_kernel, outs, scratch, [SPEC_S] + [SPEC_V] * 7, (count, *pieces, kv, q, mixed),
        micros=11, name="attend_back", ties=ties,
    )


def project_back_kernel(n_a, n_high, d0, d1, d2, d3, da_ref, x_ref, vec_ref, two_ref, ebs_ref, *refs):
    high_refs, a_refs, refs = refs[:n_high], refs[n_high : n_high + n_a], refs[n_high + n_a :]
    dx_ref, dqkv_ref, sums_ref, w, sems = refs
    load = Loader(a_refs, (ORDER_A,), w, sems, 0, 0, 640)
    load.start()
    _, y, _, ten = place()
    hat, rstd = norm_parts(x_ref[...].astype(F32))
    sums_ref[2:6, :] = two_ref[0:4, :]
    sums_ref[10:16, :] = jnp.zeros((6, hat.shape[1]), F32)
    for z in range(4):
        sums_ref[6 + z : 7 + z, :] = ebs_ref[z]
    if n_high:
        sums_ref[16:32, :] = high_refs[0][...]
    for rz in range(4):
        load.wait(rz)
    grad = jnp.zeros(hat.shape, F32)
    for pair, d in enumerate((d0, d1, d2, d3)):
        g = group_of(y, ten, pair)
        piece = d[...]
        dqkv_ref[g] = piece
        sums_ref[pl.ds(10 + g, 1), :576] = jnp.sum(piece.astype(F32), axis=0, keepdims=True)
        grad = grad + dot_nt(piece, w[g][:, :576])
    dx_ref[...] = da_ref[...] + norm_back(hat, rstd, vec_ref[0:1, :], grad)
    sums_ref[0:1, :] = jnp.sum(grad * hat, axis=0, keepdims=True)
    sums_ref[1:2, :] = jnp.sum(grad, axis=0, keepdims=True)


def project_back(pieces, da, x, vec, two, ebs, high, a, ties=()):
    tokens = x.shape[0]
    outs = [((tokens, 768), F32), ((4, tokens, 576), BF), ((16 + 16 * len(high), 768), F32)]
    scratch = [pltpu.VMEM((4, 768, 640), BF), pltpu.SemaphoreType.DMA((32,))]
    return call(
        partial(project_back_kernel, len(a), len(high)),
        outs,
        scratch,
        [SPEC_V] * (9 + len(high)) + [SPEC_A] * len(a),
        (*pieces, da, x, vec, two, ebs, *high, *a),
        micros=4,
        name="project_back",
        ties=ties,
    )


def weigh_both_kernel(m_own, m_got, z_own, z_got, h_own, h_got, a_own, a_got, out_ref):
    for z in range(4):
        expand = dot_nn(m_own[...], h_own[z]) + dot_nn(m_got[...], h_got[z])
        shrink = dot_nn(z_own[...], a_own[z]) + dot_nn(z_got[...], a_got[z])
        for at, xy in enumerate(RING):
            rows = slice(xy * 96, (xy + 1) * 96)
            out_ref[at * 4 + z, 0:96] = expand[rows].astype(BF)
            out_ref[at * 4 + z, 96:192] = shrink[rows].astype(BF)


def weigh_both(args):
    return call(weigh_both_kernel, [((16, 192, 768), BF)], [], [SPEC_V] * 8, args, micros=5, name="weigh_both")[0]


def sum_plane(chunks, mesh_shape):
    dp_size, seq_size, ten_size = mesh_shape
    groups = [
        [((h + (xy >> 1)) * seq_size + 2 * (xy & 1) + c) * ten_size + t for xy in RING]
        for h in range(0, dp_size, 2)
        for c in range(2)
        for t in range(ten_size)
    ]
    rows = chunks.shape[1]
    return lax.psum_scatter(
        chunks.reshape(16 * rows, 768), AXES, scatter_dimension=0, axis_index_groups=groups, tiled=True
    )


def sum_line(chunks):
    return lax.psum_scatter(chunks, "tensor", scatter_dimension=0, tiled=True).astype(F32)


def weigh_attention_kernel(total_ref, *refs):
    x, y, c, ten = place()
    low, high, outs, turned = refs[:8], refs[8:16], refs[16:26], refs[26]
    turned[...] = jnp.concatenate([total_ref[...], jnp.zeros((96, 768), F32)], axis=0).T
    for rz in range(4):
        z = xor_two(ten, rz)
        values = []
        for n_own, n_got, a_own, a_got, q_own, q_got, m_own, m_got in (low, high):
            qkv = dot_nn(n_own[...], q_own[z]) + dot_nn(n_got[...], q_got[z])
            out = dot_nn(a_own[...], m_own[z]) + dot_nn(a_got[...], m_got[z])
            values.append(jnp.concatenate([qkv, out], axis=1).astype(BF))
        for xy in range(4):
            rel = (16 if xy & 2 else 0) | (8 if xy & 1 else 0) | rz
            for n, order in enumerate(SUM_A):
                part, at = part_of(rel, order)
                lines = slice(xy * 96 + n * 48, xy * 96 + (n + 1) * 48)
                for k, value in enumerate(values):
                    outs[n * 5 + part][at, k * 48 : (k + 1) * 48, 0:768] = value[lines]
            block = row_block(x, y, c, rel)
            query = turned[pl.ds(pl.multiple_of(384 + block * 24, 8), 24), :][:, :32]
            other = turned[pl.ds(pl.multiple_of(192 + block * 24, 8), 24), :][:, :32]
            none = jnp.zeros((24, 32), F32)
            pair = jnp.concatenate([none, query, other, none], axis=1)
            more = turned[pl.ds(pl.multiple_of(block * 96, 32), 96), :]
            more = more + jnp.concatenate([pair, jnp.zeros((72, 128), F32)], axis=0)
            part, at = part_of(rel, SUM_A[0])
            outs[part][at, :, 768:896] = more.astype(BF)


def weigh_attention(total, low, high):
    outs = [((n, 96, width), BF) for width in (896, 768) for n in (8, 4, 2, 1, 1)]
    return call(
        weigh_attention_kernel, outs, [pltpu.VMEM((768, 128), F32)], [SPEC_V] * 17, (total, *low, *high), micros=6,
        name="weigh_attention",
    )


def spread_kernel(p0, p1, p2, p3, first_ref, second_ref):
    ten = lax.axis_index("tensor")
    for rz, p in ((0, p0), (2, p1), (1, p2), (3, p3)):
        first_ref[xor_two(ten, rz)] = p[0]
        second_ref[xor_two(ten, rz)] = p[1].astype(F32)


def spread(frames):
    _, tokens, width = frames[0].shape
    outs = [((4, tokens, width), BF), ((4, tokens, width), F32)]
    done = call(spread_kernel, outs, [], [SPEC_V] * 4, frames, name="spread")
    return [d.reshape(2, 1, 2 * tokens, width) for d in done]


def small_params(every):
    vec = every[:, 0, :, :6].transpose(1, 2, 0, 3).reshape(LAYERS, 6, 768)
    eb = every[:, :, :, 6].transpose(2, 1, 0, 3).reshape(LAYERS, 4, 1, 768)
    qv = every[:, :, :, 7, :48].reshape(8, 4, LAYERS, 2, 24).transpose(2, 3, 1, 0, 4).reshape(LAYERS, 2, 4, 192)
    qvb = jnp.concatenate([jnp.zeros_like(qv[:, 0]), qv[:, 1], qv[:, 0]], axis=-1)[:, :, None, :]
    return jnp.pad(vec, ((0, 0), (0, 2), (0, 0))), qvb, eb


def small_everywhere(chunks, order):
    x, y, c, ten = place()
    me = ((x * 2 + y) * 2 + c) * 4 + ten
    rels = []
    for a in range(4):
        for j in range(8):
            rel = sum(BITS[order[k]] for k in range(3) if j & (1 << k))
            rels.append(rel | (BITS[order[3]] if a & 1 else 0) | (BITS["c"] if a & 2 else 0))
    device = jnp.bitwise_xor(jnp.asarray(rels, jnp.int32), me)
    pick = (jnp.arange(32, dtype=jnp.int32)[:, None] == device[None, :]).astype(BF)
    rows = jnp.concatenate([chunk[:, 96:98].reshape(8, -1) for chunk in chunks], axis=0)
    every = jnp.dot(pick, rows, preferred_element_type=F32)
    return every.reshape(8, 4, LAYERS, 8, 96)


def body(shape, features, upstream, key_mask, vectors, proj_qkv, qv_bias, proj_out, expand_weight, expand_bias, shrink_weight):
    dp_size, seq_size, ten_size = shape
    dp, seq, ten = lax.axis_index("dp"), lax.axis_index("seq"), lax.axis_index("tensor")
    tokens = features.shape[2] // 2
    at = (lax.div(ten, 2), 0, lax.rem(ten, 2) * tokens, 0)
    x0 = lax.dynamic_slice(features, at, (1, 1, tokens, 768)).reshape(tokens, 768)
    dy0 = lax.dynamic_slice(upstream, at, (1, 1, tokens, 768)).reshape(tokens, 768)
    count = jnp.sum(lax.dynamic_slice(key_mask, (lax.div(ten, 2), 0, 0), (1, 1, key_mask.shape[2])), axis=(1, 2))

    width = proj_qkv.shape[1]
    wa = jnp.concatenate(
        [
            proj_qkv[:, :, 1],
            proj_qkv[:, :, 2],
            proj_qkv[:, :, 0],
            proj_out.transpose(0, 2, 1),
        ],
        axis=-1,
    )
    we = expand_weight
    ws = shrink_weight.transpose(0, 2, 1)
    if dp_size != 2:
        start = (lax.rem(dp, 2) * 4 + seq) * 96
        wa, we, ws = (
            lax.dynamic_slice_in_dim(lax.all_gather(w, ("dp", "seq"), axis=1, tiled=True), start, 96, axis=1)
            for w in (wa, we, ws)
        )
    if dp_size == 2:
        small = jnp.concatenate(
            [
                vectors.reshape(LAYERS, -1),
                expand_bias,
                qv_bias.reshape(LAYERS, -1),
                jnp.zeros((LAYERS, 48), BF),
            ],
            axis=1,
        )
    else:
        small = jnp.zeros((LAYERS, 768), BF)
    first = jnp.concatenate([wa[0], small, jnp.zeros((6, 768), BF)], axis=0)
    whole = [
        [(d * seq_size + s) * ten_size + t for d in range(h, h + 2) for s in range(seq_size) for t in range(ten_size)]
        for h in range(0, dp_size, 2)
    ]
    low_layer = Gatherer((first, we[0], ws[0]), (ORDER_A, ORDER_E, ORDER_S), shape)
    for _ in range(3):
        low_layer.go()
    (block,) = low_layer.before(jnp.concatenate([wa[1], we[1], ws[1]], axis=0))
    high = lax.all_gather(block, AXES, axis_index_groups=None if dp_size == 2 else whole)
    low_layer.go()
    a_w, e_w, s_w = ((w, [high]) for w in low_layer.core())
    if dp_size == 2:
        vec, qvb, eb = small_params(small_everywhere(a_w[0], ORDER_A))
    else:
        vec = lax.all_gather(vectors, ("dp", "seq"), axis=2, tiled=True).reshape(LAYERS, 6, 8, 96)
        eb = lax.all_gather(expand_bias, ("tensor", "dp", "seq"), axis=1, tiled=True).reshape(LAYERS, 1, 4, 8, 96)
        qv = lax.all_gather(qv_bias, ("tensor", "dp", "seq"), axis=2, tiled=True).reshape(LAYERS, 2, 4, 8, 24)
        vec = jnp.broadcast_to(vec[:, :, None], (LAYERS, 6, 4, 8, 96))
        qv = jnp.pad(qv.transpose(0, 2, 3, 1, 4).reshape(LAYERS, 1, 4, 8, 48), ((0, 0),) * 4 + ((0, 48),))
        vec, qvb, eb = small_params(jnp.concatenate([vec, eb, qv], axis=1).transpose(3, 2, 0, 1, 4).astype(F32))

    state = x0
    kept = []
    for d in range(LAYERS):
        *pieces, n_own, n_other = project(state, vec[d], qvb[d], a_w[d], tokens)
        pieces = [pieces[0]] + [swap_group(pieces[p], p, shape) for p in (1, 2, 3)]
        others = [swap(p[:, :384], "c", shape) for p in pieces]
        *mixed, kv, q, mixed_wide = attend(count, pieces, others)
        mixed = [mixed[0]] + [swap_group(mixed[p], p, shape) for p in (1, 2, 3)]
        x_in = state
        state, after, mixed_all, m_own, m_other, active, slope = mlp(mixed, x_in, vec[d], eb[d], a_w[d], e_w[d], s_w[d])
        kept.append((x_in, n_own, n_other, kv, q, mixed_wide, after, mixed_all, m_own, m_other, active, slope))
    encoded = state.astype(BF)

    grad = dy0
    for d in (1, 0):
        x_in, n_own, n_other, kv, q, mixed_wide, after, mixed_all, m_own, m_other, active, slope = kept[d]
        d0, d1, d2, d3, d_after, d_hid, da_own, da_other, sums_two, ebs, z_own, z_other = mlp_back(
            grad, after, vec[d], slope, a_w[d], e_w[d], s_w[d]
        )
        d_mixed = [d0] + [swap_group(v, p + 1, shape) for p, v in enumerate((d1, d2, d3))]
        m_got, hid_got, z_got, active_got = (swap(v, "c", shape) for v in (m_other, d_hid, z_other, active))
        if d:
            d1, d2, d3, m_got, z_got, hid_got, active_got = fence(*d_mixed[1:], m_got, z_got, hid_got, active_got)
            d_mixed = [d0, d1, d2, d3]
            chunks = weigh_both((m_own, m_got, z_own, z_got, d_hid, hid_got, active, active_got))
            high_sum = sum_plane(chunks, shape)
        else:
            high_sum, *d_mixed = fence(high_sum, *d_mixed)
            high_sum = sum_line(high_sum)
        dq, own, other = attend_back(count, d_mixed, kv, q, mixed_wide, [chunks] if d else [])
        d_kv = (own.astype(F32) + swap(other, "c", shape).astype(F32)).astype(BF)
        back = [jnp.concatenate([d_kv[p], dq[p * tokens : (p + 1) * tokens]], axis=1) for p in range(4)]
        if d == 0:
            *back, m_got, z_got, hid_got, active_got = fence(*back, m_got, z_got, hid_got, active_got)
        back = [back[0]] + [swap_group(back[p], p, shape) for p in (1, 2, 3)]
        if d == 0:
            chunks = weigh_both((m_own, m_got, z_own, z_got, d_hid, hid_got, active, active_got))
            low_sum = sum_plane(chunks, shape)
            high_sum, *back = fence(high_sum, *back)
        grad, d_qkv, total = project_back(back, d_after, x_in, vec[d], sums_two, ebs, [] if d else [high_total], a_w[d], [chunks])
        given = (
            n_own,
            swap(n_other, "c", shape),
            da_own,
            swap(da_other, "c", shape),
            d_qkv,
            swap(d_qkv, "c", shape),
            mixed_all,
            swap(mixed_all, "c", shape),
        )
        if d:
            high_total = total
            high_given = given
    if dp_size == 2:
        total = total + swap(total, "c", shape)
        embedded = total
    else:
        embedded = jnp.zeros_like(total)
        total = lax.psum(total, AXES)
    parts = weigh_attention(embedded, given, high_given)
    sums_a = [Reducer(parts[n * 5 : n * 5 + 5], order, shape) for n, order in enumerate(SUM_A)]
    frames = [jnp.stack([encoded, grad.astype(BF)])]
    last = Together(sums_a)
    (frames[0],) = last.wait(frames[0])
    frames.append(swap(frames[0], "z2", shape))
    frames += [swap(v, "z1", shape) for v in frames]
    for step in range(4):
        if step == 0:
            low_sum = sum_line(last.go(low_sum)[0])
        elif step == 1:
            frames = last.go(*frames)
        elif step == 2:
            last.go()
        else:
            (low_sum,) = last.go(low_sum)
    small = total.reshape(LAYERS, 16, 768)
    encoded, grad_features = spread(frames)
    chunk, rest = (r.finish() for r in sums_a)
    g_a = [jnp.concatenate([chunk[at : at + 48, :768], rest[at : at + 48]], axis=0) for at in (0, 48)]
    g_e, g_s = ([low_sum[:96], high_sum[:96]], [low_sum[96:], high_sum[96:]])

    if dp_size != 2:
        start = (lax.rem(dp, 2) * 4 + seq) * 96

        def down(block):
            whole = lax.dynamic_update_slice_in_dim(jnp.zeros((768, 768), F32), block, start, axis=0)
            return lax.psum_scatter(whole, ("dp", "seq"), scatter_dimension=0, tiled=True)

        g_a, g_e, g_s = ([down(g) for g in gs] for gs in (g_a, g_e, g_s))
    ga, ge, gs = jnp.stack(g_a), jnp.stack(g_e), jnp.stack(g_s)
    if dp_size == 2:
        turned = chunk[:, 768:864].T.reshape(3, LAYERS, 16, 96)
        grad_vectors = turned[0, :, :6]
        grad_eb = lax.dynamic_index_in_dim(turned[0, :, 6:10], ten, axis=1, keepdims=False)
        pair = lax.dynamic_index_in_dim(turned[1:, :, 10:14], ten, axis=2, keepdims=False)
        grad_qv = pair[:, :, :24].transpose(1, 0, 2)
    else:
        mine = dp * seq_size + seq
        grad_vectors = lax.dynamic_slice_in_dim(small[:, :6], mine * width, width, axis=2)
        eb_width, qv_width = expand_bias.shape[1], qv_bias.shape[2]
        grad_eb = lax.dynamic_slice_in_dim(
            lax.dynamic_index_in_dim(small[:, 6:10], ten, axis=1, keepdims=False), mine * eb_width, eb_width, axis=1
        )
        qv = lax.dynamic_index_in_dim(small[:, 10:14], ten, axis=1, keepdims=False)
        grad_qv = jnp.stack(
            [
                lax.dynamic_slice_in_dim(qv[:, 384:576], mine * qv_width, qv_width, axis=1),
                lax.dynamic_slice_in_dim(qv[:, 192:384], mine * qv_width, qv_width, axis=1),
            ],
            axis=1,
        )
    grad_qkv = jnp.stack([ga[:, :, 384:576], ga[:, :, :192], ga[:, :, 192:384]], axis=2)
    return (
        encoded,
        grad_features,
        grad_vectors,
        grad_qkv,
        grad_qv,
        ga[:, :, 576:].transpose(0, 2, 1),
        ge,
        grad_eb,
        gs.transpose(0, 2, 1),
    )


def solution(mesh):
    placed = (
        P(None, "dp", "seq", None),
        P(None, "dp", "seq", None),
        P(None, "dp", None),
        P(None, None, ("dp", "seq")),
        P(None, ("dp", "seq"), None, "tensor"),
        P(None, None, ("tensor", "dp", "seq")),
        P(None, "tensor", ("dp", "seq")),
        P(None, ("dp", "seq"), "tensor"),
        P(None, ("tensor", "dp", "seq")),
        P(None, "tensor", ("dp", "seq")),
    )
    shape = tuple(mesh.shape[axis] for axis in AXES)
    return jax.shard_map(
        partial(body, shape),
        mesh=mesh,
        in_specs=placed,
        out_specs=(
            P(None, "dp", "seq", None),
            P(None, "dp", "seq", None),
            P(None, None, ("dp", "seq")),
            P(None, ("dp", "seq"), None, "tensor"),
            P(None, None, ("tensor", "dp", "seq")),
            P(None, "tensor", ("dp", "seq")),
            P(None, ("dp", "seq"), "tensor"),
            P(None, ("tensor", "dp", "seq")),
            P(None, "tensor", ("dp", "seq")),
        ),
        check_vma=False,
    )
```

```python
from functools import partial

import jax
import jax.numpy as jnp
from jax import lax
from jax.experimental import pallas as pl
from jax.experimental.pallas import tpu as pltpu
from jax.sharding import PartitionSpec as P

HD = 64
LAYERS = 2
AXES = ("dp", "seq", "tensor")
BF = jnp.bfloat16
F32 = jnp.float32
LIMIT = 48
COST = 1.0e9

BITS = {"x": 16, "y": 8, "c": 4, "z2": 2, "z1": 1}

ORDER_E = ("z2", "z1", "x", "y")
ORDER_S = ("z2", "y", "z1", "x")
ORDER_A = ("z2", "x", "y", "z1")
SUM_A = (("x", "y", "z1", "z2"), ("y", "x", "z1", "z2"))
RING = (0, 1, 3, 2)


SPEC_V = pl.BlockSpec(memory_space=pltpu.VMEM)
SPEC_S = pl.BlockSpec(memory_space=pltpu.SMEM)
SPEC_A = pl.BlockSpec(memory_space=pl.ANY)


def swap(value, bit, mesh_shape):
    dp_size, seq_size, ten_size = mesh_shape
    pairs = []
    for d in range(dp_size):
        for s in range(seq_size):
            for t in range(ten_size):
                e, u, v = d, s, t
                if bit == "x":
                    e = d ^ 1
                elif bit == "y":
                    u = s ^ 2
                elif bit == "c":
                    u = s ^ 1
                elif bit == "z2":
                    v = t ^ 2
                else:
                    v = t ^ 1
                pairs.append(((d * seq_size + s) * ten_size + t, (e * seq_size + u) * ten_size + v))
    return lax.ppermute(value, AXES, pairs)


def swap_group(value, pair, mesh_shape):
    dp_size, seq_size, ten_size = mesh_shape
    ry, rp = pair >> 1, pair & 1
    pairs = []
    for d in range(dp_size):
        for s in range(seq_size):
            for t in range(ten_size):
                to = (d * seq_size + (s ^ (2 * ry))) * ten_size + (t ^ rp)
                pairs.append(((d * seq_size + s) * ten_size + t, to))
    return lax.ppermute(value, AXES, pairs)


def fence(*values):
    return lax.optimization_barrier(values)


class Gatherer:
    def __init__(self, blocks, orders, mesh_shape):
        self.cur, self.orders, self.mesh_shape, self.step = [b[None] for b in blocks], orders, mesh_shape, 0

    def go(self):
        got = [swap(c, o[self.step], self.mesh_shape) for c, o in zip(self.cur, self.orders)]
        self.step += 1
        if self.step < 4:
            self.cur = list(fence(*(jnp.concatenate([c, g], axis=0) for c, g in zip(self.cur, got))))
        else:
            self.more = list(fence(*got))

    def wait(self, *values):
        count = len(self.cur)
        out = fence(*self.cur, *values)
        self.cur = list(out[:count])
        return out[count:]

    def before(self, *values):
        now = self.more if self.step == 4 else self.cur
        count = len(now)
        out = fence(*now, *values)
        if self.step == 4:
            self.more = list(out[:count])
        else:
            self.cur = list(out[:count])
        return out[count:]

    def core(self):
        turned = [[swap(v, "c", self.mesh_shape) for v in pair] for pair in zip(self.cur, self.more)]
        return [[c, m, *t] for c, m, t in zip(self.cur, self.more, turned)]


class Reducer:
    def __init__(self, parts, order, mesh_shape):
        self.parts, self.order, self.mesh_shape, self.step = list(parts), order, mesh_shape, 0

    def send(self):
        return swap(self.parts[self.step].astype(BF), self.order[self.step], self.mesh_shape)

    def take(self, got):
        step = self.step
        for later in range(step + 1, 5):
            size = 8 >> later if later < 4 else 1
            start = size if later < 4 else 0
            self.parts[later] = self.parts[later].astype(F32) + got[start : start + size].astype(F32)
        self.step += 1

    def finish(self):
        return self.parts[4][0]


class Together:
    def __init__(self, sums):
        self.sums = sums

    def wait(self, *values):
        out = list(fence(*(r.parts[r.step] for r in self.sums), *values))
        for r in self.sums:
            r.parts[r.step] = out.pop(0)
        return out

    def go(self, *others):
        got = [r.send() for r in self.sums]
        out = fence(*got, *others)
        for r, g in zip(self.sums, out):
            r.take(g)
        return out[len(got) :]


def part_of(rel, order):
    flags = [1 if rel & BITS[b] else 0 for b in order]
    for step in range(4):
        if flags[step]:
            place = 0
            for f in flags[step + 1 :]:
                place = place * 2 + f
            return step, place
    return 4, 0


def place():
    dp, seq, ten = lax.axis_index("dp"), lax.axis_index("seq"), lax.axis_index("tensor")
    return lax.rem(dp, 2), lax.div(seq, 2), lax.rem(seq, 2), ten


def xor_bit(value, flag):
    return 1 - value if flag else value


def xor_two(value, flags):
    if flags == 0:
        return value
    high, low = lax.div(value, 2), lax.rem(value, 2)
    return xor_bit(high, flags & 2) * 2 + xor_bit(low, flags & 1)


def row_block(x, y, c, rel):
    return (xor_bit(x, rel & 16) * 2 + xor_bit(y, rel & 8)) * 2 + xor_bit(c, rel & 4)


def group_of(y, ten, pair):
    return xor_bit(y, pair & 2) * 2 + xor_bit(lax.rem(ten, 2), pair & 1)


class Loader:
    def __init__(self, refs, orders, scratch, sems, row=0, col=0, width=768):
        x, y, c, ten = place()
        self.copies = {k: [] for k in range(4)}
        self.ten = None if len(refs) == 1 else ten
        if len(refs) == 1:
            for n in range(32):
                block, key = divmod(n, 4)
                dst = scratch.at[key, pl.ds(block * 96, 96)]
                src = refs[0].at[n, pl.ds(row, 96), pl.ds(col, width)]
                self.copies[key].append(pltpu.make_async_copy(src, dst, sems.at[n]))
            return
        rows = 96 * 4 // len(refs)
        for n in range(8 * len(refs)):
            a, j = divmod(n, 8)
            order = orders[a // 4]
            rel = sum(BITS[order[k]] for k in range(3) if j & (1 << k))
            rel |= BITS[order[3]] if a & 1 else 0
            rel |= BITS["c"] if a & 2 else 0
            to = pl.multiple_of(row_block(x, y, c, rel) * 96 + a // 4 * rows, 32)
            dst = scratch.at[xor_two(ten, rel & 3), pl.ds(to, rows)]
            src = refs[a].at[j, pl.ds(0, rows), pl.ds(col, width)]
            self.copies[rel & 3].append(pltpu.make_async_copy(src, dst, sems.at[n]))

    def start(self):
        for k in range(4):
            for copy in self.copies[k]:
                copy.start()

    def wait(self, k):
        for copy in self.copies[k]:
            copy.wait()

    def index(self, k):
        return k if self.ten is None else xor_two(self.ten, k)


def dot_nn(left, right):
    return jnp.dot(left, right, preferred_element_type=F32)


def dot_nt(left, right):
    return lax.dot_general(left, right, (((1,), (1,)), ((), ())), preferred_element_type=F32)


def norm_parts(value):
    center = value - jnp.mean(value, axis=-1, keepdims=True)
    spread = jnp.mean(center * center, axis=-1, keepdims=True)
    rstd = lax.rsqrt(spread + 1e-05)
    return center * rstd, rstd


def norm_back(hat, rstd, gain, grad):
    scaled = grad * gain
    first = jnp.mean(scaled, axis=-1, keepdims=True)
    second = jnp.mean(scaled * hat, axis=-1, keepdims=True)
    return rstd * (scaled - first - hat * second)


def put_transposed(value, turned, own_ref, other_ref, absolute=False):
    x, y, c, _ = place()
    turned[...] = value.T
    for xy in range(4):
        for side, ref in ((0, own_ref), (4, other_ref)):
            if absolute:
                row = (2 * xy + xor_bit(c, side)) * 96
            else:
                row = row_block(x, y, c, (16 if xy & 2 else 0) | (8 if xy & 1 else 0) | side) * 96
            ref[pl.ds(xy * 96, 96), :] = turned[pl.ds(pl.multiple_of(row, 32), 96), :].astype(BF)


def call(kernel, outs, scratch, specs, args, micros=1, name=None, ties=(), limit=LIMIT):
    return pl.pallas_call(
        lambda *refs: kernel(*refs[len(ties) :]),
        out_shape=[jax.ShapeDtypeStruct(s, d) for s, d in outs],
        in_specs=[SPEC_A] * len(ties) + list(specs),
        out_specs=[SPEC_V] * len(outs),
        scratch_shapes=scratch,
        compiler_params=pltpu.CompilerParams(vmem_limit_bytes=limit * 1024 * 1024),
        cost_estimate=pl.CostEstimate(flops=int(micros * COST), bytes_accessed=1000, transcendentals=0),
        name=name,
    )(*ties, *args)


def project_kernel(n_a, x_ref, vec_ref, bias_ref, *refs):
    a_refs, refs = refs[:n_a], refs[n_a:]
    outs, (own_ref, other_ref, w, turned, sems) = refs[:4], refs[4:]
    load = Loader(a_refs, (ORDER_A,), w, sems, 0, 0, 640)
    load.start()
    _, y, _, ten = place()
    hat, _ = norm_parts(x_ref[...].astype(F32))
    normed = hat * vec_ref[0:1, :] + vec_ref[1:2, :]
    low = normed.astype(BF)
    put_transposed(normed, turned, own_ref, other_ref)
    for rz in range(4):
        load.wait(rz)
    for pair in range(4):
        g = group_of(y, ten, pair)
        packed = dot_nn(low, w[g])[:, :576] + bias_ref[g]
        outs[pair][...] = packed.astype(BF)


def project(x, vec, bias, a, tokens, ties=()):
    outs = [((tokens, 576), BF)] * 4 + [((384, tokens), BF)] * 2
    scratch = [pltpu.VMEM((4, 768, 640), BF), pltpu.VMEM((768, tokens), F32), pltpu.SemaphoreType.DMA((32,))]
    return call(
        partial(project_kernel, len(a)), outs, scratch, [SPEC_V] * 3 + [SPEC_A] * len(a), (x, vec, bias, *a),
        micros=4, name="project", ties=ties,
    )


def attend_kernel(count_ref, p0, p1, p2, p3, o0, o1, o2, o3, m0, m1, m2, m3, kv_ref, q_ref, mixed_ref):
    _, y, c, ten = place()
    tokens = p0.shape[0]
    half = lax.rem(ten, 2)
    for pair, (p, o) in enumerate(((p0, o0), (p1, o1), (p2, o2), (p3, o3))):
        for side, ref in ((0, p), (1, o)):
            block = (xor_bit(y, pair & 2) * 2 + xor_bit(c, side)) * 2 + xor_bit(half, pair & 1)
            kv_ref[pl.ds(pl.multiple_of(block * tokens, 64), tokens), :] = ref[:, :384]
        q_ref[pl.ds(pair * tokens, tokens), :] = p[:, 384:576] * jnp.asarray(HD ** (-0.5), BF)
    total = kv_ref.shape[0]
    count = count_ref[0]
    ones = jnp.ones((total, HD), BF)
    valid = lax.broadcasted_iota(jnp.int32, (tokens, 128), 1) + (total - 128) < count
    mixed_ref[:, 192:256] = jnp.zeros((4 * tokens, 64), F32)
    for h in range(3):
        keys = kv_ref[:, h * HD : (h + 1) * HD]
        values = jnp.concatenate([kv_ref[:, 192 + h * HD : 192 + (h + 1) * HD], ones], axis=1)
        for pair, m in enumerate((m0, m1, m2, m3)):
            rows = pl.ds(pair * tokens, tokens)
            scores = dot_nt(q_ref[rows, h * HD : (h + 1) * HD], keys)
            last = jnp.where(valid, scores[:, total - 128 :], -1000000000.0)
            scores = jnp.concatenate([scores[:, : total - 128], last], axis=1)
            highest = jnp.max(scores, axis=-1, keepdims=True)
            expo = jnp.exp(scores - highest).astype(BF)
            both = dot_nn(expo, values)
            weight = both[:, HD : HD + 1]
            mixed = both[:, :HD] / weight
            mixed_ref[rows, h * HD : (h + 1) * HD] = mixed
            m[:, h * HD : (h + 1) * HD] = mixed.astype(BF)
            mixed_ref[rows, 192 + h : 193 + h] = highest + jnp.log(weight)


def attend(count, pieces, others, ties=()):
    tokens = pieces[0].shape[0]
    outs = [((tokens, 192), BF)] * 4 + [
        ((8 * tokens, 384), BF),
        ((4 * tokens, 192), BF),
        ((4 * tokens, 256), F32),
    ]
    return call(
        attend_kernel, outs, [], [SPEC_S] + [SPEC_V] * 8, (count, *pieces, *others),
        micros=7, name="attend", ties=ties,
    )


def mlp_kernel(n_a, n_e, m0, m1, m2, m3, x_ref, vec_ref, eb_ref, *refs):
    a_refs, e_refs = refs[:n_a], refs[n_a : n_a + n_e]
    s_refs, refs = refs[n_a + n_e : n_a + 2 * n_e], refs[n_a + 2 * n_e :]
    (x_out, after_ref, mixed_ref, own_ref, other_ref, active_ref, slope_ref, wo, we, ws, turned, sa, se, ss) = refs
    load_a = Loader(a_refs, (ORDER_A,), wo, sa, 0, 512, 256)
    load_e = Loader(e_refs, (ORDER_E,), we, se, 96)
    load_s = Loader(s_refs, (ORDER_S,), ws, ss, 192)
    load_a.start()
    load_e.start()
    load_s.start()
    _, y, _, ten = place()
    for rz in range(4):
        load_a.wait(rz)
    after = x_ref[...].astype(F32) + vec_ref[2:3, :]
    for pair, m in enumerate((m0, m1, m2, m3)):
        g = group_of(y, ten, pair)
        piece = m[...]
        mixed_ref[g] = piece
        after = after + dot_nt(piece, wo[g][:, 64:])
    after_ref[...] = after
    hat, _ = norm_parts(after)
    normed = hat * vec_ref[3:4, :] + vec_ref[4:5, :]
    low = normed.astype(BF)
    put_transposed(normed, turned, own_ref, other_ref, True)
    out = after + vec_ref[5:6, :]
    for rz in range(4):
        z = load_e.index(rz)
        load_e.wait(rz)
        hidden = dot_nn(low, we[z]) + eb_ref[z]
        lower = 0.5 * (1.0 + lax.erf(hidden * 0.7071067811865476))
        slope_ref[z] = lower + hidden * (jnp.exp(-0.5 * hidden * hidden) * 0.3989422804014327)
        active = (hidden * lower).astype(BF)
        active_ref[z] = active
        load_s.wait(rz)
        out = out + dot_nt(active, ws[z])
    x_out[...] = out


def mlp(pieces, x, vec, eb, a, e, s, ties=()):
    tokens = x.shape[0]
    outs = [
        ((tokens, 768), F32),
        ((tokens, 768), F32),
        ((4, tokens, 192), BF),
        ((384, tokens), BF),
        ((384, tokens), BF),
        ((4, tokens, 768), BF),
        ((4, tokens, 768), F32),
    ]
    scratch = [
        pltpu.VMEM((4, 768, 256), BF),
        pltpu.VMEM((4, 768, 768), BF),
        pltpu.VMEM((4, 768, 768), BF),
        pltpu.VMEM((768, tokens), F32),
        pltpu.SemaphoreType.DMA((32,)),
        pltpu.SemaphoreType.DMA((32,)),
        pltpu.SemaphoreType.DMA((32,)),
    ]
    return call(
        partial(mlp_kernel, len(a), len(e)), outs, scratch, [SPEC_V] * 7 + [SPEC_A] * (len(a) + 2 * len(e)), (*pieces, x, vec, eb, *a, *e, *s),
        micros=12, name="mlp", ties=ties,
    )


def mlp_back_kernel(n_a, n_e, dy_ref, after_ref, vec_ref, slope_ref, *refs):
    a_refs, e_refs = refs[:n_a], refs[n_a : n_a + n_e]
    s_refs, refs = refs[n_a + n_e : n_a + 2 * n_e], refs[n_a + 2 * n_e :]
    d_out, refs = refs[:4], refs[4:]
    (da_ref, hid_ref, a_own, a_other, sums_ref, ebs_ref, z_own, z_other, wo, we, ws, turned, sa, se, ss) = refs
    load_a = Loader(a_refs, (ORDER_A,), wo, sa, 0, 512, 256)
    load_e = Loader(e_refs, (ORDER_E,), we, se, 96)
    load_s = Loader(s_refs, (ORDER_S,), ws, ss, 192)
    load_s.start()
    load_e.start()
    load_a.start()
    _, y, _, ten = place()
    dy = dy_ref[...].astype(F32)
    dz = dy.astype(BF)
    dz_wide = dz.astype(F32)
    put_transposed(dz_wide, turned, z_own, z_other, True)
    grad = jnp.zeros(dy.shape, F32)
    for rz in range(4):
        z = load_s.index(rz)
        load_s.wait(rz)
        d_active = dot_nn(dz, ws[z])
        d_hidden = (d_active * slope_ref[z]).astype(BF)
        hid_ref[z] = d_hidden
        ebs_ref[z] = jnp.sum(d_hidden.astype(F32), axis=0, keepdims=True)
        load_e.wait(rz)
        grad = grad + dot_nt(d_hidden, we[z])
    hat, rstd = norm_parts(after_ref[...])
    d_after = dy + norm_back(hat, rstd, vec_ref[3:4, :], grad)
    da_ref[...] = d_after
    da = d_after.astype(BF)
    da_wide = da.astype(F32)
    put_transposed(da_wide, turned, a_own, a_other)
    sums_ref[0:1, :] = jnp.sum(da_wide, axis=0, keepdims=True)
    sums_ref[1:2, :] = jnp.sum(grad * hat, axis=0, keepdims=True)
    sums_ref[2:3, :] = jnp.sum(grad, axis=0, keepdims=True)
    sums_ref[3:4, :] = jnp.sum(dz_wide, axis=0, keepdims=True)
    sums_ref[4:8, :] = jnp.zeros((4, dy.shape[1]), F32)
    for rz in range(4):
        load_a.wait(rz)
    for pair in range(4):
        g = group_of(y, ten, pair)
        d_out[pair][...] = dot_nn(da, wo[g])[:, 64:].astype(BF)


def mlp_back(dy, after, vec, slope, a, e, s, ties=()):
    tokens = dy.shape[0]
    outs = [((tokens, 192), BF)] * 4 + [
        ((tokens, 768), F32),
        ((4, tokens, 768), BF),
        ((384, tokens), BF),
        ((384, tokens), BF),
        ((8, 768), F32),
        ((4, 1, 768), F32),
        ((384, tokens), BF),
        ((384, tokens), BF),
    ]
    scratch = [
        pltpu.VMEM((4, 768, 256), BF),
        pltpu.VMEM((4, 768, 768), BF),
        pltpu.VMEM((4, 768, 768), BF),
        pltpu.VMEM((768, tokens), F32),
        pltpu.SemaphoreType.DMA((32,)),
        pltpu.SemaphoreType.DMA((32,)),
        pltpu.SemaphoreType.DMA((32,)),
    ]
    return call(
        partial(mlp_back_kernel, len(a), len(e)), outs, scratch, [SPEC_V] * 4 + [SPEC_A] * (len(a) + 2 * len(e)),
        (dy, after, vec, slope, *a, *e, *s), micros=11, name="mlp_back", ties=ties,
    )


def attend_back_kernel(count_ref, d0, d1, d2, d3, kv_ref, q_ref, mixed_ref, dq_ref, own_ref, other_ref, do, inner, stat, dkv):
    _, y, c, ten = place()
    tokens = d0.shape[0]
    half = lax.rem(ten, 2)
    inner[...] = jnp.zeros(inner.shape, F32)
    for pair, d in enumerate((d0, d1, d2, d3)):
        rows = pl.ds(pair * tokens, tokens)
        grad = d[...]
        do[rows, :] = grad
        for h in range(3):
            cols = slice(h * HD, (h + 1) * HD)
            inner[rows, h : h + 1] = jnp.sum(grad[:, cols].astype(F32) * mixed_ref[rows, cols], axis=-1, keepdims=True)
    stat[0] = mixed_ref[:, 128:256].T
    stat[1] = inner[...].T
    total, queries = kv_ref.shape[0], q_ref.shape[0]
    count = count_ref[0]
    step = 256
    valid = lax.broadcasted_iota(jnp.int32, (128, step), 0) + (total - 128) < count
    for h in range(3):
        cols = slice(h * HD, (h + 1) * HD)
        keys = kv_ref[:, cols]
        values = kv_ref[:, 192 + h * HD : 192 + (h + 1) * HD]
        turned = keys.astype(F32).T.astype(BF)
        d_keys = jnp.zeros((total, HD), F32)
        d_values = jnp.zeros((total, HD), F32)
        for block in range(queries // step):
            rows = slice(block * step, (block + 1) * step)
            query = q_ref[rows, cols]
            grad = do[rows, cols]
            scores = dot_nt(keys, query)
            last = jnp.where(valid, scores[total - 128 :], -1000000000.0)
            scores = jnp.concatenate([scores[: total - 128], last], axis=0)
            probs = jnp.exp(scores - stat[0, 64 + h : 65 + h, rows])
            d_probs = dot_nt(values, grad)
            d_scores = (probs * (d_probs - stat[1, h : h + 1, rows])).astype(BF)
            d_values = d_values + dot_nn(probs.astype(BF), grad)
            d_keys = d_keys + dot_nn(d_scores, query)
            d_query = dot_nn(turned, d_scores) * HD ** (-0.5)
            dq_ref[rows, cols] = d_query.T.astype(BF)
        dkv[:, cols] = d_keys.astype(BF)
        dkv[:, 192 + h * HD : 192 + (h + 1) * HD] = d_values.astype(BF)
    for pair in range(4):
        for side, ref in ((0, own_ref), (1, other_ref)):
            block = (xor_bit(y, pair & 2) * 2 + xor_bit(c, side)) * 2 + xor_bit(half, pair & 1)
            ref[pair] = dkv[pl.ds(pl.multiple_of(block * tokens, 64), tokens), :]


def attend_back(count, pieces, kv, q, mixed, ties=()):
    tokens = pieces[0].shape[0]
    outs = [((4 * tokens, 192), BF), ((4, tokens, 384), BF), ((4, tokens, 384), BF)]
    scratch = [
        pltpu.VMEM((4 * tokens, 192), BF),
        pltpu.VMEM((4 * tokens, 128), F32),
        pltpu.VMEM((2, 128, 4 * tokens), F32),
        pltpu.VMEM((8 * tokens, 384), BF),
    ]
    return call(
        attend_back_kernel, outs, scratch, [SPEC_S] + [SPEC_V] * 7, (count, *pieces, kv, q, mixed),
        micros=11, name="attend_back", ties=ties,
    )


def project_back_kernel(n_a, n_high, d0, d1, d2, d3, da_ref, x_ref, vec_ref, two_ref, ebs_ref, *refs):
    high_refs, a_refs, refs = refs[:n_high], refs[n_high : n_high + n_a], refs[n_high + n_a :]
    dx_ref, dqkv_ref, sums_ref, w, sems = refs
    load = Loader(a_refs, (ORDER_A,), w, sems, 0, 0, 640)
    load.start()
    _, y, _, ten = place()
    hat, rstd = norm_parts(x_ref[...].astype(F32))
    sums_ref[2:6, :] = two_ref[0:4, :]
    sums_ref[10:16, :] = jnp.zeros((6, hat.shape[1]), F32)
    for z in range(4):
        sums_ref[6 + z : 7 + z, :] = ebs_ref[z]
    if n_high:
        sums_ref[16:32, :] = high_refs[0][...]
    for rz in range(4):
        load.wait(rz)
    grad = jnp.zeros(hat.shape, F32)
    for pair, d in enumerate((d0, d1, d2, d3)):
        g = group_of(y, ten, pair)
        piece = d[...]
        dqkv_ref[g] = piece
        sums_ref[pl.ds(10 + g, 1), :576] = jnp.sum(piece.astype(F32), axis=0, keepdims=True)
        grad = grad + dot_nt(piece, w[g][:, :576])
    dx_ref[...] = da_ref[...] + norm_back(hat, rstd, vec_ref[0:1, :], grad)
    sums_ref[0:1, :] = jnp.sum(grad * hat, axis=0, keepdims=True)
    sums_ref[1:2, :] = jnp.sum(grad, axis=0, keepdims=True)


def project_back(pieces, da, x, vec, two, ebs, high, a, ties=()):
    tokens = x.shape[0]
    outs = [((tokens, 768), F32), ((4, tokens, 576), BF), ((16 + 16 * len(high), 768), F32)]
    scratch = [pltpu.VMEM((4, 768, 640), BF), pltpu.SemaphoreType.DMA((32,))]
    return call(
        partial(project_back_kernel, len(a), len(high)),
        outs,
        scratch,
        [SPEC_V] * (9 + len(high)) + [SPEC_A] * len(a),
        (*pieces, da, x, vec, two, ebs, *high, *a),
        micros=4,
        name="project_back",
        ties=ties,
    )


def weigh_both_kernel(m_own, m_got, z_own, z_got, h_own, h_got, a_own, a_got, out_ref):
    for z in range(4):
        expand = dot_nn(m_own[...], h_own[z]) + dot_nn(m_got[...], h_got[z])
        shrink = dot_nn(z_own[...], a_own[z]) + dot_nn(z_got[...], a_got[z])
        for at, xy in enumerate(RING):
            rows = slice(xy * 96, (xy + 1) * 96)
            out_ref[at * 4 + z, 0:96] = expand[rows].astype(BF)
            out_ref[at * 4 + z, 96:192] = shrink[rows].astype(BF)


def weigh_both(args):
    return call(weigh_both_kernel, [((16, 192, 768), BF)], [], [SPEC_V] * 8, args, micros=5, name="weigh_both")[0]


def sum_plane(chunks, mesh_shape):
    dp_size, seq_size, ten_size = mesh_shape
    groups = [
        [((h + (xy >> 1)) * seq_size + 2 * (xy & 1) + c) * ten_size + t for xy in RING]
        for h in range(0, dp_size, 2)
        for c in range(2)
        for t in range(ten_size)
    ]
    rows = chunks.shape[1]
    return lax.psum_scatter(
        chunks.reshape(16 * rows, 768), AXES, scatter_dimension=0, axis_index_groups=groups, tiled=True
    )


def sum_line(chunks):
    return lax.psum_scatter(chunks, "tensor", scatter_dimension=0, tiled=True).astype(F32)


def weigh_attention_kernel(total_ref, *refs):
    x, y, c, ten = place()
    low, high, outs, turned = refs[:8], refs[8:16], refs[16:26], refs[26]
    turned[...] = jnp.concatenate([total_ref[...], jnp.zeros((96, 768), F32)], axis=0).T
    for rz in range(4):
        z = xor_two(ten, rz)
        values = []
        for n_own, n_got, a_own, a_got, q_own, q_got, m_own, m_got in (low, high):
            qkv = dot_nn(n_own[...], q_own[z]) + dot_nn(n_got[...], q_got[z])
            out = dot_nn(a_own[...], m_own[z]) + dot_nn(a_got[...], m_got[z])
            values.append(jnp.concatenate([qkv, out], axis=1).astype(BF))
        for xy in range(4):
            rel = (16 if xy & 2 else 0) | (8 if xy & 1 else 0) | rz
            for n, order in enumerate(SUM_A):
                part, at = part_of(rel, order)
                lines = slice(xy * 96 + n * 48, xy * 96 + (n + 1) * 48)
                for k, value in enumerate(values):
                    outs[n * 5 + part][at, k * 48 : (k + 1) * 48, 0:768] = value[lines]
            block = row_block(x, y, c, rel)
            query = turned[pl.ds(pl.multiple_of(384 + block * 24, 8), 24), :][:, :32]
            other = turned[pl.ds(pl.multiple_of(192 + block * 24, 8), 24), :][:, :32]
            none = jnp.zeros((24, 32), F32)
            pair = jnp.concatenate([none, query, other, none], axis=1)
            more = turned[pl.ds(pl.multiple_of(block * 96, 32), 96), :]
            more = more + jnp.concatenate([pair, jnp.zeros((72, 128), F32)], axis=0)
            part, at = part_of(rel, SUM_A[0])
            outs[part][at, :, 768:896] = more.astype(BF)


def weigh_attention(total, low, high):
    outs = [((n, 96, width), BF) for width in (896, 768) for n in (8, 4, 2, 1, 1)]
    return call(
        weigh_attention_kernel, outs, [pltpu.VMEM((768, 128), F32)], [SPEC_V] * 17, (total, *low, *high), micros=6,
        name="weigh_attention",
    )


def spread_kernel(p0, p1, p2, p3, first_ref, second_ref):
    ten = lax.axis_index("tensor")
    for rz, p in ((0, p0), (2, p1), (1, p2), (3, p3)):
        first_ref[xor_two(ten, rz)] = p[0]
        second_ref[xor_two(ten, rz)] = p[1].astype(F32)


def spread(frames):
    _, tokens, width = frames[0].shape
    outs = [((4, tokens, width), BF), ((4, tokens, width), F32)]
    done = call(spread_kernel, outs, [], [SPEC_V] * 4, frames, name="spread")
    return [d.reshape(2, 1, 2 * tokens, width) for d in done]


def small_params(every):
    vec = every[:, 0, :, :6].transpose(1, 2, 0, 3).reshape(LAYERS, 6, 768)
    eb = every[:, :, :, 6].transpose(2, 1, 0, 3).reshape(LAYERS, 4, 1, 768)
    qv = every[:, :, :, 7, :48].reshape(8, 4, LAYERS, 2, 24).transpose(2, 3, 1, 0, 4).reshape(LAYERS, 2, 4, 192)
    qvb = jnp.concatenate([jnp.zeros_like(qv[:, 0]), qv[:, 1], qv[:, 0]], axis=-1)[:, :, None, :]
    return jnp.pad(vec, ((0, 0), (0, 2), (0, 0))), qvb, eb


def small_everywhere(chunks, order):
    x, y, c, ten = place()
    me = ((x * 2 + y) * 2 + c) * 4 + ten
    rels = []
    for a in range(4):
        for j in range(8):
            rel = sum(BITS[order[k]] for k in range(3) if j & (1 << k))
            rels.append(rel | (BITS[order[3]] if a & 1 else 0) | (BITS["c"] if a & 2 else 0))
    device = jnp.bitwise_xor(jnp.asarray(rels, jnp.int32), me)
    pick = (jnp.arange(32, dtype=jnp.int32)[:, None] == device[None, :]).astype(BF)
    rows = jnp.concatenate([chunk[:, 96:98].reshape(8, -1) for chunk in chunks], axis=0)
    every = jnp.dot(pick, rows, preferred_element_type=F32)
    return every.reshape(8, 4, LAYERS, 8, 96)


def body(shape, features, upstream, key_mask, vectors, proj_qkv, qv_bias, proj_out, expand_weight, expand_bias, shrink_weight):
    dp_size, seq_size, ten_size = shape
    dp, seq, ten = lax.axis_index("dp"), lax.axis_index("seq"), lax.axis_index("tensor")
    tokens = features.shape[2] // 2
    at = (lax.div(ten, 2), 0, lax.rem(ten, 2) * tokens, 0)
    x0 = lax.dynamic_slice(features, at, (1, 1, tokens, 768)).reshape(tokens, 768)
    dy0 = lax.dynamic_slice(upstream, at, (1, 1, tokens, 768)).reshape(tokens, 768)
    count = jnp.sum(lax.dynamic_slice(key_mask, (lax.div(ten, 2), 0, 0), (1, 1, key_mask.shape[2])), axis=(1, 2))

    width = proj_qkv.shape[1]
    wa = jnp.concatenate(
        [
            proj_qkv[:, :, 1],
            proj_qkv[:, :, 2],
            proj_qkv[:, :, 0],
            proj_out.transpose(0, 2, 1),
        ],
        axis=-1,
    )
    we = expand_weight
    ws = shrink_weight.transpose(0, 2, 1)
    if dp_size != 2:
        start = (lax.rem(dp, 2) * 4 + seq) * 96
        wa, we, ws = (
            lax.dynamic_slice_in_dim(lax.all_gather(w, ("dp", "seq"), axis=1, tiled=True), start, 96, axis=1)
            for w in (wa, we, ws)
        )
    if dp_size == 2:
        small = jnp.concatenate(
            [
                vectors.reshape(LAYERS, -1),
                expand_bias,
                qv_bias.reshape(LAYERS, -1),
                jnp.zeros((LAYERS, 48), BF),
            ],
            axis=1,
        )
    else:
        small = jnp.zeros((LAYERS, 768), BF)
    first = jnp.concatenate([wa[0], small, jnp.zeros((6, 768), BF)], axis=0)
    whole = [
        [(d * seq_size + s) * ten_size + t for d in range(h, h + 2) for s in range(seq_size) for t in range(ten_size)]
        for h in range(0, dp_size, 2)
    ]
    low_layer = Gatherer((first, we[0], ws[0]), (ORDER_A, ORDER_E, ORDER_S), shape)
    for _ in range(3):
        low_layer.go()
    (block,) = low_layer.before(jnp.concatenate([wa[1], we[1], ws[1]], axis=0))
    high = lax.all_gather(block, AXES, axis_index_groups=None if dp_size == 2 else whole)
    low_layer.go()
    a_w, e_w, s_w = ((w, [high]) for w in low_layer.core())
    if dp_size == 2:
        vec, qvb, eb = small_params(small_everywhere(a_w[0], ORDER_A))
    else:
        vec = lax.all_gather(vectors, ("dp", "seq"), axis=2, tiled=True).reshape(LAYERS, 6, 8, 96)
        eb = lax.all_gather(expand_bias, ("tensor", "dp", "seq"), axis=1, tiled=True).reshape(LAYERS, 1, 4, 8, 96)
        qv = lax.all_gather(qv_bias, ("tensor", "dp", "seq"), axis=2, tiled=True).reshape(LAYERS, 2, 4, 8, 24)
        vec = jnp.broadcast_to(vec[:, :, None], (LAYERS, 6, 4, 8, 96))
        qv = jnp.pad(qv.transpose(0, 2, 3, 1, 4).reshape(LAYERS, 1, 4, 8, 48), ((0, 0),) * 4 + ((0, 48),))
        vec, qvb, eb = small_params(jnp.concatenate([vec, eb, qv], axis=1).transpose(3, 2, 0, 1, 4).astype(F32))

    state = x0
    kept = []
    for d in range(LAYERS):
        *pieces, n_own, n_other = project(state, vec[d], qvb[d], a_w[d], tokens)
        pieces = [pieces[0]] + [swap_group(pieces[p], p, shape) for p in (1, 2, 3)]
        others = [swap(p[:, :384], "c", shape) for p in pieces]
        *mixed, kv, q, mixed_wide = attend(count, pieces, others)
        mixed = [mixed[0]] + [swap_group(mixed[p], p, shape) for p in (1, 2, 3)]
        x_in = state
        state, after, mixed_all, m_own, m_other, active, slope = mlp(mixed, x_in, vec[d], eb[d], a_w[d], e_w[d], s_w[d])
        kept.append((x_in, n_own, n_other, kv, q, mixed_wide, after, mixed_all, m_own, m_other, active, slope))
    encoded = state.astype(BF)

    grad = dy0
    for d in (1, 0):
        x_in, n_own, n_other, kv, q, mixed_wide, after, mixed_all, m_own, m_other, active, slope = kept[d]
        d0, d1, d2, d3, d_after, d_hid, da_own, da_other, sums_two, ebs, z_own, z_other = mlp_back(
            grad, after, vec[d], slope, a_w[d], e_w[d], s_w[d]
        )
        d_mixed = [d0] + [swap_group(v, p + 1, shape) for p, v in enumerate((d1, d2, d3))]
        m_got, hid_got, z_got, active_got = (swap(v, "c", shape) for v in (m_other, d_hid, z_other, active))
        if d:
            d1, d2, d3, m_got, z_got, hid_got, active_got = fence(*d_mixed[1:], m_got, z_got, hid_got, active_got)
            d_mixed = [d0, d1, d2, d3]
            chunks = weigh_both((m_own, m_got, z_own, z_got, d_hid, hid_got, active, active_got))
            high_sum = sum_plane(chunks, shape)
        else:
            high_sum, *d_mixed = fence(high_sum, *d_mixed)
            high_sum = sum_line(high_sum)
        dq, own, other = attend_back(count, d_mixed, kv, q, mixed_wide, [chunks] if d else [])
        d_kv = (own.astype(F32) + swap(other, "c", shape).astype(F32)).astype(BF)
        back = [jnp.concatenate([d_kv[p], dq[p * tokens : (p + 1) * tokens]], axis=1) for p in range(4)]
        if d == 0:
            *back, m_got, z_got, hid_got, active_got = fence(*back, m_got, z_got, hid_got, active_got)
        back = [back[0]] + [swap_group(back[p], p, shape) for p in (1, 2, 3)]
        if d == 0:
            chunks = weigh_both((m_own, m_got, z_own, z_got, d_hid, hid_got, active, active_got))
            low_sum = sum_plane(chunks, shape)
            high_sum, *back = fence(high_sum, *back)
        grad, d_qkv, total = project_back(back, d_after, x_in, vec[d], sums_two, ebs, [] if d else [high_total], a_w[d], [chunks])
        given = (
            n_own,
            swap(n_other, "c", shape),
            da_own,
            swap(da_other, "c", shape),
            d_qkv,
            swap(d_qkv, "c", shape),
            mixed_all,
            swap(mixed_all, "c", shape),
        )
        if d:
            high_total = total
            high_given = given
    if dp_size == 2:
        total = total + swap(total, "c", shape)
        embedded = total
    else:
        embedded = jnp.zeros_like(total)
        total = lax.psum(total, AXES)
    parts = weigh_attention(embedded, given, high_given)
    sums_a = [Reducer(parts[n * 5 : n * 5 + 5], order, shape) for n, order in enumerate(SUM_A)]
    frames = [jnp.stack([encoded, grad.astype(BF)])]
    last = Together(sums_a)
    (frames[0],) = last.wait(frames[0])
    frames.append(swap(frames[0], "z2", shape))
    frames += [swap(v, "z1", shape) for v in frames]
    for step in range(4):
        if step == 0:
            low_sum = sum_line(last.go(low_sum)[0])
        elif step == 1:
            frames = last.go(*frames)
        elif step == 2:
            last.go()
        else:
            ge, gs = (jnp.stack([low_sum[at : at + 96], high_sum[at : at + 96]]) for at in (0, 96))
            ge, gs = last.go(ge, gs.transpose(0, 2, 1))
    small = total.reshape(LAYERS, 16, 768)
    encoded, grad_features = spread(frames)
    chunk, rest = (r.finish() for r in sums_a)
    g_a = [jnp.concatenate([chunk[at : at + 48, :768], rest[at : at + 48]], axis=0) for at in (0, 48)]

    if dp_size != 2:
        start = (lax.rem(dp, 2) * 4 + seq) * 96

        def down(block):
            whole = lax.dynamic_update_slice_in_dim(jnp.zeros((768, 768), F32), block, start, axis=0)
            return lax.psum_scatter(whole, ("dp", "seq"), scatter_dimension=0, tiled=True)

        g_a = [down(g) for g in g_a]
        ge = jnp.stack([down(g) for g in ge])
        gs = jnp.stack([down(g) for g in gs.transpose(0, 2, 1)]).transpose(0, 2, 1)
    ga = jnp.stack(g_a)
    if dp_size == 2:
        turned = chunk[:, 768:864].T.reshape(3, LAYERS, 16, 96)
        grad_vectors = turned[0, :, :6]
        grad_eb = lax.dynamic_index_in_dim(turned[0, :, 6:10], ten, axis=1, keepdims=False)
        pair = lax.dynamic_index_in_dim(turned[1:, :, 10:14], ten, axis=2, keepdims=False)
        grad_qv = pair[:, :, :24].transpose(1, 0, 2)
    else:
        mine = dp * seq_size + seq
        grad_vectors = lax.dynamic_slice_in_dim(small[:, :6], mine * width, width, axis=2)
        eb_width, qv_width = expand_bias.shape[1], qv_bias.shape[2]
        grad_eb = lax.dynamic_slice_in_dim(
            lax.dynamic_index_in_dim(small[:, 6:10], ten, axis=1, keepdims=False), mine * eb_width, eb_width, axis=1
        )
        qv = lax.dynamic_index_in_dim(small[:, 10:14], ten, axis=1, keepdims=False)
        grad_qv = jnp.stack(
            [
                lax.dynamic_slice_in_dim(qv[:, 384:576], mine * qv_width, qv_width, axis=1),
                lax.dynamic_slice_in_dim(qv[:, 192:384], mine * qv_width, qv_width, axis=1),
            ],
            axis=1,
        )
    grad_qkv = jnp.stack([ga[:, :, 384:576], ga[:, :, :192], ga[:, :, 192:384]], axis=2)
    return (
        encoded,
        grad_features,
        grad_vectors,
        grad_qkv,
        grad_qv,
        ga[:, :, 576:].transpose(0, 2, 1),
        ge,
        grad_eb,
        gs,
    )


def solution(mesh):
    placed = (
        P(None, "dp", "seq", None),
        P(None, "dp", "seq", None),
        P(None, "dp", None),
        P(None, None, ("dp", "seq")),
        P(None, ("dp", "seq"), None, "tensor"),
        P(None, None, ("tensor", "dp", "seq")),
        P(None, "tensor", ("dp", "seq")),
        P(None, ("dp", "seq"), "tensor"),
        P(None, ("tensor", "dp", "seq")),
        P(None, "tensor", ("dp", "seq")),
    )
    shape = tuple(mesh.shape[axis] for axis in AXES)
    return jax.shard_map(
        partial(body, shape),
        mesh=mesh,
        in_specs=placed,
        out_specs=(
            P(None, "dp", "seq", None),
            P(None, "dp", "seq", None),
            P(None, None, ("dp", "seq")),
            P(None, ("dp", "seq"), None, "tensor"),
            P(None, None, ("tensor", "dp", "seq")),
            P(None, "tensor", ("dp", "seq")),
            P(None, ("dp", "seq"), "tensor"),
            P(None, ("tensor", "dp", "seq")),
            P(None, "tensor", ("dp", "seq")),
        ),
        check_vma=False,
    )
```
